32 devices in a mesh: dir: 2 (over core), rows: 16 (over z, y, x).
Axes of the slice: x: 2, y: 2, z: 4, core: 2. Of those that a mesh axis runs over, the one named last changes fastest.
Arguments:
- spectra: bfloat16 [16, 64, 2, 41, 128], P('rows', None, 'dir'), may hold values from -6 to 6
- mask_grad: bfloat16 [16, 64, 2, 41, 128], P('rows', None, 'dir'), may hold values from -6 to 6
- clip_starts: int32 [16, 64, 2], P('rows'), may hold values from 0 to 1, as said below
- split_weight: float32 [5248, 128], P('rows'), may hold values from -0.5 to 0.5
- split_velocity: float32 [5248, 128], P('rows'), may hold values from -0.009765625 to 0.009765625
- split_average: float32 [5248, 128], P('rows'), may hold values from -0.5 to 0.5
- lstm_weight: float32 [1536, 1024], P('rows'), may hold values from -0.3125 to 0.3125
- lstm_velocity: float32 [1536, 1024], P('rows'), may hold values from -0.009765625 to 0.009765625
- lstm_average: float32 [1536, 1024], P('rows'), may hold values from -0.3125 to 0.3125
- proj_weight: float32 [1024, 128], P('rows'), may hold values from -0.5 to 0.5
- proj_velocity: float32 [1024, 128], P('rows'), may hold values from -0.009765625 to 0.009765625
- proj_average: float32 [1024, 128], P('rows'), may hold values from -0.5 to 0.5
- up_weight: float32 [5248, 512], P('rows'), may hold values from -0.5 to 0.5
- up_velocity: float32 [5248, 512], P('rows'), may hold values from -0.009765625 to 0.009765625
- up_average: float32 [5248, 512], P('rows'), may hold values from -0.5 to 0.5
- down_weight: float32 [20992, 256], P('rows'), may hold values from -0.25 to 0.25
- down_velocity: float32 [20992, 256], P('rows'), may hold values from -0.009765625 to 0.009765625
- down_average: float32 [20992, 256], P('rows'), may hold values from -0.25 to 0.25
- gain_weight: float32 [84, 128], replicated, may hold values from 0.5 to 1.5
- gain_velocity: float32 [84, 128], replicated, may hold values from -0.009765625 to 0.009765625
- gain_average: float32 [84, 128], replicated, may hold values from 0.1 to 1.9
- bias_weight: float32 [321, 128], replicated, may hold values from -3 to 7
- bias_velocity: float32 [321, 128], replicated, may hold values from -0.009765625 to 0.009765625
- bias_average: float32 [321, 128], replicated, may hold values from -1.2 to 1.2
Outputs:
- band_mask: bfloat16 [16, 64, 2, 41, 128], P('rows', None, 'dir')
- spectra_grad: float32 [16, 64, 2, 41, 128], P('rows', None, 'dir')
- grad_norm: float32 [], replicated
- split_grad: float32 [5248, 128], P('rows')
- split_velocity_new: float32 [5248, 128], P('rows')
- split_weight_new: float32 [5248, 128], P('rows')
- split_average_new: float32 [5248, 128], P('rows')
- lstm_grad: float32 [1536, 1024], P('rows')
- lstm_velocity_new: float32 [1536, 1024], P('rows')
- lstm_weight_new: float32 [1536, 1024], P('rows')
- lstm_average_new: float32 [1536, 1024], P('rows')
- proj_grad: float32 [1024, 128], P('rows')
- proj_velocity_new: float32 [1024, 128], P('rows')
- proj_weight_new: float32 [1024, 128], P('rows')
- proj_average_new: float32 [1024, 128], P('rows')
- up_grad: float32 [5248, 512], P('rows')
- up_velocity_new: float32 [5248, 512], P('rows')
- up_weight_new: float32 [5248, 512], P('rows')
- up_average_new: float32 [5248, 512], P('rows')
- down_grad: float32 [20992, 256], P('rows')
- down_velocity_new: float32 [20992, 256], P('rows')
- down_weight_new: float32 [20992, 256], P('rows')
- down_average_new: float32 [20992, 256], P('rows')
- gain_grad: float32 [84, 128], replicated
- gain_velocity_new: float32 [84, 128], replicated
- gain_weight_new: float32 [84, 128], replicated
- gain_average_new: float32 [84, 128], replicated
- bias_grad: float32 [321, 128], replicated
- bias_velocity_new: float32 [321, 128], replicated
- bias_weight_new: float32 [321, 128], replicated
- bias_average_new: float32 [321, 128], replicated
The draws below stay inside these ranges and needn't reach their ends.
Inputs may be any that keep to these rules, and one draw needn't show every extreme that they name: `clip_starts`: each packed sequence of 256 frames has exactly one frame flagged 1, at any of its frames; all others are 0.
All inputs are finite; a program needn't handle non-finite values.
Results may differ from the reference program's by a relative error of at most 0.018.
Values may be sent and summed in bfloat16 or wider, within the bound.
No kernel may reach another device: no remote copies, remote signals or barrier semaphores. Data moves between devices by JAX's collectives and lax.ppermute only.
A program may use at most 320 MiB of HBM per device.

```python
import math
import jax
import jax.numpy as jnp
from jax import lax

D = 128
H = 256
BANDS = 41
SUBF = 128
FR_DEV = 64
MICRO = 2
CHAIN = 4
FRAMES = 256
BLOCKS = 16
PARAMS = 10488448


def draw_clip_starts(key, part):
    groups = BLOCKS // CHAIN
    chosen = jax.random.randint(jax.random.fold_in(key, 17), (groups, MICRO), 0, CHAIN * FR_DEV).astype(jnp.int32)
    block_ids = jnp.arange(BLOCKS, dtype=jnp.int32)
    frame_ids = jnp.arange(FR_DEV, dtype=jnp.int32)
    whole_frame = (block_ids % CHAIN)[:, None] * FR_DEV + frame_ids[None, :]
    target = chosen[block_ids // CHAIN]
    return (whole_frame[:, :, None] == target[:, None, :]).astype(jnp.int32)


def draw_bias_weight(key, part):
    key = jax.random.fold_in(key, 29)
    row_count = 7 * BANDS + 16 * H // D + 2
    lstm_rows = 16 * H // D
    base = jnp.clip(0.2 * jax.random.normal(jax.random.fold_in(key, 1), (row_count, D), jnp.float32), -1.2, 1.2)
    chooser = jax.random.uniform(jax.random.fold_in(key, 2), (2, H), jnp.float32)
    slow_rate = jnp.exp(jax.random.uniform(jax.random.fold_in(key, 3), (2, H), jnp.float32, math.log(0.5), math.log(2.0))) / FRAMES
    fast_rate = jnp.exp(jax.random.uniform(jax.random.fold_in(key, 4), (2, H), jnp.float32, math.log(0.05), math.log(0.1)))
    slow_share = 0.6
    decay_rate = jnp.where(chooser < slow_share, slow_rate, fast_rate)
    forget_bias = -jnp.log(jnp.expm1(decay_rate))
    input_bias = -2.0 + 0.3 * jnp.clip(jax.random.normal(jax.random.fold_in(key, 5), (2, H), jnp.float32), -3.0, 3.0)
    lstm_part = base[BANDS:BANDS + lstm_rows].reshape(4, 4, H)
    lstm_part = lstm_part.at[:2, 0].set(input_bias).at[:2, 1].set(forget_bias)
    return base.at[BANDS:BANDS + lstm_rows].set(lstm_part.reshape(lstm_rows, D))


def shard_levels(key, dims, pieces, least, top_value):
    factor_of, own = 1.0, jax.random.fold_in(key, 6)
    for dim, shards_of in pieces:
        heights = jnp.exp(jax.random.uniform(jax.random.fold_in(own, dim), (shards_of,), jnp.float32, least / len(pieces), top_value / len(pieces)))
        factor_of = factor_of * jnp.repeat(heights, dims[dim] // shards_of).reshape([-1 if axis == dim else 1 for axis in range(len(dims))])
    return factor_of


def normal_values(key, extent, scale, most, shards=(), held_as=jnp.bfloat16):
    drawn = scale * jax.random.normal(key, extent, jnp.float32)
    if shards:
        drawn = drawn * shard_levels(key, extent, shards, -0.22, 0.18)
    return jnp.clip(drawn, -most, most).astype(held_as)


def setup_inputs(seed: int = 0) -> dict:
    streams_of = jax.random.split(jax.random.key(seed), 25)
    spectra = normal_values(streams_of[0], (BLOCKS, FR_DEV, MICRO, BANDS, SUBF), 1.0, 6.0, ((0, 16), (2, 2)))
    mask_grad = normal_values(streams_of[1], (BLOCKS, FR_DEV, MICRO, BANDS, SUBF), 1.0, 6.0, ((0, 16), (2, 2)))
    clip_starts = draw_clip_starts(jax.random.fold_in(streams_of[24], 71), 0)
    split_weight = normal_values(streams_of[3], (BANDS * SUBF, D), SUBF ** -0.5, 0.5, ((0, 16),), jnp.float32)
    split_velocity = normal_values(streams_of[4], (BANDS * SUBF, D), (PARAMS // 25) ** -0.5, 0.009765625, ((0, 16),), jnp.float32)
    split_average = normal_values(streams_of[5], (BANDS * SUBF, D), SUBF ** -0.5, 0.5, ((0, 16),), jnp.float32)
    lstm_weight = normal_values(streams_of[6], (4 * (D + H), 4 * H), (D + H) ** -0.5, 0.3125, ((0, 16),), jnp.float32)
    lstm_velocity = normal_values(streams_of[7], (4 * (D + H), 4 * H), (PARAMS // 25) ** -0.5, 0.009765625, ((0, 16),), jnp.float32)
    lstm_average = normal_values(streams_of[8], (4 * (D + H), 4 * H), (D + H) ** -0.5, 0.3125, ((0, 16),), jnp.float32)
    proj_weight = normal_values(streams_of[9], (4 * H, D), (H // 2) ** -0.5, 0.5, ((0, 16),), jnp.float32)
    proj_velocity = normal_values(streams_of[10], (4 * H, D), (PARAMS // 25) ** -0.5, 0.009765625, ((0, 16),), jnp.float32)
    proj_average = normal_values(streams_of[11], (4 * H, D), (H // 2) ** -0.5, 0.5, ((0, 16),), jnp.float32)
    up_weight = normal_values(streams_of[12], (BANDS * D, 4 * D), D ** -0.5, 0.5, ((0, 16),), jnp.float32)
    up_velocity = normal_values(streams_of[13], (BANDS * D, 4 * D), (PARAMS // 25) ** -0.5, 0.009765625, ((0, 16),), jnp.float32)
    up_average = normal_values(streams_of[14], (BANDS * D, 4 * D), D ** -0.5, 0.5, ((0, 16),), jnp.float32)
    down_weight = normal_values(streams_of[15], (4 * BANDS * D, 2 * SUBF), (4 * D) ** -0.5, 0.25, ((0, 16),), jnp.float32)
    down_velocity = normal_values(streams_of[16], (4 * BANDS * D, 2 * SUBF), (PARAMS // 25) ** -0.5, 0.009765625, ((0, 16),), jnp.float32)
    down_average = normal_values(streams_of[17], (4 * BANDS * D, 2 * SUBF), (4 * D) ** -0.5, 0.25, ((0, 16),), jnp.float32)
    gain_weight = jnp.clip(1.0 + 0.1 * jax.random.normal(streams_of[18], (2 * BANDS + 2, D), jnp.float32), 0.5, 1.5)
    gain_velocity = normal_values(streams_of[19], (2 * BANDS + 2, D), (PARAMS // 25) ** -0.5, 0.009765625, (), jnp.float32)
    gain_average = jnp.clip(1.0 + 0.18 * jax.random.normal(streams_of[20], (2 * BANDS + 2, D), jnp.float32), 0.1, 1.9)
    bias_weight = draw_bias_weight(jax.random.fold_in(streams_of[24], 71), 0)
    bias_velocity = normal_values(streams_of[22], (7 * BANDS + 16 * H // D + 2, D), (PARAMS // 25) ** -0.5, 0.009765625, (), jnp.float32)
    bias_average = normal_values(streams_of[23], (7 * BANDS + 16 * H // D + 2, D), 0.2, 1.2, (), jnp.float32)
    return {"spectra": spectra, "mask_grad": mask_grad, "clip_starts": clip_starts, "split_weight": split_weight, "split_velocity": split_velocity, "split_average": split_average, "lstm_weight": lstm_weight, "lstm_velocity": lstm_velocity, "lstm_average": lstm_average, "proj_weight": proj_weight, "proj_velocity": proj_velocity, "proj_average": proj_average, "up_weight": up_weight, "up_velocity": up_velocity, "up_average": up_average, "down_weight": down_weight, "down_velocity": down_velocity, "down_average": down_average, "gain_weight": gain_weight, "gain_velocity": gain_velocity, "gain_average": gain_average, "bias_weight": bias_weight, "bias_velocity": bias_velocity, "bias_average": bias_average}


EPSILON = 1e-05
MOMENTUM = 0.9
LEARN_RATE = 5.0
GAIN_RATE = 50.0
AVERAGE = 0.5
CLIP_NORM = 5.0
PRECISE = lax.Precision.HIGHEST

@jax.custom_vjp
def low(v):
    return lax.optimization_barrier(v.astype(jnp.bfloat16)).astype(jnp.float32)

@jax.custom_vjp
def low_back(v):
    return v

def low_keep(v):
    return (low(v), None)

def low_pass(kept, grad):
    return (grad,)

def back_keep(v):
    return (v, None)

def back_low(kept, grad):
    return (low(grad),)
low.defvjp(low_keep, low_pass)
low_back.defvjp(back_keep, back_low)

def product(pattern, left_side, right_side):
    return jnp.einsum(pattern, left_side, right_side, precision=PRECISE, preferred_element_type=jnp.float32)

def layer_norm(values, gain_row):
    centre = values - lax.optimization_barrier(jnp.mean(values, axis=-1, keepdims=True))
    spread = lax.optimization_barrier(jnp.mean(centre * centre, axis=-1, keepdims=True))
    return centre * lax.rsqrt(spread + EPSILON) * gain_row

def gate_split(gate_vals, hidden_width):
    in_gate = jax.nn.sigmoid(gate_vals[:, :hidden_width])
    forget = jax.nn.sigmoid(gate_vals[:, hidden_width:2 * hidden_width])
    candidate = jnp.tanh(gate_vals[:, 2 * hidden_width:3 * hidden_width])
    outlet = jax.nn.sigmoid(gate_vals[:, 3 * hidden_width:])
    return (in_gate, forget, candidate, outlet)

def run_lstm(gate_in, keeper, recur_mat):
    hidden_width = recur_mat.shape[0]

    def advance(carried, inputs):
        hidden, cell_state = carried
        gate_step, keep_step = inputs
        keep_col = keep_step[:, None]
        kept_hidden = hidden * keep_col
        gate_vals = low_back(gate_step + jnp.dot(kept_hidden, recur_mat, precision=PRECISE, preferred_element_type=jnp.float32))
        in_gate, forget, candidate, outlet = gate_split(gate_vals, hidden_width)
        new_cell = forget * (cell_state * keep_col) + in_gate * candidate
        new_hidden = low(outlet * jnp.tanh(new_cell))
        return ((new_hidden, new_cell), new_hidden)
    zero_state = jnp.zeros((gate_in.shape[1], hidden_width), jnp.float32)
    return lax.scan(jax.checkpoint(advance), (zero_state, zero_state), (gate_in, keeper))[1]

def both_ways(gate_fore, gate_back, keep_fore, keep_back, recur_fore, recur_back):
    forward_hidden = run_lstm(gate_fore, keep_fore, recur_fore)
    reverse_hidden = run_lstm(gate_back[::-1], keep_back[::-1], recur_back)[::-1]
    return jnp.concatenate([low_back(forward_hidden), low_back(reverse_hidden)], axis=-1)

def unpack(gain_weight, bias_weight):
    lstm_rows = 16 * H // D
    proj_start = BANDS + lstm_rows
    up_start = proj_start + 2
    down_start = up_start + 4 * BANDS
    return (gain_weight[:BANDS], gain_weight[BANDS], gain_weight[BANDS + 1], gain_weight[BANDS + 2:], bias_weight[:BANDS], bias_weight[BANDS:proj_start].reshape(4, 4 * H), bias_weight[proj_start:up_start], bias_weight[up_start:down_start].reshape(BANDS, 4 * D), bias_weight[down_start:].reshape(BANDS, 2 * SUBF))

def forward(spectrum, start_flags, split_weight, lstm_weight, proj_weight, up_weight, down_weight, gain_weight, bias_weight):
    frames, seq_count = start_flags.shape
    split_mat = low(split_weight).reshape(BANDS, SUBF, D)
    lstm_mat = low(lstm_weight).reshape(4, D + H, 4 * H)
    proj_mat = low(proj_weight).reshape(2, 2 * H, D)
    up_mat = low(up_weight).reshape(BANDS, D, 4 * D)
    down_mat = low(down_weight).reshape(BANDS, 4 * D, 2 * SUBF)
    split_gain, time_gain, band_gain, mask_gain, split_bias, lstm_bias, proj_bias, up_bias, down_bias = unpack(gain_weight, bias_weight)
    normed = low(layer_norm(spectrum, split_gain))
    embedded = low_back(product('fmbs,bsd->fmbd', normed, split_mat) + split_bias)
    next_flags = jnp.concatenate([start_flags[1:], jnp.zeros((1, seq_count), jnp.float32)], axis=0)
    keep_fore = jnp.repeat(1.0 - start_flags, BANDS, axis=1)
    keep_back = jnp.repeat(1.0 - next_flags, BANDS, axis=1)
    time_rows = low(layer_norm(embedded, time_gain))
    gate_fore = (product('fmbd,dg->fmbg', time_rows, lstm_mat[0, :D]) + lstm_bias[0]).reshape(frames, seq_count * BANDS, 4 * H)
    gate_back = (product('fmbd,dg->fmbg', time_rows, lstm_mat[1, :D]) + lstm_bias[1]).reshape(frames, seq_count * BANDS, 4 * H)
    time_joined = both_ways(gate_fore, gate_back, keep_fore, keep_back, lstm_mat[0, D:], lstm_mat[1, D:]).reshape(frames, seq_count, BANDS, 2 * H)
    after_time = embedded + low_back(product('fmbh,hd->fmbd', time_joined, proj_mat[0]) + proj_bias[0])
    band_rows = low(layer_norm(after_time, band_gain))
    band_fore = (product('fmbd,dg->bfmg', band_rows, lstm_mat[2, :D]) + lstm_bias[2]).reshape(BANDS, frames * seq_count, 4 * H)
    band_back = (product('fmbd,dg->bfmg', band_rows, lstm_mat[3, :D]) + lstm_bias[3]).reshape(BANDS, frames * seq_count, 4 * H)
    band_keep = jnp.ones((BANDS, frames * seq_count), jnp.float32)
    band_joined = both_ways(band_fore, band_back, band_keep, band_keep, lstm_mat[2, D:], lstm_mat[3, D:])
    band_joined = jnp.moveaxis(band_joined.reshape(BANDS, frames, seq_count, 2 * H), 0, 2)
    after_band = after_time + low_back(product('fmbh,hd->fmbd', band_joined, proj_mat[1]) + proj_bias[1])
    mask_in = low(layer_norm(after_band, mask_gain))
    hidden_act = low(jnp.tanh(low_back(product('fmbd,bde->fmbe', mask_in, up_mat) + up_bias)))
    output_pre = low_back(product('fmbe,bes->fmbs', hidden_act, down_mat) + down_bias)
    return output_pre[..., :SUBF] * jax.nn.sigmoid(output_pre[..., SUBF:])

def update(gradient, velocity, weight_now, average, clip_scale, rate):
    clipped = gradient * clip_scale
    velocity_new = MOMENTUM * velocity + clipped
    weight_new = weight_now - rate * (clipped + MOMENTUM * velocity_new)
    average_new = AVERAGE * average + (1.0 - AVERAGE) * weight_new
    return (clipped, velocity_new, weight_new, average_new)

def reference(spectra, mask_grad, clip_starts, split_weight, split_velocity, split_average, lstm_weight, lstm_velocity, lstm_average, proj_weight, proj_velocity, proj_average, up_weight, up_velocity, up_average, down_weight, down_velocity, down_average, gain_weight, gain_velocity, gain_average, bias_weight, bias_velocity, bias_average):
    groups = BLOCKS // CHAIN
    spectrum_groups = spectra.astype(jnp.float32).reshape(groups, CHAIN * FR_DEV, MICRO, BANDS, SUBF)
    cotangent_groups = mask_grad.astype(jnp.float32).reshape(groups, CHAIN * FR_DEV, MICRO, BANDS, SUBF)
    flag_groups = clip_starts.astype(jnp.float32).reshape(groups, CHAIN * FR_DEV, MICRO)
    weights = (split_weight, lstm_weight, proj_weight, up_weight, down_weight, gain_weight, bias_weight)

    def one_group(totals, inputs):
        spectrum, cotangent, start_flags = inputs

        def local_forward(spectrum_in, split_in, lstm_in, proj_in, up_in, down_in, gain_in, bias_in):
            return forward(spectrum_in, start_flags, split_in, lstm_in, proj_in, up_in, down_in, gain_in, bias_in)
        result, pullback = jax.vjp(local_forward, spectrum, *weights)
        grads = pullback(cotangent)
        new_totals = tuple((total_part + grad_part for total_part, grad_part in zip(totals, grads[1:])))
        return (new_totals, (result, grads[0]))
    initial = tuple((jnp.zeros_like(weight_part) for weight_part in weights))
    totals, (masks, spectrum_grads) = lax.scan(one_group, initial, (spectrum_groups, cotangent_groups, flag_groups))
    square = sum((jnp.sum(part * part) for part in totals))
    grad_norm = jnp.sqrt(square)
    clip_scale = jnp.minimum(1.0, CLIP_NORM / (grad_norm + 1e-06))
    band_mask = masks.reshape(spectra.shape).astype(jnp.bfloat16)
    spectra_grad = spectrum_grads.reshape(spectra.shape)
    split_out = update(totals[0], split_velocity, split_weight, split_average, clip_scale, LEARN_RATE)
    lstm_out = update(totals[1], lstm_velocity, lstm_weight, lstm_average, clip_scale, LEARN_RATE)
    proj_out = update(totals[2], proj_velocity, proj_weight, proj_average, clip_scale, LEARN_RATE)
    up_out = update(totals[3], up_velocity, up_weight, up_average, clip_scale, LEARN_RATE)
    down_out = update(totals[4], down_velocity, down_weight, down_average, clip_scale, LEARN_RATE)
    gain_out = update(totals[5], gain_velocity, gain_weight, gain_average, clip_scale, GAIN_RATE)
    bias_out = update(totals[6], bias_velocity, bias_weight, bias_average, clip_scale, GAIN_RATE)
    return (band_mask, spectra_grad, grad_norm, split_out[0], split_out[1], split_out[2], split_out[3], lstm_out[0], lstm_out[1], lstm_out[2], lstm_out[3], proj_out[0], proj_out[1], proj_out[2], proj_out[3], up_out[0], up_out[1], up_out[2], up_out[3], down_out[0], down_out[1], down_out[2], down_out[3], gain_out[0], gain_out[1], gain_out[2], gain_out[3], bias_out[0], bias_out[1], bias_out[2], bias_out[3])
```

```python
import functools

import jax
import jax.numpy as jnp
import numpy as np
from jax import lax
from jax.experimental import pallas as pl
from jax.experimental.pallas import tpu as pltpu
from jax.sharding import PartitionSpec as P

D = 128
H = 256
G4 = 4 * H
BANDS = 41
SUBF = 128
CHAIN = 4
SLOTS = 11
STRIDE = 10
ROWS_T = 16
STEPS_B = 42
VMEM = 60 << 20

EPSILON = 1e-05
MOMENTUM = 0.9
LEARN_RATE = 5.0
GAIN_RATE = 50.0
AVERAGE = 0.5
CLIP_NORM = 5.0

BF = jnp.bfloat16
F32 = jnp.float32


def mm(a, b):
    return jnp.dot(a, b, preferred_element_type=F32)


def mm_nt(a, b):
    return lax.dot_general(a, b, (((1,), (1,)), ((), ())), preferred_element_type=F32)


def mm_tn(a, b):
    return lax.dot_general(a, b, (((0,), (0,)), ((), ())), preferred_element_type=F32)


def ln(v):
    c = v - jnp.mean(v, axis=-1, keepdims=True)
    r = lax.rsqrt(jnp.mean(c * c, axis=-1, keepdims=True) + EPSILON)
    return c * r, r


def ln_back(n, r, gain, dy):
    dg = dy * gain
    return r * (
        dg - jnp.mean(dg, axis=-1, keepdims=True) - n * jnp.mean(dg * n, axis=-1, keepdims=True)
    )


def rowsum(v):
    return jnp.sum(v, axis=0, keepdims=True)


def forward_chunk(keep, x_ref, w_ref, b_ref, outs, gates, hk_s, ck_s, steps, chunk, rows, unroll, hall):
    n = steps // chunk
    j = pl.program_id(0)
    first = (j * chunk, (n - 1 - j) * chunk)

    @pl.when(j == 0)
    def _():
        hk_s[...] = jnp.zeros_like(hk_s)
        ck_s[...] = jnp.zeros_like(ck_s)

    for d in range(2):
        x = x_ref[pl.ds(pl.multiple_of(first[d] * rows, chunk * rows), chunk * rows), :]
        gates[d] = mm(x, w_ref[d, :D]) + b_ref[d]

    def step(t, carry):
        new = []
        for d in range(2):
            hk, ck = carry[2 * d], carry[2 * d + 1]
            tt = t if d == 0 else chunk - 1 - t
            at = first[d] + tt
            now = keep[d * steps + at]
            later = jnp.minimum(at + 1, steps - 1) if d == 0 else jnp.maximum(at - 1, 0)
            nxt = keep[d * steps + later]
            h_ref, hk_ref, cf_ref = outs[3 * d : 3 * d + 3]
            a = gates[d, pl.ds(pl.multiple_of(tt * rows, rows), rows), :] + mm(hk, w_ref[d, D:])
            ti = jnp.tanh(a[:, :H])
            tf = jnp.tanh(a[:, H : 2 * H])
            g = jnp.tanh(a[:, 2 * H : 3 * H])
            to = jnp.tanh(a[:, 3 * H :])
            i = 0.5 * ti + 0.5
            f = 0.5 * tf + 0.5
            o = 0.5 * to + 0.5
            c = f * ck + i * g
            tc = jnp.tanh(c)
            h = o * tc
            h_low = h.astype(BF)
            hk_ref[tt] = hk
            h_ref[tt] = h_low
            if hall is not None:
                hall[d, pl.ds(pl.multiple_of(at * rows, rows), rows), :] = h_low
            cf_ref[tt, :, :H] = o * (1.0 - tc * tc)
            cf_ref[tt, :, H : 2 * H] = g * (0.5 - 0.5 * ti * ti)
            cf_ref[tt, :, 2 * H : 3 * H] = ck * (0.5 - 0.5 * tf * tf)
            cf_ref[tt, :, 3 * H : 4 * H] = i * (1.0 - g * g)
            cf_ref[tt, :, 4 * H : 5 * H] = tc * (0.5 - 0.5 * to * to)
            cf_ref[tt, :, 5 * H :] = f * now
            new += [(h * nxt).astype(BF), c * nxt]
        return tuple(new)

    done = lax.fori_loop(
        0, chunk, step, (hk_s[0], ck_s[0], hk_s[1], ck_s[1]), unroll=unroll
    )
    for d in range(2):
        hk_s[d] = done[2 * d]
        ck_s[d] = done[2 * d + 1]


def backward_chunk(
    keep, x_ref, ol, w_ref, p_ref, ins, dw, dp, db, wt, pt, da, sh, rg, ch_s, cc_s, steps, chunk, rows, unroll
):
    n = steps // chunk
    j = pl.program_id(0)
    first = ((n - 1 - j) * chunk, j * chunk)
    span = chunk * rows

    @pl.when(j == 0)
    def _():
        ch_s[...] = jnp.zeros_like(ch_s)
        cc_s[...] = jnp.zeros_like(cc_s)
        rg[...] = jnp.zeros_like(rg)
        dw[...] = jnp.zeros_like(dw)
        dp[...] = jnp.zeros_like(dp)
        db[...] = jnp.zeros_like(db)
        for d in range(2):
            wt[d] = w_ref[d].T
            pt[d] = p_ref[pl.ds(d * H, H), :].T

    at_rows = [pl.ds(pl.multiple_of(first[d] * rows, span), span) for d in range(2)]
    for d in range(2):
        sh[d] = mm(ol[at_rows[d], :], pt[d]).astype(BF)

    def step(t, carry):
        new = []
        for d in range(2):
            ch, cc = carry[2 * d], carry[2 * d + 1]
            tt = chunk - 1 - t if d == 0 else t
            now = keep[d * steps + first[d] + tt]
            cf = ins[3 * d + 2]
            here = pl.ds(pl.multiple_of(tt * rows, rows), rows)
            dh = sh[d, here, :].astype(F32) + ch
            dc = cc + dh * cf[tt, :, :H]
            da_now = jnp.concatenate(
                [
                    (dc * cf[tt, :, H : 2 * H]).astype(BF),
                    (dc * cf[tt, :, 2 * H : 3 * H]).astype(BF),
                    (dc * cf[tt, :, 3 * H : 4 * H]).astype(BF),
                    (dh * cf[tt, :, 4 * H : 5 * H]).astype(BF),
                ],
                axis=-1,
            )
            da[d, here, :] = da_now
            new += [mm(da_now, wt[d, :, D:]) * now, dc * cf[tt, :, 5 * H :]]
        return tuple(new)

    done = lax.fori_loop(0, chunk, step, (ch_s[0], cc_s[0], ch_s[1], cc_s[1]), unroll=unroll)
    ones = jnp.ones((8, span), BF)
    for d in range(2):
        ch_s[d] = done[2 * d]
        cc_s[d] = done[2 * d + 1]
        here = at_rows[d]
        grad = da[d]
        rg[here, :] = rg[here, :] + mm(grad, wt[d, :, :D])
        dw[d, :D, :] = dw[d, :D, :] + mm_tn(x_ref[here, :], grad)
        dw[d, D:, :] = dw[d, D:, :] + mm_tn(ins[3 * d + 1][...].reshape(span, H), grad)
        db[d] = db[d] + mm(ones, grad)
        at_p = pl.ds(d * H, H)
        dp[at_p, :] = dp[at_p, :] + mm_tn(ins[3 * d][...].reshape(span, H), ol[here, :])


def time_forward_kernel(
    steps, chunk, keep, sp, sm, sg, sb, tg, bg, w, b, p, pb,
    emb, at, br, xs, h0, hk0, cf0, h1, hk1, cf1,
    gates, hk_s, ck_s, xt, hall,
):
    n = steps // chunk
    j = pl.program_id(0)
    frames = sp.shape[2]

    @pl.when(j == 0)
    def _():
        xt[...] = jnp.zeros_like(xt)
        for k in range(SLOTS):
            v = sp[:, k].reshape(steps, D).astype(F32)
            normed = (ln(v)[0] * sg[pl.ds(k, 1), :]).astype(BF)
            e = mm(normed, sm[k]) + sb[pl.ds(k, 1), :]
            emb[:, k] = e.reshape(CHAIN, frames, D)
            xt[pl.ds(k, steps, stride=ROWS_T), :] = ln(e)[0] * tg[...]
        xs[...] = xt[...].astype(BF)

    forward_chunk(
        keep, xs, w, b, (h0, hk0, cf0, h1, hk1, cf1), gates, hk_s, ck_s, steps, chunk, ROWS_T, 4, hall
    )

    @pl.when(j == n - 1)
    def _():
        span = 512
        for s in range(0, steps * ROWS_T, span):
            here = pl.ds(s, span)
            xt[here, :] = mm(hall[0, here, :], p[:H]) + mm(hall[1, here, :], p[H:])
        for k in range(SLOTS):
            to = xt[pl.ds(k, steps, stride=ROWS_T), :] + pb[...]
            a = emb[:, k].reshape(steps, D) + to
            at[:, k] = a.reshape(CHAIN, frames, D)
            br[:, k] = (ln(a)[0] * bg[...]).astype(BF).reshape(CHAIN, frames, D)


def band_forward_kernel(
    steps, chunk, keep, rows_in, w, b, p,
    bo, xs, h0, hk0, cf0, h1, hk1, cf1,
    gates, hk_s, ck_s, hall,
):
    n = steps // chunk
    j = pl.program_id(0)
    frames = rows_in.shape[2]

    @pl.when(j == 0)
    def _():
        for q in range(CHAIN):
            many = STRIDE if q + 1 < CHAIN else SLOTS
            xs[pl.ds(q * STRIDE * frames, many * frames), :] = rows_in[q, :many].reshape(
                many * frames, D
            )
        xs[pl.ds(BANDS * frames, (steps - BANDS) * frames), :] = jnp.zeros(
            ((steps - BANDS) * frames, D), BF
        )

    forward_chunk(
        keep, xs, w, b, (h0, hk0, cf0, h1, hk1, cf1), gates, hk_s, ck_s, steps, chunk, frames, 1, hall
    )

    @pl.when(j == n - 1)
    def _():
        for k in range(BANDS):
            here = pl.ds(k * frames, frames)
            out = (mm(hall[0, here, :], p[:H]) + mm(hall[1, here, :], p[H:])).astype(BF)
            for q in range(CHAIN):
                if 0 <= k - q * STRIDE < SLOTS:
                    bo[q, k - q * STRIDE] = out


def mask_kernel(
    valid, at, bo, cot, um, dm, mg, ub, db, pb,
    mask, abg, abl, dum, ddm, dub, ddb, dmg, dpb,
):
    frames = at.shape[2]
    rows = CHAIN * frames
    ab = at[:, 0].reshape(rows, D) + (bo[:, 0].reshape(rows, D).astype(F32) + pb[...])
    n, r = ln(ab)
    mi = (n * mg[0]).astype(BF)
    act_f = jnp.tanh(mm(mi, um[0]) + ub[0])
    act = act_f.astype(BF)
    pre = mm(act, dm[0]) + db[0]
    value = pre[:, :SUBF]
    gate = 0.5 * jnp.tanh(0.5 * pre[:, SUBF:]) + 0.5
    mask[:, 0] = (value * gate).astype(BF).reshape(CHAIN, frames, SUBF)
    c = cot[:, 0].reshape(rows, D).astype(F32) * valid[pl.program_id(0)]
    cg = c * gate
    og = jnp.concatenate([cg.astype(BF), (cg * value * (1.0 - gate)).astype(BF)], axis=-1)
    ddb[0] = rowsum(og.astype(F32))
    ddm[0] = mm_tn(act, og).astype(BF)
    pg = (mm_nt(og, dm[0]) * (1.0 - act_f * act_f)).astype(BF)
    dub[0] = rowsum(pg.astype(F32))
    dum[0] = mm_tn(mi, pg).astype(BF)
    dy = mm_nt(pg, um[0])
    dmg[0] = rowsum(dy * n)
    grad = ln_back(n, r, mg[0], dy)
    abg[:, 0] = grad.reshape(CHAIN, frames, D)
    low = grad.astype(BF)
    abl[:, 0] = low.reshape(CHAIN, frames, D)
    dpb[0] = rowsum(low.astype(F32))


def band_backward_kernel(
    steps, chunk, keep, ol_in, xs, w, p, h0, hk0, cf0, h1, hk1, cf1,
    dw, dp, db, rows_out,
    ol, wt, pt, da, sh, rg, ch_s, cc_s,
):
    n = steps // chunk
    j = pl.program_id(0)
    frames = ol_in.shape[2]

    @pl.when(j == 0)
    def _():
        for q in range(CHAIN):
            many = STRIDE if q + 1 < CHAIN else SLOTS
            ol[pl.ds(q * STRIDE * frames, many * frames), :] = ol_in[q, :many].reshape(
                many * frames, D
            )
        ol[pl.ds(BANDS * frames, (steps - BANDS) * frames), :] = jnp.zeros(
            ((steps - BANDS) * frames, D), BF
        )

    backward_chunk(
        keep, xs, ol, w, p, (h0, hk0, cf0, h1, hk1, cf1), dw, dp, db,
        wt, pt, da, sh, rg, ch_s, cc_s, steps, chunk, frames, 1,
    )

    @pl.when(j == n - 1)
    def _():
        for q in range(CHAIN):
            many = STRIDE if q + 1 < CHAIN else SLOTS
            rows_out[q, :many] = (
                rg[pl.ds(q * STRIDE * frames, many * frames), :].astype(BF).reshape(many, frames, D)
            )
            if many < SLOTS:
                rows_out[q, many] = jnp.zeros((frames, D), BF)


def time_backward_kernel(
    steps, chunk, keep, bgrad, abg, at, emb, sp, sm, sg, tg, bg, xs, w, p, h0, hk0, cf0, h1, hk1, cf1,
    dw, dp, db, spg, dsm, dsb, dsg, dtg, dbg, dpb,
    ol, wt, pt, da, sh, rg, ch_s, cc_s, xt, atg,
):
    n = steps // chunk
    j = pl.program_id(0)
    frames = bgrad.shape[2]

    @pl.when(j == 0)
    def _():
        xt[...] = jnp.zeros_like(xt)
        dbg[...] = jnp.zeros_like(dbg)
        dtg[...] = jnp.zeros_like(dtg)
        dpb[...] = jnp.zeros_like(dpb)
        for k in range(SLOTS):
            norm, r = ln(at[:, k].reshape(steps, D))
            dy = bgrad[:, k].reshape(steps, D).astype(F32)
            dbg[...] = dbg[...] + rowsum(dy * norm)
            a = abg[:, k].reshape(steps, D) + ln_back(norm, r, bg[...], dy)
            atg[k] = a
            low = a.astype(BF).astype(F32)
            dpb[...] = dpb[...] + rowsum(low)
            xt[pl.ds(k, steps, stride=ROWS_T), :] = low
        ol[...] = xt[...].astype(BF)

    backward_chunk(
        keep, xs, ol, w, p, (h0, hk0, cf0, h1, hk1, cf1), dw, dp, db,
        wt, pt, da, sh, rg, ch_s, cc_s, steps, chunk, ROWS_T, 4,
    )

    @pl.when(j == n - 1)
    def _():
        for k in range(SLOTS):
            dy = rg[pl.ds(k, steps, stride=ROWS_T), :]
            norm, r = ln(emb[:, k].reshape(steps, D))
            dtg[...] = dtg[...] + rowsum(dy * norm)
            el = (atg[k] + ln_back(norm, r, tg[...], dy)).astype(BF)
            dsb[pl.ds(k, 1), :] = rowsum(el.astype(F32))
            gain = sg[pl.ds(k, 1), :]
            norm, r = ln(sp[:, k].reshape(steps, D).astype(F32))
            dsm[k] = mm_tn((norm * gain).astype(BF), el)
            dy = mm_nt(el, sm[k])
            dsg[pl.ds(k, 1), :] = rowsum(dy * norm)
            spg[:, k] = ln_back(norm, r, gain, dy).astype(spg.dtype).reshape(CHAIN, frames, D)


def whole(shape):
    zeros = (0,) * len(shape)
    return pl.BlockSpec(shape, lambda j: zeros)


def picked(shape, index):
    rest = (index,) + (0,) * (len(shape) - 1)
    return pl.BlockSpec(shape, lambda j: rest)


SMEM = pl.BlockSpec(memory_space=pltpu.SMEM)


def sds(shape, dtype):
    return jax.ShapeDtypeStruct(shape, dtype)


def chunk_specs(n, chunk, rows, flip):
    up = lambda j: (j, 0, 0)
    down = lambda j: (n - 1 - j, 0, 0)
    specs = []
    for way in (down, up) if flip else (up, down):
        specs += [
            pl.BlockSpec((chunk, rows, H), way),
            pl.BlockSpec((chunk, rows, H), way),
            pl.BlockSpec((chunk, rows, 6 * H), way),
        ]
    return specs


def chunk_shapes(steps, rows):
    return [
        sds((steps, rows, H), BF),
        sds((steps, rows, H), BF),
        sds((steps, rows, 6 * H), F32),
    ] * 2


def params():
    return pltpu.CompilerParams(vmem_limit_bytes=VMEM, dimension_semantics=("arbitrary",))


def time_forward(keep, sp, sm, sg, sb, tg, bg, w, b, p, pb):
    frames = sp.shape[2]
    steps, chunk = CHAIN * frames, 32
    n = steps // chunk
    slab = (CHAIN, SLOTS, frames, D)
    return pl.pallas_call(
        functools.partial(time_forward_kernel, steps, chunk),
        grid=(n,),
        in_specs=[SMEM]
        + [whole(v.shape) for v in (sp, sm, sg, sb, tg, bg)]
        + [picked((2, D + H, G4), 0), picked((2, 1, G4), 0), picked((2 * H, D), 0), whole(pb.shape)],
        out_specs=[whole(slab)] * 3
        + [whole((steps * ROWS_T, D))]
        + chunk_specs(n, chunk, ROWS_T, False),
        out_shape=[sds(slab, F32), sds(slab, F32), sds(slab, BF), sds((steps * ROWS_T, D), BF)]
        + chunk_shapes(steps, ROWS_T),
        scratch_shapes=[
            pltpu.VMEM((2, chunk * ROWS_T, G4), F32),
            pltpu.VMEM((2, ROWS_T, H), BF),
            pltpu.VMEM((2, ROWS_T, H), F32),
            pltpu.VMEM((steps * ROWS_T, D), F32),
            pltpu.VMEM((2, steps * ROWS_T, H), BF),
        ],
        compiler_params=params(),
        name="time_forward",
    )(keep, sp, sm, sg, sb, tg, bg, w, b, p, pb)


def band_forward(keep, rows_in, w, b, p):
    frames = rows_in.shape[2]
    steps, chunk = STEPS_B, 14
    n = steps // chunk
    slab = (CHAIN, SLOTS, frames, D)
    return pl.pallas_call(
        functools.partial(band_forward_kernel, steps, chunk),
        grid=(n,),
        in_specs=[SMEM, whole(slab), picked((2, D + H, G4), 1), picked((2, 1, G4), 1), picked((2 * H, D), 1)],
        out_specs=[whole(slab), whole((steps * frames, D))] + chunk_specs(n, chunk, frames, False),
        out_shape=[sds(slab, BF), sds((steps * frames, D), BF)] + chunk_shapes(steps, frames),
        scratch_shapes=[
            pltpu.VMEM((2, chunk * frames, G4), F32),
            pltpu.VMEM((2, frames, H), BF),
            pltpu.VMEM((2, frames, H), F32),
            pltpu.VMEM((2, steps * frames, H), BF),
        ],
        compiler_params=params(),
        name="band_forward",
    )(keep, rows_in, w, b, p)


def mask_stage(valid, at, bo, cot, um, dm, mg, ub, db, pb):
    frames = at.shape[2]
    slab = (CHAIN, SLOTS, frames, D)
    part = pl.BlockSpec((CHAIN, 1, frames, D), lambda k: (0, k, 0, 0))

    def band(*shape):
        return pl.BlockSpec((1,) + shape, lambda k: (k, 0, 0))

    return pl.pallas_call(
        mask_kernel,
        grid=(SLOTS,),
        in_specs=[
            SMEM, part, part, part, band(D, 4 * D), band(4 * D, 2 * SUBF),
            band(1, D), band(1, 4 * D), band(1, 2 * SUBF), whole((1, D)),
        ],
        out_specs=[
            part, part, part, band(D, 4 * D), band(4 * D, 2 * SUBF),
            band(1, 4 * D), band(1, 2 * SUBF), band(1, D), band(1, D),
        ],
        out_shape=[
            sds(slab, BF), sds(slab, F32), sds(slab, BF),
            sds((SLOTS, D, 4 * D), BF), sds((SLOTS, 4 * D, 2 * SUBF), BF),
            sds((SLOTS, 1, 4 * D), F32), sds((SLOTS, 1, 2 * SUBF), F32),
            sds((SLOTS, 1, D), F32), sds((SLOTS, 1, D), F32),
        ],
        compiler_params=params(),
        name="mask_stage",
    )(valid, at, bo, cot, um, dm, mg, ub, db, pb)


def backward_scratch(steps, chunk, rows):
    span = chunk * rows
    return [
        pltpu.VMEM((steps * rows, D), BF),
        pltpu.VMEM((2, G4, D + H), BF),
        pltpu.VMEM((2, D, H), BF),
        pltpu.VMEM((2, span, G4), BF),
        pltpu.VMEM((2, span, H), BF),
        pltpu.VMEM((steps * rows, D), F32),
        pltpu.VMEM((2, rows, H), F32),
        pltpu.VMEM((2, rows, H), F32),
    ]


def band_backward(keep, ol_in, xs, w, p, saved):
    frames = ol_in.shape[2]
    steps, chunk = STEPS_B, 14
    n = steps // chunk
    slab = (CHAIN, SLOTS, frames, D)
    return pl.pallas_call(
        functools.partial(band_backward_kernel, steps, chunk),
        grid=(n,),
        in_specs=[SMEM, whole(slab), whole(xs.shape), picked((2, D + H, G4), 1), picked((2 * H, D), 1)]
        + chunk_specs(n, chunk, frames, True),
        out_specs=[whole((2, D + H, G4)), whole((2 * H, D)), whole((2, 8, G4)), whole(slab)],
        out_shape=[sds((2, D + H, G4), F32), sds((2 * H, D), F32), sds((2, 8, G4), F32), sds(slab, BF)],
        scratch_shapes=backward_scratch(steps, chunk, frames),
        compiler_params=params(),
        name="band_backward",
    )(keep, ol_in, xs, w, p, *saved)


def time_backward(keep, bgrad, abg, at, emb, sp, sm, sg, tg, bg, xs, w, p, saved):
    frames = bgrad.shape[2]
    steps, chunk = CHAIN * frames, 32
    n = steps // chunk
    slab = (CHAIN, SLOTS, frames, D)
    outs = [
        sds((2, D + H, G4), F32), sds((2 * H, D), F32), sds((2, 8, G4), F32), sds(slab, F32),
        sds((SLOTS, SUBF, D), F32), sds((SLOTS, D), F32), sds((SLOTS, D), F32),
        sds((1, D), F32), sds((1, D), F32), sds((1, D), F32),
    ]
    return pl.pallas_call(
        functools.partial(time_backward_kernel, steps, chunk),
        grid=(n,),
        in_specs=[SMEM]
        + [whole(v.shape) for v in (bgrad, abg, at, emb, sp, sm, sg, tg, bg, xs)]
        + [picked((2, D + H, G4), 0), picked((2 * H, D), 0)]
        + chunk_specs(n, chunk, ROWS_T, True),
        out_specs=[whole(v.shape) for v in outs],
        out_shape=outs,
        scratch_shapes=backward_scratch(steps, chunk, ROWS_T)
        + [pltpu.VMEM((steps * ROWS_T, D), F32), pltpu.VMEM((SLOTS, steps, D), F32)],
        compiler_params=params(),
        name="time_backward",
    )(keep, bgrad, abg, at, emb, sp, sm, sg, tg, bg, xs, w, p, *saved)


def row_bits():
    return (lax.axis_size("rows") - 1).bit_length()


def swap_dir(v):
    return lax.ppermute(v, "dir", [(0, 1), (1, 0)])


def swap_bit(v, bit):
    return lax.ppermute(v, "rows", [(r, r ^ (1 << bit)) for r in range(lax.axis_size("rows"))])


def my_bit(bit):
    return (lax.axis_index("rows") >> bit) & 1


def chain_groups():
    many = lax.axis_size("rows") // CHAIN
    return [[CHAIN * g + q for q in range(CHAIN)] for g in range(many)]


def place_groups():
    many = lax.axis_size("rows") // CHAIN
    return [[CHAIN * g + q for g in range(many)] for q in range(CHAIN)]


def across_chain(v):
    return lax.all_to_all(v, "rows", 0, 0, axis_index_groups=chain_groups(), tiled=True)


def to_bands(v):
    return across_chain(jnp.stack([v[STRIDE * q : STRIDE * q + SLOTS] for q in range(CHAIN)]))


def to_frames(v):
    v = across_chain(v)
    return jnp.concatenate([v[q, : STRIDE if q + 1 < CHAIN else SLOTS] for q in range(CHAIN)])


def quarter_route():
    rows = lax.axis_size("rows")
    many = rows // CHAIN
    return [(s, (s % many) * CHAIN + s // many) for s in range(rows)]


def band_weights(shard, unit):
    place = lax.axis_index("rows") % CHAIN
    part = unit // CHAIN
    low = lax.ppermute(shard.astype(BF), "rows", quarter_route())
    own = lax.all_gather(low, "rows", axis=0, axis_index_groups=place_groups(), tiled=True)
    route = [(r, r + 1) for r in range(lax.axis_size("rows")) if r % CHAIN + 1 < CHAIN]
    before = lax.ppermute(own[-3 * part :], "rows", route)
    padded = jnp.concatenate([before, own, jnp.zeros_like(before)])
    start = part * (3 - place)
    found = lax.dynamic_slice_in_dim(padded, start, SLOTS * unit, 0)
    return found.reshape(SLOTS, unit, -1)


def band_totals(grads, unit):
    place = lax.axis_index("rows") % CHAIN
    part = unit // CHAIN
    rows = lax.axis_size("rows")
    route = [(r, r - 1) for r in range(rows) if r % CHAIN > 0]
    after = lax.ppermute(grads[: 3 * part], "rows", route)
    at = STRIDE * unit
    filled = jnp.concatenate([grads[:at], grads[at : at + 3 * part] + after, grads[at + 3 * part :]])
    own = lax.dynamic_slice_in_dim(filled, part * place, BANDS * unit // CHAIN, 0)
    shard = lax.psum_scatter(
        own, "rows", scatter_dimension=0, axis_index_groups=place_groups(), tiled=True
    )
    shard = lax.ppermute(shard, "rows", [(b, a) for a, b in quarter_route()])
    return shard.astype(F32) + swap_dir(shard).astype(F32)


def half_totals(grads):
    bits = row_bits() - 1
    half = 1 << bits
    v = grads.reshape(half, 2, grads.shape[0] // half // 2, grads.shape[1])
    side = lax.axis_index("dir")
    v = lax.dynamic_index_in_dim(v, side, 1, False) + swap_dir(
        lax.dynamic_index_in_dim(v, 1 - side, 1, False).astype(BF)
    ).astype(F32)
    for bit in range(bits):
        v = v.reshape(v.shape[0] // 2, 2, *v.shape[1:])
        mine = my_bit(bit)
        v = lax.dynamic_index_in_dim(v, mine, 1, False) + swap_bit(
            lax.dynamic_index_in_dim(v, 1 - mine, 1, False).astype(BF), bit
        ).astype(F32)
    v = v[0]
    v = (v + swap_bit(v.astype(BF), bits).astype(F32)).astype(BF)
    other = swap_dir(v)
    return jnp.where(
        side == 0, jnp.concatenate([v, other]), jnp.concatenate([other, v])
    ).astype(F32)


def sum_all(v, dirs):
    if dirs:
        v = v + swap_dir(v)
    for bit in range(row_bits()):
        v = v + swap_bit(v, bit)
    return v


def update(gradient, velocity, weight_now, average, clip_scale, rate):
    clipped = gradient * clip_scale
    velocity_new = MOMENTUM * velocity + clipped
    weight_new = weight_now - rate * (clipped + MOMENTUM * velocity_new)
    average_new = AVERAGE * average + (1.0 - AVERAGE) * weight_new
    return (clipped, velocity_new, weight_new, average_new)


def halved_columns():
    scale = np.full((1, G4), 0.5, np.float32)
    scale[:, 2 * H : 3 * H] = 1.0
    return jnp.asarray(scale)


def on_device(
    spectra,
    mask_grad,
    clip_starts,
    split_weight,
    split_velocity,
    split_average,
    lstm_weight,
    lstm_velocity,
    lstm_average,
    proj_weight,
    proj_velocity,
    proj_average,
    up_weight,
    up_velocity,
    up_average,
    down_weight,
    down_velocity,
    down_average,
    gain_weight,
    gain_velocity,
    gain_average,
    bias_weight,
    bias_velocity,
    bias_average,
):
    side = lax.axis_index("dir")
    row = lax.axis_index("rows")
    place = row % CHAIN
    last_place = place == CHAIN - 1
    frames = spectra.shape[1]
    steps = CHAIN * frames
    scale = halved_columns()

    lstm_mat = lax.all_gather((lstm_weight * scale).astype(BF), "rows", axis=0, tiled=True).reshape(
        4, D + H, G4
    )
    split_mat = band_weights(split_weight, SUBF)
    proj_mat = lax.all_gather(proj_weight.astype(BF), "rows", axis=0, tiled=True)
    up_mat = band_weights(up_weight, D)
    down_mat = band_weights(down_weight, 4 * D)
    first = STRIDE * place

    def mine(rows):
        return lax.dynamic_slice_in_dim(rows, first, SLOTS, 0)

    o_lstm = BANDS
    o_proj = o_lstm + 16 * H // D
    o_up = o_proj + 2
    o_down = o_up + 4 * BANDS
    split_gain = mine(gain_weight[:BANDS])
    time_gain = gain_weight[BANDS : BANDS + 1]
    band_gain = gain_weight[BANDS + 1 : BANDS + 2]
    mask_gain = mine(gain_weight[BANDS + 2 :])[:, None]
    split_bias = mine(bias_weight[:BANDS])
    lstm_bias = (bias_weight[o_lstm:o_proj].reshape(4, G4) * scale)[:, None]
    time_pb = bias_weight[o_proj : o_proj + 1]
    band_pb = bias_weight[o_proj + 1 : o_up]
    up_bias = mine(bias_weight[o_up:o_down].reshape(BANDS, 4 * D))[:, None]
    down_bias = mine(bias_weight[o_down:].reshape(BANDS, 2 * SUBF))[:, None]

    flags = lax.dynamic_index_in_dim(clip_starts[0], side, 1, False).astype(BF)
    flag_slab = jnp.broadcast_to(flags[:, None], (frames, SUBF))
    spec = jnp.transpose(spectra[0, :, 0], (1, 0, 2))
    sent = jnp.stack(
        [
            jnp.concatenate([spec[STRIDE * q : STRIDE * q + SLOTS], flag_slab[None]])
            for q in range(CHAIN)
        ]
    )
    sp = across_chain(sent)
    starts = sp[:, SLOTS, :, 0].reshape(steps).astype(F32)
    keep_time = jnp.concatenate([1.0 - starts, 1.0 - starts[1:], jnp.ones((1,), F32)])
    keep_np = np.ones((2 * STEPS_B,), np.float32)
    keep_np[STEPS_B + BANDS - 1] = 0.0
    keep_band = jnp.asarray(keep_np)
    cot = to_bands(jnp.transpose(mask_grad[0, :, 0], (1, 0, 2)))
    valid = jnp.concatenate([jnp.ones((SLOTS - 1,), F32), last_place.astype(F32)[None]])

    emb, after_time, band_rows, xs_t, *saved_t = time_forward(
        keep_time, sp, split_mat, split_gain, split_bias, time_gain, band_gain, lstm_mat, lstm_bias, proj_mat, time_pb
    )
    band_out, xs_b, *saved_b = band_forward(
        keep_band, across_chain(band_rows), lstm_mat, lstm_bias, proj_mat
    )
    band_out = across_chain(band_out)
    mask, abg, abl, d_up, d_down, d_ub, d_db, d_mg, d_bpb = mask_stage(
        valid, after_time, band_out, cot, up_mat, down_mat, mask_gain, up_bias, down_bias, band_pb
    )
    band_mask = jnp.transpose(to_frames(mask), (1, 0, 2))[None, :, None]

    up_total = band_totals(d_up.reshape(SLOTS * D, 4 * D), D)
    down_total = band_totals(d_down.reshape(SLOTS * 4 * D, 2 * SUBF), 4 * D)
    dw_b, dp_b, db_b, bgrad = band_backward(
        keep_band, across_chain(abl), xs_b, lstm_mat, proj_mat, saved_b
    )
    dw_t, dp_t, db_t, spg, d_split, d_sb, d_sg, d_tg, d_bg, d_tpb = time_backward(
        keep_time, across_chain(bgrad), abg, after_time, emb, sp, split_mat, split_gain, time_gain, band_gain,
        xs_t, lstm_mat, proj_mat, saved_t,
    )
    spectra_grad = jnp.transpose(to_frames(spg), (1, 0, 2))[None, :, None]

    lstm_t = half_totals(dw_t.reshape(2 * (D + H), G4) * scale)
    lstm_b = half_totals(dw_b.reshape(2 * (D + H), G4) * scale)
    proj_t = half_totals(dp_t)
    proj_b = half_totals(dp_b)
    upper = row >= lax.axis_size("rows") // 2
    lstm_total = jnp.where(upper, lstm_b, lstm_t)
    proj_total = jnp.where(upper, proj_b, proj_t)
    split_total = band_totals(d_split.reshape(SLOTS * SUBF, D).astype(BF), SUBF)

    def placed(part):
        wide = jnp.zeros((BANDS,) + part.shape[1:], F32)
        kept = jnp.where(
            (jnp.arange(SLOTS) < STRIDE)[:, None] | last_place, part, 0.0
        )
        return lax.dynamic_update_slice_in_dim(wide, kept, first, 0)

    db_all = jnp.concatenate([db_t[:, 0], db_b[:, 0]]) * scale
    small = jnp.concatenate(
        [
            placed(d_sg),
            d_tg,
            d_bg,
            placed(d_mg[:, 0]),
            placed(d_sb),
            db_all.reshape(16 * H // D, D),
            d_tpb,
            jnp.sum(d_bpb, axis=0),
            placed(d_ub[:, 0]).reshape(4 * BANDS, D),
            placed(d_db[:, 0]).reshape(2 * BANDS, D),
        ]
    )
    small = sum_all(small, True)
    gain_total = small[: 2 * BANDS + 2]
    bias_total = small[2 * BANDS + 2 :]

    shards = (split_total, lstm_total, proj_total, up_total, down_total)
    square = sum(jnp.sum(v * v) for v in shards)
    square = sum_all(jnp.full((8, 128), square, F32), False)[0, 0]
    grad_norm = jnp.sqrt(square + jnp.sum(small * small))
    clip_scale = jnp.minimum(1.0, CLIP_NORM / (grad_norm + 1e-06))
    outputs = (band_mask, spectra_grad, grad_norm)
    olds = (
        (split_velocity, split_weight, split_average),
        (lstm_velocity, lstm_weight, lstm_average),
        (proj_velocity, proj_weight, proj_average),
        (up_velocity, up_weight, up_average),
        (down_velocity, down_weight, down_average),
    )
    for total, old in zip(shards, olds):
        outputs += update(total, *old, clip_scale, LEARN_RATE)
    outputs += update(gain_total, gain_velocity, gain_weight, gain_average, clip_scale, GAIN_RATE)
    outputs += update(bias_total, bias_velocity, bias_weight, bias_average, clip_scale, GAIN_RATE)
    return outputs


def solution(mesh):
    per_row = P("rows", None)
    row_major = P("rows", None, "dir", None, None)
    return jax.shard_map(
        on_device,
        mesh=mesh,
        in_specs=(row_major, row_major, P("rows", None, None)) + (per_row,) * 15 + (P(),) * 6,
        out_specs=(row_major, row_major, P()) + (per_row,) * 20 + (P(),) * 8,
        check_vma=False,
    )
```

```python
import functools

import jax
import jax.numpy as jnp
import numpy as np
from jax import lax
from jax.experimental import pallas as pl
from jax.experimental.pallas import tpu as pltpu
from jax.sharding import PartitionSpec as P

D = 128
H = 256
G4 = 4 * H
BANDS = 41
SUBF = 128
CHAIN = 4
SLOTS = 12
FILL = 128
ROWS_T = 16
STEPS_B = 42
VMEM = 60 << 20
HALF = (D + H) // CHAIN // 2
HALF_P = H // CHAIN // 2

EPSILON = 1e-05
MOMENTUM = 0.9
LEARN_RATE = 5.0
GAIN_RATE = 50.0
AVERAGE = 0.5
CLIP_NORM = 5.0


GAIN_TIME, GAIN_BAND, GAIN_MASK = BANDS, BANDS + 1, BANDS + 2
BIAS_LSTM = BANDS
BIAS_PROJ = BIAS_LSTM + 16 * H // D
BIAS_UP = BIAS_PROJ + 2
BIAS_DOWN = BIAS_UP + 4 * BANDS
EARLY_BIAS = BANDS
EARLY = EARLY_BIAS + BIAS_DOWN + 2 * BANDS - BIAS_PROJ - 1
EARLY_ROWS = -(-EARLY // 16) * 16
LATE_BIAS = GAIN_MASK
LATE = LATE_BIAS + BIAS_PROJ + 1
LATE_ROWS = -(-LATE // 16) * 16

BF = jnp.bfloat16
F32 = jnp.float32


def mm(a, b):
    return jnp.dot(a, b, preferred_element_type=F32)


def mm_nt(a, b):
    return lax.dot_general(a, b, (((1,), (1,)), ((), ())), preferred_element_type=F32)


def mm_tn(a, b):
    return lax.dot_general(a, b, (((0,), (0,)), ((), ())), preferred_element_type=F32)


def ln(v):
    c = v - jnp.mean(v, axis=-1, keepdims=True)
    r = lax.rsqrt(jnp.mean(c * c, axis=-1, keepdims=True) + EPSILON)
    return c * r, r


def ln_back(n, r, gain, dy):
    dg = dy * gain
    return r * (
        dg - jnp.mean(dg, axis=-1, keepdims=True) - n * jnp.mean(dg * n, axis=-1, keepdims=True)
    )


def rowsum(v):
    return jnp.sum(v, axis=0, keepdims=True)


UP_PART = 2 * D
MASK_PART = UP_PART + 4 * D
PROJ_PART = 2 * CHAIN * HALF_P
MISC_SPLIT = 2 * PROJ_PART
MISC_LATE = MISC_SPLIT + SLOTS * SUBF
MISC_EARLY = MISC_LATE + LATE_ROWS
MISC = MISC_EARLY + EARLY_ROWS


def shard_start(shard, rows):
    return -(-shard * BANDS // rows)


def band_blocks(rows):
    if rows == CHAIN * CHAIN:
        three = SLOTS // CHAIN
        return [
            [
                (shard_start(CHAIN * z + q, rows), three, shard_start(CHAIN * z + q + 1, rows) - shard_start(CHAIN * z + q, rows))
                for z in range(CHAIN)
            ]
            for q in range(CHAIN)
        ]
    each = BANDS // CHAIN
    return [[(each * q, SLOTS, each if q + 1 < CHAIN else BANDS - each * q)] for q in range(CHAIN)]


def band_table(rows):
    return [
        [first + i if i < filled else -1 for first, places, filled in blocks for i in range(places)]
        for blocks in band_blocks(rows)
    ]


def wide_row(rows, first, many):
    return jnp.concatenate([rows[pl.ds(first + i, 1), :] for i in range(many)], axis=1)


def forward_chunk(keep, x_ref, w_ref, bias, scale, first_row, outs, gates, hk_s, ck_s, steps, chunk, rows, unroll, hall):
    n = steps // chunk
    j = pl.program_id(0)
    first = (j * chunk, (n - 1 - j) * chunk)

    @pl.when(j == 0)
    def _():
        hk_s[...] = jnp.zeros_like(hk_s)
        ck_s[...] = jnp.zeros_like(ck_s)

    for d in range(2):
        x = x_ref[pl.ds(pl.multiple_of(first[d] * rows, chunk * rows), chunk * rows), :]
        b = wide_row(bias, first_row + d * (G4 // D), G4 // D) * scale[...]
        gates[d] = mm(x, w_ref[d, :D]) + b

    def step(t, carry):
        new = []
        for d in range(2):
            hk, ck = carry[2 * d], carry[2 * d + 1]
            tt = t if d == 0 else chunk - 1 - t
            at = first[d] + tt
            now = keep[d * steps + at]
            later = jnp.minimum(at + 1, steps - 1) if d == 0 else jnp.maximum(at - 1, 0)
            nxt = keep[d * steps + later]
            h_ref, hk_ref, cf_ref = outs[3 * d : 3 * d + 3]
            a = gates[d, pl.ds(pl.multiple_of(tt * rows, rows), rows), :] + mm(hk, w_ref[d, D:])
            ti = jnp.tanh(a[:, :H])
            tf = jnp.tanh(a[:, H : 2 * H])
            g = jnp.tanh(a[:, 2 * H : 3 * H])
            to = jnp.tanh(a[:, 3 * H :])
            i = 0.5 * ti + 0.5
            f = 0.5 * tf + 0.5
            o = 0.5 * to + 0.5
            c = f * ck + i * g
            tc = jnp.tanh(c)
            h = o * tc
            h_low = h.astype(BF)
            hk_ref[tt] = hk
            h_ref[tt] = h_low
            if hall is not None:
                hall[d, pl.ds(pl.multiple_of(at * rows, rows), rows), :] = h_low
            cf_ref[tt, :, :H] = o * (1.0 - tc * tc)
            cf_ref[tt, :, H : 2 * H] = g * (0.5 - 0.5 * ti * ti)
            cf_ref[tt, :, 2 * H : 3 * H] = ck * (0.5 - 0.5 * tf * tf)
            cf_ref[tt, :, 3 * H : 4 * H] = i * (1.0 - g * g)
            cf_ref[tt, :, 4 * H : 5 * H] = tc * (0.5 - 0.5 * to * to)
            cf_ref[tt, :, 5 * H :] = f * now
            new += [(h * nxt).astype(BF), c * nxt]
        return tuple(new)

    done = lax.fori_loop(
        0, chunk, step, (hk_s[0], ck_s[0], hk_s[1], ck_s[1]), unroll=unroll
    )
    for d in range(2):
        hk_s[d] = done[2 * d]
        ck_s[d] = done[2 * d + 1]


def backward_chunk(
    keep, x_ref, ol, w_ref, p_ref, ins, dw, dp, db, wt, pt, da, sh, rg, ch_s, cc_s, steps, chunk, rows, unroll
):
    n = steps // chunk
    j = pl.program_id(0)
    first = ((n - 1 - j) * chunk, j * chunk)
    span = chunk * rows

    @pl.when(j == 0)
    def _():
        ch_s[...] = jnp.zeros_like(ch_s)
        cc_s[...] = jnp.zeros_like(cc_s)
        rg[...] = jnp.zeros_like(rg)
        dw[...] = jnp.zeros_like(dw)
        dp[...] = jnp.zeros_like(dp)
        db[...] = jnp.zeros_like(db)
        for d in range(2):
            wt[d] = w_ref[d].T
            pt[d] = p_ref[pl.ds(d * H, H), :].T

    at_rows = [pl.ds(pl.multiple_of(first[d] * rows, span), span) for d in range(2)]
    for d in range(2):
        sh[d] = mm(ol[at_rows[d], :], pt[d]).astype(BF)

    def step(t, carry):
        new = []
        for d in range(2):
            ch, cc = carry[2 * d], carry[2 * d + 1]
            tt = chunk - 1 - t if d == 0 else t
            now = keep[d * steps + first[d] + tt]
            cf = ins[3 * d + 2]
            here = pl.ds(pl.multiple_of(tt * rows, rows), rows)
            dh = sh[d, here, :].astype(F32) + ch
            dc = cc + dh * cf[tt, :, :H]
            da_now = jnp.concatenate(
                [
                    (dc * cf[tt, :, H : 2 * H]).astype(BF),
                    (dc * cf[tt, :, 2 * H : 3 * H]).astype(BF),
                    (dc * cf[tt, :, 3 * H : 4 * H]).astype(BF),
                    (dh * cf[tt, :, 4 * H : 5 * H]).astype(BF),
                ],
                axis=-1,
            )
            da[d, here, :] = da_now
            new += [mm(da_now, wt[d, :, D:]) * now, dc * cf[tt, :, 5 * H :]]
        return tuple(new)

    done = lax.fori_loop(0, chunk, step, (ch_s[0], cc_s[0], ch_s[1], cc_s[1]), unroll=unroll)
    ones = jnp.ones((8, span), BF)
    for d in range(2):
        ch_s[d] = done[2 * d]
        cc_s[d] = done[2 * d + 1]
        here = at_rows[d]
        grad = da[d]
        rg[here, :] = rg[here, :] + mm(grad, wt[d, :, :D])
        dw[d, :D, :] = dw[d, :D, :] + mm_tn(x_ref[here, :], grad)
        dw[d, D:, :] = dw[d, D:, :] + mm_tn(ins[3 * d + 1][...].reshape(span, H), grad)
        db[d] = db[d] + mm(ones, grad)
        at_p = pl.ds(d * H, H)
        dp[at_p, :] = dp[at_p, :] + mm_tn(ins[3 * d][...].reshape(span, H), ol[here, :])


def lay_weights(side, near, far, w):
    for way in range(2):
        for q in range(CHAIN):
            for part, of in ((near, side), (far, 1 - side)):
                at = pl.multiple_of(q * 2 * HALF + of * HALF, HALF)
                w[way, pl.ds(at, HALF), :] = part[q, way, :HALF, :]


def part_totals(side, dw, dp, scale, keep_w, send_w, keep_p, send_p):
    for way in range(2):
        for q in range(CHAIN):
            for k_ref, of in ((keep_w, side), (send_w, 1 - side)):
                at = pl.multiple_of(q * 2 * HALF + of * HALF, HALF)
                k_ref[q, way] = (dw[way, pl.ds(at, HALF), :] * scale[...]).astype(BF)
            for k_ref, of in ((keep_p, side), (send_p, 1 - side)):
                at = pl.multiple_of(way * H + q * 2 * HALF_P + of * HALF_P, HALF_P)
                k_ref[pl.ds((q * 2 + way) * HALF_P, HALF_P), :] = dp[pl.ds(at, HALF_P), :].astype(BF)


def bias_total(db, scale, out, first):
    for way in range(2):
        row = db[way, :1, :] * scale[...]
        for i in range(G4 // D):
            out[pl.ds(first + way * (G4 // D) + i, 1), :] = row[:, i * D : (i + 1) * D]


def time_forward_kernel(
    steps, chunk, keep, bands, side, sp, sm, gain, bias, scale, near, far, p, _,
    emb, at, br, xs, w, _out, h0, hk0, cf0, h1, hk1, cf1,
    gates, hk_s, ck_s, xt, hall,
):
    n = steps // chunk
    j = pl.program_id(0)
    frames = sp.shape[2]

    @pl.when(j == 0)
    def _():
        lay_weights(side[0], near, far, w)
        xt[...] = jnp.zeros_like(xt)
        for k in range(SLOTS):
            v = sp[:, k].reshape(steps, D).astype(F32)
            normed = (ln(v)[0] * gain[pl.ds(bands[k], 1), :]).astype(BF)
            e = mm(normed, sm[k]) + bias[pl.ds(bands[k], 1), :]
            emb[:, k] = e.reshape(CHAIN, frames, D)
            xt[pl.ds(k, steps, stride=ROWS_T), :] = ln(e)[0] * gain[pl.ds(GAIN_TIME, 1), :]
        xs[...] = xt[...].astype(BF)

    forward_chunk(
        keep, xs, w, bias, scale, BIAS_LSTM, (h0, hk0, cf0, h1, hk1, cf1), gates, hk_s, ck_s, steps, chunk, ROWS_T, 4, hall
    )

    @pl.when(j == n - 1)
    def _():
        span = 512
        for s in range(0, steps * ROWS_T, span):
            here = pl.ds(s, span)
            xt[here, :] = mm(hall[0, here, :], p[:H]) + mm(hall[1, here, :], p[H:])
        for k in range(SLOTS):
            to = xt[pl.ds(k, steps, stride=ROWS_T), :] + bias[pl.ds(BIAS_PROJ, 1), :]
            a = emb[:, k].reshape(steps, D) + to
            at[:, k] = a.reshape(CHAIN, frames, D)
            br[:, k] = (ln(a)[0] * gain[pl.ds(GAIN_BAND, 1), :]).astype(BF).reshape(CHAIN, frames, D)


def band_forward_kernel(
    steps, chunk, table, keep, side, rows_in, near, far, bias, scale, p,
    bo, xs, w, h0, hk0, cf0, h1, hk1, cf1,
    gates, hk_s, ck_s, hall,
):
    n = steps // chunk
    j = pl.program_id(0)
    frames = rows_in.shape[2]

    @pl.when(j == 0)
    def _():
        lay_weights(side[0], near, far, w)
        for q in range(CHAIN):
            for k in range(SLOTS):
                if table[q][k] >= 0:
                    xs[pl.ds(table[q][k] * frames, frames), :] = rows_in[q, k]
        xs[pl.ds(BANDS * frames, (steps - BANDS) * frames), :] = jnp.zeros(
            ((steps - BANDS) * frames, D), BF
        )

    forward_chunk(
        keep, xs, w, bias, scale, BIAS_LSTM + 2 * G4 // D, (h0, hk0, cf0, h1, hk1, cf1), gates, hk_s, ck_s, steps, chunk, frames, 1, hall
    )

    @pl.when(j == n - 1)
    def _():
        for q in range(CHAIN):
            for k in range(SLOTS):
                here = pl.ds(max(table[q][k], 0) * frames, frames)
                bo[q, k] = (mm(hall[0, here, :], p[:H]) + mm(hall[1, here, :], p[H:])).astype(BF)


def mask_kernel(
    bands, valid, side, at, bo, cot, um, dm, gain, bias,
    mask, abg, abl, kept, sent, early,
):
    frames = at.shape[2]
    rows = CHAIN * frames

    k = pl.program_id(0)
    band = bands[k]

    @pl.when(k == 0)
    def _():
        early[...] = jnp.zeros_like(early)

    def halves(v, first):
        half = v.shape[1] // 2
        lower = side[0] == 0
        near = jnp.where(lower, v[:, :half], v[:, half:]).astype(BF)
        far = jnp.where(lower, v[:, half:], v[:, :half]).astype(BF)
        many = v.shape[0]
        for i in range(half // D):
            kept[0, first + i * many : first + (i + 1) * many, :] = near[:, i * D : (i + 1) * D]
            sent[0, first + i * many : first + (i + 1) * many, :] = far[:, i * D : (i + 1) * D]

    ab = at[:, 0].reshape(rows, D) + (bo[:, 0].reshape(rows, D).astype(F32) + bias[pl.ds(BIAS_PROJ + 1, 1), :])
    n, r = ln(ab)
    mg = gain[pl.ds(GAIN_MASK + band, 1), :]
    mi = (n * mg).astype(BF)
    act_f = jnp.tanh(mm(mi, um[0]) + wide_row(bias, BIAS_UP + 4 * band, 4))
    act = act_f.astype(BF)
    pre = mm(act, dm[0]) + wide_row(bias, BIAS_DOWN + 2 * band, 2)
    value = pre[:, :SUBF]
    gate = 0.5 * jnp.tanh(0.5 * pre[:, SUBF:]) + 0.5
    mask[:, 0] = (value * gate).astype(BF).reshape(CHAIN, frames, SUBF)
    c = cot[:, 0].reshape(rows, D).astype(F32) * valid[k]
    cg = c * gate
    og = jnp.concatenate([cg.astype(BF), (cg * value * (1.0 - gate)).astype(BF)], axis=-1)
    ddb = rowsum(og.astype(F32))
    halves(mm_tn(act, og), UP_PART)
    pg = (mm_nt(og, dm[0]) * (1.0 - act_f * act_f)).astype(BF)
    dub = rowsum(pg.astype(F32))
    halves(mm_tn(mi, pg), 0)
    dy = mm_nt(pg, um[0])
    dmg = rowsum(dy * n)
    grad = ln_back(n, r, mg, dy)
    abg[:, 0] = grad.reshape(CHAIN, frames, D)
    low = grad.astype(BF)
    abl[:, 0] = low.reshape(CHAIN, frames, D)

    @pl.when(valid[k] > 0.0)
    def _():
        early[pl.ds(band, 1), :] = dmg
        early[pl.ds(EARLY_BIAS, 1), :] = early[pl.ds(EARLY_BIAS, 1), :] + rowsum(low.astype(F32))
        for i in range(4):
            row = EARLY_BIAS + BIAS_UP - BIAS_PROJ - 1 + 4 * band + i
            early[pl.ds(row, 1), :] = dub[:, i * D : (i + 1) * D]
        for i in range(2):
            row = EARLY_BIAS + BIAS_DOWN - BIAS_PROJ - 1 + 2 * band + i
            early[pl.ds(row, 1), :] = ddb[:, i * D : (i + 1) * D]


def band_backward_kernel(
    steps, chunk, table, keep, side, scale, ol_in, xs, w, p, h0, hk0, cf0, h1, hk1, cf1,
    keep_w, send_w, keep_p, send_p, bias_rows, rows_out,
    ol, wt, pt, da, sh, rg, ch_s, cc_s, dw, dp, db,
):
    n = steps // chunk
    j = pl.program_id(0)
    frames = ol_in.shape[2]

    @pl.when(j == 0)
    def _():
        for q in range(CHAIN):
            for k in range(SLOTS):
                if table[q][k] >= 0:
                    ol[pl.ds(table[q][k] * frames, frames), :] = ol_in[q, k]
        ol[pl.ds(BANDS * frames, (steps - BANDS) * frames), :] = jnp.zeros(
            ((steps - BANDS) * frames, D), BF
        )

    backward_chunk(
        keep, xs, ol, w, p, (h0, hk0, cf0, h1, hk1, cf1), dw, dp, db,
        wt, pt, da, sh, rg, ch_s, cc_s, steps, chunk, frames, 1,
    )

    @pl.when(j == n - 1)
    def _():
        part_totals(side[0], dw, dp, scale, keep_w, send_w, keep_p, send_p)
        bias_total(db, scale, bias_rows, 0)
        for q in range(CHAIN):
            for k in range(SLOTS):
                if table[q][k] >= 0:
                    rows_out[q, k] = rg[pl.ds(table[q][k] * frames, frames), :].astype(BF)
                else:
                    rows_out[q, k] = jnp.zeros((frames, D), BF)


def time_backward_kernel(
    steps, chunk, keep, bands, valid, side, scale, bgrad, abg, at, emb, sp, sm, gain, bias_b, keep_b, send_b, early, xs, w, p, h0, hk0, cf0, h1, hk1, cf1,
    keep_w, send_w, keep_m, send_m, spg,
    ol, wt, pt, da, sh, rg, ch_s, cc_s, dw, dp, db, xt, atg, late, dsm,
):
    n = steps // chunk
    j = pl.program_id(0)
    frames = bgrad.shape[2]

    @pl.when(j == 0)
    def _():
        xt[...] = jnp.zeros_like(xt)
        late[...] = jnp.zeros_like(late)
        dbg = jnp.zeros((1, D), F32)
        dpb = jnp.zeros((1, D), F32)
        for k in range(SLOTS):
            norm, r = ln(at[:, k].reshape(steps, D))
            dy = bgrad[:, k].reshape(steps, D).astype(F32)
            dbg = dbg + rowsum(dy * norm)
            a = abg[:, k].reshape(steps, D) + ln_back(norm, r, gain[pl.ds(GAIN_BAND, 1), :], dy)
            atg[k] = a
            low = a.astype(BF).astype(F32)
            dpb = dpb + rowsum(low)
            xt[pl.ds(k, steps, stride=ROWS_T), :] = low
        ol[...] = xt[...].astype(BF)
        late[pl.ds(GAIN_BAND, 1), :] = dbg
        late[pl.ds(LATE_BIAS + BIAS_PROJ, 1), :] = dpb
        late[pl.ds(LATE_BIAS + BIAS_LSTM + 2 * G4 // D, 2 * G4 // D), :] = bias_b[...]

    backward_chunk(
        keep, xs, ol, w, p, (h0, hk0, cf0, h1, hk1, cf1), dw, dp, db,
        wt, pt, da, sh, rg, ch_s, cc_s, steps, chunk, ROWS_T, 4,
    )

    @pl.when(j == n - 1)
    def _():
        part_totals(side[0], dw, dp, scale, keep_w, send_w, keep_m, send_m)
        bias_total(db, scale, late, LATE_BIAS + BIAS_LSTM)
        dtg = jnp.zeros((1, D), F32)
        for k in range(SLOTS):
            dy = rg[pl.ds(k, steps, stride=ROWS_T), :]
            norm, r = ln(emb[:, k].reshape(steps, D))
            dtg = dtg + rowsum(dy * norm)
            el = (atg[k] + ln_back(norm, r, gain[pl.ds(GAIN_TIME, 1), :], dy)).astype(BF)
            dsb = rowsum(el.astype(F32))
            own = gain[pl.ds(bands[k], 1), :]
            norm, r = ln(sp[:, k].reshape(steps, D).astype(F32))
            dsm[k] = mm_tn((norm * own).astype(BF), el).astype(BF)
            dy = mm_nt(el, sm[k])
            dsg = rowsum(dy * norm)

            @pl.when(valid[k] > 0.0)
            def _():
                late[pl.ds(bands[k], 1), :] = dsg
                late[pl.ds(LATE_BIAS + bands[k], 1), :] = dsb

            spg[:, k] = ln_back(norm, r, own, dy).astype(spg.dtype).reshape(CHAIN, frames, D)
        late[pl.ds(GAIN_TIME, 1), :] = dtg
        for out, band_part in ((keep_m, keep_b), (send_m, send_b)):
            out[pl.ds(PROJ_PART, PROJ_PART), :] = band_part[...]
            out[pl.ds(MISC_EARLY, EARLY_ROWS), :] = early[...].astype(BF)
            out[pl.ds(MISC_SPLIT, SLOTS * SUBF), :] = dsm[...].reshape(SLOTS * SUBF, D)
            out[pl.ds(MISC_LATE, LATE_ROWS), :] = late[...].astype(BF)


def whole(shape):
    zeros = (0,) * len(shape)
    return pl.BlockSpec(shape, lambda j: zeros)


SMEM = pl.BlockSpec(memory_space=pltpu.SMEM)
ANY = pl.BlockSpec(memory_space=pl.ANY)


def sds(shape, dtype):
    return jax.ShapeDtypeStruct(shape, dtype)


def chunk_specs(n, chunk, rows, flip):
    up = lambda j: (j, 0, 0)
    down = lambda j: (n - 1 - j, 0, 0)
    specs = []
    for way in (down, up) if flip else (up, down):
        specs += [
            pl.BlockSpec((chunk, rows, H), way),
            pl.BlockSpec((chunk, rows, H), way),
            pl.BlockSpec((chunk, rows, 6 * H), way),
        ]
    return specs


def chunk_shapes(steps, rows):
    return [
        sds((steps, rows, H), BF),
        sds((steps, rows, H), BF),
        sds((steps, rows, 6 * H), F32),
    ] * 2


def params():
    return pltpu.CompilerParams(vmem_limit_bytes=VMEM, dimension_semantics=("arbitrary",))


def cost(micros):
    return pl.CostEstimate(flops=micros * 10**9, bytes_accessed=micros * 10**6, transcendentals=0)


def time_forward(keep, bands, side, sp, sm, gain, bias, scale, near, far, p, later):
    frames = sp.shape[2]
    steps, chunk = CHAIN * frames, 32
    n = steps // chunk
    slab = (CHAIN, SLOTS, frames, D)
    return pl.pallas_call(
        functools.partial(time_forward_kernel, steps, chunk),
        grid=(n,),
        in_specs=[SMEM, SMEM, SMEM]
        + [whole(v.shape) for v in (sp, sm, gain, bias, scale, near, far, p)]
        + [ANY],
        out_specs=[whole(slab)] * 3
        + [whole((steps * ROWS_T, D)), whole((2, D + H, G4)), ANY]
        + chunk_specs(n, chunk, ROWS_T, False),
        out_shape=[sds(slab, F32), sds(slab, F32), sds(slab, BF), sds((steps * ROWS_T, D), BF), sds((2, D + H, G4), BF), sds(later.shape, later.dtype)]
        + chunk_shapes(steps, ROWS_T),
        input_output_aliases={11: 5},
        scratch_shapes=[
            pltpu.VMEM((2, chunk * ROWS_T, G4), F32),
            pltpu.VMEM((2, ROWS_T, H), BF),
            pltpu.VMEM((2, ROWS_T, H), F32),
            pltpu.VMEM((steps * ROWS_T, D), F32),
            pltpu.VMEM((2, steps * ROWS_T, H), BF),
        ],
        compiler_params=params(),
        cost_estimate=cost(66),
        name="time_forward",
    )(keep, bands, side, sp, sm, gain, bias, scale, near, far, p, later)


def band_forward(table, keep, side, rows_in, near, far, bias, scale, p):
    frames = rows_in.shape[2]
    steps, chunk = STEPS_B, 14
    n = steps // chunk
    slab = (CHAIN, SLOTS, frames, D)
    return pl.pallas_call(
        functools.partial(band_forward_kernel, steps, chunk, table),
        grid=(n,),
        in_specs=[SMEM, SMEM, whole(slab)]
        + [whole(v.shape) for v in (near, far, bias, scale, p)],
        out_specs=[whole(slab), whole((steps * frames, D)), whole((2, D + H, G4))] + chunk_specs(n, chunk, frames, False),
        out_shape=[sds(slab, BF), sds((steps * frames, D), BF), sds((2, D + H, G4), BF)] + chunk_shapes(steps, frames),
        scratch_shapes=[
            pltpu.VMEM((2, chunk * frames, G4), F32),
            pltpu.VMEM((2, frames, H), BF),
            pltpu.VMEM((2, frames, H), F32),
            pltpu.VMEM((2, steps * frames, H), BF),
        ],
        compiler_params=params(),
        cost_estimate=cost(27),
        name="band_forward",
    )(keep, side, rows_in, near, far, bias, scale, p)


def mask_stage(bands, valid, side, at, bo, cot, um, dm, gain, bias):
    frames = at.shape[2]
    slab = (CHAIN, SLOTS, frames, D)
    part = pl.BlockSpec((CHAIN, 1, frames, D), lambda k: (0, k, 0, 0))

    def band(*shape):
        return pl.BlockSpec((1,) + shape, lambda k: (k, 0, 0))

    return pl.pallas_call(
        mask_kernel,
        grid=(SLOTS,),
        in_specs=[
            SMEM, SMEM, SMEM, part, part, part, band(D, 4 * D), band(4 * D, 2 * SUBF),
            whole(gain.shape), whole(bias.shape),
        ],
        out_specs=[
            part, part, part, band(MASK_PART, D), band(MASK_PART, D),
            whole((EARLY_ROWS, D)),
        ],
        out_shape=[
            sds(slab, BF), sds(slab, F32), sds(slab, BF),
            sds((SLOTS, MASK_PART, D), BF), sds((SLOTS, MASK_PART, D), BF),
            sds((EARLY_ROWS, D), F32),
        ],
        compiler_params=params(),
        cost_estimate=cost(16),
        name="mask_stage",
    )(bands, valid, side, at, bo, cot, um, dm, gain, bias)


def backward_scratch(steps, chunk, rows):
    span = chunk * rows
    return [
        pltpu.VMEM((steps * rows, D), BF),
        pltpu.VMEM((2, G4, D + H), BF),
        pltpu.VMEM((2, D, H), BF),
        pltpu.VMEM((2, span, G4), BF),
        pltpu.VMEM((2, span, H), BF),
        pltpu.VMEM((steps * rows, D), F32),
        pltpu.VMEM((2, rows, H), F32),
        pltpu.VMEM((2, rows, H), F32),
        pltpu.VMEM((2, D + H, G4), F32),
        pltpu.VMEM((2 * H, D), F32),
        pltpu.VMEM((2, 8, G4), F32),
    ]


def total_shapes(small):
    return [sds((CHAIN, 2, HALF, G4), BF)] * 2 + [sds((small, D), BF)] * 2


def band_backward(table, keep, side, scale, ol_in, xs, w, p, saved):
    frames = ol_in.shape[2]
    steps, chunk = STEPS_B, 14
    n = steps // chunk
    slab = (CHAIN, SLOTS, frames, D)
    return pl.pallas_call(
        functools.partial(band_backward_kernel, steps, chunk, table),
        grid=(n,),
        in_specs=[SMEM, SMEM]
        + [whole(v.shape) for v in (scale, ol_in, xs, w, p)]
        + chunk_specs(n, chunk, frames, True),
        out_specs=[whole(v.shape) for v in total_shapes(PROJ_PART)] + [whole((2 * G4 // D, D)), whole(slab)],
        out_shape=total_shapes(PROJ_PART) + [sds((2 * G4 // D, D), F32), sds(slab, BF)],
        scratch_shapes=backward_scratch(steps, chunk, frames),
        compiler_params=params(),
        cost_estimate=cost(32),
        name="band_backward",
    )(keep, side, scale, ol_in, xs, w, p, *saved)


def time_backward(keep, bands, valid, side, scale, bgrad, abg, at, emb, sp, sm, gain, bias_b, keep_b, send_b, early, xs, w, p, saved):
    frames = bgrad.shape[2]
    steps, chunk = CHAIN * frames, 32
    n = steps // chunk
    slab = (CHAIN, SLOTS, frames, D)
    outs = total_shapes(MISC) + [sds(slab, BF)]
    return pl.pallas_call(
        functools.partial(time_backward_kernel, steps, chunk),
        grid=(n,),
        in_specs=[SMEM, SMEM, SMEM, SMEM]
        + [whole(v.shape) for v in (scale, bgrad, abg, at, emb, sp, sm, gain, bias_b, keep_b, send_b, early, xs, w, p)]
        + chunk_specs(n, chunk, ROWS_T, True),
        out_specs=[whole(v.shape) for v in outs],
        out_shape=outs,
        scratch_shapes=backward_scratch(steps, chunk, ROWS_T)
        + [pltpu.VMEM((steps * ROWS_T, D), F32), pltpu.VMEM((SLOTS, steps, D), F32)]
        + [pltpu.VMEM((LATE_ROWS, D), F32), pltpu.VMEM((SLOTS, SUBF, D), BF)],
        compiler_params=params(),
        cost_estimate=cost(96),
        name="time_backward",
    )(keep, bands, valid, side, scale, bgrad, abg, at, emb, sp, sm, gain, bias_b, keep_b, send_b, early, xs, w, p, *saved)


def chain_groups():
    many = lax.axis_size("rows") // CHAIN
    return [[CHAIN * g + q for q in range(CHAIN)] for g in range(many)]


def place_groups():
    many = lax.axis_size("rows") // CHAIN
    return [[CHAIN * g + q for g in range(many)] for q in range(CHAIN)]


def across(v, groups, axis=0):
    return lax.all_to_all(v, "rows", axis, axis, axis_index_groups=groups, tiled=True)


def spread(v, groups):
    return across(jnp.broadcast_to(v[None], (len(groups[0]),) + v.shape), groups)


def swap_dir(v):
    return lax.ppermute(v, "dir", [(0, 1), (1, 0)])


def ordered(side, near, far):
    return jnp.where(side == 0, jnp.stack([near, far]), jnp.stack([far, near]))


def to_bands(v, more=None):
    v = jnp.concatenate([v, v[:1]])
    parts = []
    for blocks in band_blocks(lax.axis_size("rows")):
        cuts = [v[first : first + places] for first, places, _ in blocks]
        parts.append(jnp.concatenate(cuts + ([] if more is None else [more])))
    return jnp.stack(parts)


def from_bands(v):
    found = {}
    for q, blocks in enumerate(band_blocks(lax.axis_size("rows"))):
        at = 0
        for first, places, filled in blocks:
            found[first] = v[q, at : at + filled]
            at += places
    return jnp.concatenate([found[first] for first in sorted(found)])


def my_bit(bit):
    return (lax.axis_index("rows") >> bit) & 1


def swap_bit(v, bit):
    return lax.ppermute(v, "rows", [(r, r ^ (1 << bit)) for r in range(lax.axis_size("rows"))])


def double(v, bit):
    return ordered(my_bit(bit), v, swap_bit(v, bit))


def halve(v, bit, axis):
    mine = my_bit(bit)
    kept = lax.dynamic_index_in_dim(v, mine, axis, False)
    return kept + swap_bit(lax.dynamic_index_in_dim(v, 1 - mine, axis, False), bit)


def my_rows(values):
    return jnp.asarray(np.array(values, np.int32))[lax.axis_index("rows")]


def fills(rows):
    return [shard_start(s, rows) * D - s * BANDS * D // rows for s in range(rows)]


def tied(v, *others):
    for other in others:
        one = lax.slice(other, (0,) * other.ndim, (1,) * other.ndim).reshape(())
        v = jnp.where(jnp.isnan(one), jnp.zeros_like(v), v)
    return v


def whole_bands(shard):
    rows = lax.axis_size("rows")
    unit = shard.shape[0] * rows // (BANDS * D)
    head = FILL * unit
    after = lax.ppermute(shard[:head], "rows", [(r + 1, r) for r in range(rows - 1)])
    spare = jnp.zeros((head,) + shard.shape[1:], shard.dtype)
    long = jnp.concatenate([shard, after, spare])
    return lax.dynamic_slice_in_dim(long, my_rows(fills(rows)) * unit, SLOTS // CHAIN * D * unit, 0)


def to_shard(own, unit):
    rows = lax.axis_size("rows")
    fill = my_rows(fills(rows)) * unit
    many = BANDS * D * unit // rows
    head = jnp.zeros((FILL * unit,) + own.shape[1:], own.dtype)
    over = lax.dynamic_slice_in_dim(jnp.concatenate([own, head]), many - fill, FILL * unit, 0)
    before = lax.ppermute(over, "rows", [(r, r + 1) for r in range(rows - 1)])
    moved = lax.dynamic_slice_in_dim(jnp.concatenate([head, own]), FILL * unit - fill, many, 0)
    before = jnp.concatenate([before, jnp.zeros((many - FILL * unit,) + own.shape[1:], own.dtype)])
    row = lax.broadcasted_iota(jnp.int32, (many, 1), 0)
    return jnp.where(row < fill, before, moved)


def square_slice():
    return lax.axis_size("rows") == CHAIN * CHAIN


def pick_bands(wide):
    blocks = band_blocks(lax.axis_size("rows"))
    place = lax.axis_index("rows") % CHAIN
    wide = jnp.concatenate([wide, wide[:1]])
    cuts = []
    for at in range(len(blocks[0])):
        first = jnp.asarray(np.array([b[at][0] for b in blocks], np.int32))[place]
        cuts.append(lax.dynamic_slice_in_dim(wide, first, blocks[0][at][1], 0))
    return jnp.concatenate(cuts)


def place_bands(part, valid):
    blocks = band_blocks(lax.axis_size("rows"))
    place = lax.axis_index("rows") % CHAIN
    part = part * valid[:, None]
    total = jnp.zeros((BANDS + 1, part.shape[1]), F32)
    row = 0
    for at in range(len(blocks[0])):
        first = jnp.asarray(np.array([b[at][0] for b in blocks], np.int32))[place]
        cut = part[row : row + blocks[0][at][1]]
        total = lax.dynamic_update_slice_in_dim(total, cut, first, 0)
        row += blocks[0][at][1]
    return total[:BANDS]


def band_weights(shard, gate=None):
    rows = lax.axis_size("rows")
    unit = shard.shape[0] * rows // BANDS
    low = shard.astype(BF)
    if not square_slice():
        full = lax.all_gather(low, "rows", axis=0, tiled=True).reshape(BANDS, unit, -1)
        return pick_bands(full)
    own = whole_bands(low)
    if gate is not None:
        own = tied(own, gate)
    own = lax.all_gather(own, "rows", axis=0, axis_index_groups=place_groups(), tiled=True)
    return own.reshape(SLOTS, unit, -1)


def band_sums(grads, apart):
    if not square_slice():
        return grads
    if not apart:
        return halve(halve(grads.reshape(2, 2, SLOTS // CHAIN, *grads.shape[1:]), 3, 0), 2, 0)
    return lax.psum_scatter(
        grads, "rows", scatter_dimension=0, axis_index_groups=place_groups(), tiled=True
    )


def shard_sums(own, unit, valid):
    if square_slice():
        return to_shard(own.reshape(SLOTS // CHAIN * unit, -1), unit // D)
    flat = place_bands(own.reshape(SLOTS, -1).astype(F32), valid).astype(BF)
    flat = flat.reshape(BANDS * unit, -1)
    return lax.psum_scatter(flat, "rows", scatter_dimension=0, tiled=True)


def both_cores(kept, sent):
    return kept + swap_dir(sent)


def mask_totals(side, own, valid):
    pair = ordered(side, own, swap_dir(own))
    many = own.shape[0]
    up = pair[:, :, :UP_PART].reshape(2, many, UP_PART // D, D, D)
    up = jnp.transpose(up, (1, 3, 0, 2, 4)).reshape(many, D, 4 * D)
    down = jnp.transpose(pair[:, :, UP_PART:], (1, 2, 0, 3)).reshape(many, 4 * D, 2 * SUBF)
    return shard_sums(up, D, valid).astype(F32), shard_sums(down, 4 * D, valid).astype(F32)


def sum_rows(v, bits, wire=F32):
    for bit in bits:
        v = v + swap_bit(v.astype(wire), bit).astype(F32)
    return v


def gather_first(side, lstm_low, proj_low, split_weight, sp):
    if not square_slice():
        lstm = lax.all_gather(lstm_low, "rows", axis=0, tiled=True)
        proj = lax.all_gather(proj_low, "rows", axis=0, tiled=True).reshape(2, 2 * H, D)
        cut = jnp.transpose(lstm.reshape(2, 2, CHAIN, 2, HALF, G4), (0, 3, 2, 1, 4, 5))
        near = lax.dynamic_index_in_dim(cut, side, 1, False)
        far = lax.dynamic_index_in_dim(cut, 1 - side, 1, False)
        return (near[0], far[0], proj[0]), lambda dep: (near[1], far[1], proj[1]), band_weights(split_weight)
    packed = jnp.concatenate(
        [
            lax.dynamic_slice_in_dim(lstm_low, side * HALF, HALF, 0),
            lax.dynamic_slice_in_dim(proj_low, side * HALF_P, HALF_P, 0).reshape(-1, G4),
        ]
    )
    split = whole_bands(split_weight.astype(BF))
    column = double(packed, 3)
    column = double(tied(column, split), 2)
    split = double(split, 3)
    time = tied(column[:, 0], split, sp)
    split = double(split, 2)
    time = double(time, 0)
    time = double(tied(time, split), 1)
    split = jnp.swapaxes(split, 0, 1).reshape(SLOTS, SUBF, D)

    def finish(near):
        near = near.reshape(CHAIN, 2, *packed.shape)
        far = swap_dir(near)
        proj = ordered(side, near[:, :, HALF:], far[:, :, HALF:])
        return near, far, jnp.transpose(proj, (2, 1, 0, 3, 4)).reshape(2 * H, D)

    done = finish(time)
    band = spread(tied(column[:, 1], time), chain_groups())
    return done, lambda dep: finish(tied(band, dep)), split


def lstm_totals(side, time, band, proj):
    flat = HALF_P * D // G4
    if not square_slice():
        v = jnp.stack([time, band])
        pair = ordered(side, v, swap_dir(v))
        lstm = jnp.transpose(pair, (1, 3, 2, 0, 4, 5)).reshape(-1, G4)
        pair = ordered(side, proj, swap_dir(proj)).reshape(2, 2, CHAIN, 2, HALF_P, D)
        proj = jnp.transpose(pair, (1, 3, 2, 0, 4, 5)).reshape(-1, D)
        return tuple(
            lax.psum_scatter(t, "rows", scatter_dimension=0, tiled=True).astype(F32)
            for t in (lstm, proj)
        )
    parts = [proj[i * PROJ_PART : (i + 1) * PROJ_PART].reshape(CHAIN, 2, flat, G4) for i in range(2)]
    v = jnp.concatenate([time] + parts, axis=2).reshape(2, 2, 2, HALF + 2 * flat, G4)
    v = halve(halve(v, 0, 1), 1, 0)
    time = v[:, : HALF + flat]
    band = jnp.concatenate([band, v[:, HALF + flat :]], axis=1)
    v = halve(halve(jnp.stack([time, band]), 3, 0), 2, 0)
    pair = ordered(side, v, swap_dir(v)).astype(F32)
    return pair[:, :HALF].reshape(2 * HALF, G4), pair[:, HALF:].reshape(2 * HALF_P, D)


def update(gradient, velocity, weight_now, average, clip_scale, rate):
    clipped = gradient * clip_scale
    velocity_new = MOMENTUM * velocity + clipped
    weight_new = weight_now - rate * (clipped + MOMENTUM * velocity_new)
    average_new = AVERAGE * average + (1.0 - AVERAGE) * weight_new
    return (clipped, velocity_new, weight_new, average_new)


def halved_columns():
    scale = np.full((1, G4), 0.5, np.float32)
    scale[:, 2 * H : 3 * H] = 1.0
    return jnp.asarray(scale)


def on_device(
    spectra,
    mask_grad,
    clip_starts,
    split_weight,
    split_velocity,
    split_average,
    lstm_weight,
    lstm_velocity,
    lstm_average,
    proj_weight,
    proj_velocity,
    proj_average,
    up_weight,
    up_velocity,
    up_average,
    down_weight,
    down_velocity,
    down_average,
    gain_weight,
    gain_velocity,
    gain_average,
    bias_weight,
    bias_velocity,
    bias_average,
):
    side = lax.axis_index("dir")
    row = lax.axis_index("rows")
    place = row % CHAIN
    rows = lax.axis_size("rows")
    bits = range((rows - 1).bit_length())
    frames = spectra.shape[1]
    steps = CHAIN * frames
    scale = halved_columns()
    which = side.astype(jnp.int32)[None]
    table = band_table(rows)
    valid = jnp.asarray((np.array(table) >= 0).astype(np.float32))[place]
    bands = jnp.asarray(np.maximum(np.array(table), 0).astype(np.int32))[place]

    flags = lax.dynamic_index_in_dim(clip_starts[0], side, 1, False).astype(BF)
    flag_slab = jnp.broadcast_to(flags[:, None], (frames, SUBF))
    sp = across(
        to_bands(jnp.transpose(spectra[0, :, 0], (1, 0, 2)), flag_slab[None]), chain_groups()
    )
    starts = sp[:, SLOTS, :, 0].reshape(steps).astype(F32)
    keep_time = jnp.concatenate([1.0 - starts, 1.0 - starts[1:], jnp.ones((1,), F32)])
    keep_np = np.ones((2 * STEPS_B,), np.float32)
    keep_np[STEPS_B + BANDS - 1] = 0.0
    keep_band = jnp.asarray(keep_np)
    cot_parts = to_bands(jnp.transpose(mask_grad[0, :, 0], (1, 0, 2)))

    time_w, band_finish, split_mat = gather_first(
        side, (lstm_weight * scale).astype(BF), proj_weight.astype(BF), split_weight, sp
    )
    up_mat = band_weights(up_weight, time_w[0])
    down_mat = band_weights(down_weight, time_w[0])

    emb, after_time, band_rows, xs_t, w_time, cot_parts, *saved_t = time_forward(
        keep_time, bands, which, sp, split_mat, gain_weight, bias_weight, scale, *time_w, cot_parts
    )
    band_w = band_finish(band_rows)
    band_out, xs_b, w_band, *saved_b = band_forward(
        table, keep_band, which, across(band_rows, chain_groups()), band_w[0], band_w[1], bias_weight, scale, band_w[2]
    )
    mask, abg, abl, kept, sent, early = mask_stage(
        bands, valid, which, after_time, across(band_out, chain_groups()), across(cot_parts, chain_groups()),
        up_mat, down_mat, gain_weight, bias_weight,
    )

    ol_in = across(abl, chain_groups())
    mask_in = across(mask, chain_groups())
    mask_own = both_cores(kept, sent)
    ol_in = tied(ol_in, mask_own)
    mask_own = band_sums(mask_own, True)
    keep_w, send_w, keep_b, send_b, bias_b, bgrad = band_backward(
        table, keep_band, which, scale, ol_in, xs_b, w_band, band_w[2], saved_b
    )
    bgrad = across(bgrad, chain_groups())
    lstm_b = both_cores(tied(keep_w, bgrad), send_w)
    if square_slice():
        lstm_b = lax.psum_scatter(
            lstm_b.reshape(-1, G4), "rows", scatter_dimension=0, axis_index_groups=chain_groups(), tiled=True
        ).reshape(2, HALF, G4)
    bgrad = tied(bgrad, mask_own, mask_in)
    band_mask = jnp.transpose(from_bands(mask_in), (1, 0, 2))[None, :, None]
    keep_w, send_w, keep_m, send_m, spg = time_backward(
        keep_time, bands, valid, which, scale, bgrad, abg, after_time, emb, sp, split_mat,
        gain_weight, bias_b, keep_b, send_b, early, xs_t, w_time, time_w[2], saved_t,
    )
    spectra_grad = jnp.transpose(from_bands(across(spg, chain_groups())), (1, 0, 2))
    spectra_grad = spectra_grad[None, :, None].astype(F32)

    lstm_t = both_cores(keep_w, send_w)
    misc = both_cores(keep_m, send_m)
    lstm_total, proj_total = lstm_totals(side, lstm_t, lstm_b, misc[:MISC_SPLIT])
    split_own = band_sums(misc[MISC_SPLIT:MISC_LATE].reshape(SLOTS, SUBF, D), False)
    split_total = shard_sums(split_own, SUBF, valid).astype(F32)
    up_total, down_total = mask_totals(side, mask_own, valid)
    small = sum_rows(misc[MISC_LATE:].astype(F32), bits, BF)
    late, early = small[:LATE], small[LATE_ROWS : LATE_ROWS + EARLY]
    gain_total = jnp.concatenate([late[:LATE_BIAS], early[:EARLY_BIAS]])
    bias_total = jnp.concatenate([late[LATE_BIAS:], early[EARLY_BIAS:]])

    shards = (split_total, lstm_total, proj_total, up_total, down_total)
    square = sum(jnp.sum(v * v) for v in shards)
    square = sum_rows(jnp.full((8, 128), square, F32), bits)[0, 0]
    square = square + jnp.sum(gain_total * gain_total) + jnp.sum(bias_total * bias_total)
    grad_norm = jnp.sqrt(square)
    clip_scale = jnp.minimum(1.0, CLIP_NORM / (grad_norm + 1e-06))
    outputs = (band_mask, spectra_grad, grad_norm)
    olds = (
        (split_velocity, split_weight, split_average),
        (lstm_velocity, lstm_weight, lstm_average),
        (proj_velocity, proj_weight, proj_average),
        (up_velocity, up_weight, up_average),
        (down_velocity, down_weight, down_average),
    )
    for total, old in zip(shards, olds):
        outputs += update(total, *old, clip_scale, LEARN_RATE)
    outputs += update(gain_total, gain_velocity, gain_weight, gain_average, clip_scale, GAIN_RATE)
    outputs += update(bias_total, bias_velocity, bias_weight, bias_average, clip_scale, GAIN_RATE)
    return outputs


def solution(mesh):
    per_row = P("rows", None)
    row_major = P("rows", None, "dir", None, None)
    return jax.shard_map(
        on_device,
        mesh=mesh,
        in_specs=(row_major, row_major, P("rows", None, None)) + (per_row,) * 15 + (P(),) * 6,
        out_specs=(row_major, row_major, P()) + (per_row,) * 20 + (P(),) * 8,
        check_vma=False,
    )
```

```python
import functools

import jax
import jax.numpy as jnp
import numpy as np
from jax import lax
from jax.experimental import pallas as pl
from jax.experimental.pallas import tpu as pltpu
from jax.sharding import PartitionSpec as P

D = 128
H = 256
G4 = 4 * H
BANDS = 41
SUBF = 128
CHAIN = 4
SLOTS = 12
FILL = 128
ROWS_T = 16
STEPS_B = 42
VMEM = 60 << 20
HALF = (D + H) // CHAIN // 2
HALF_P = H // CHAIN // 2

EPSILON = 1e-05
MOMENTUM = 0.9
LEARN_RATE = 5.0
GAIN_RATE = 50.0
AVERAGE = 0.5
CLIP_NORM = 5.0


GAIN_TIME, GAIN_BAND, GAIN_MASK = BANDS, BANDS + 1, BANDS + 2
BIAS_LSTM = BANDS
BIAS_PROJ = BIAS_LSTM + 16 * H // D
BIAS_UP = BIAS_PROJ + 2
BIAS_DOWN = BIAS_UP + 4 * BANDS
EARLY_BIAS = BANDS
EARLY = EARLY_BIAS + BIAS_DOWN + 2 * BANDS - BIAS_PROJ - 1
EARLY_ROWS = -(-EARLY // 16) * 16
LATE_BIAS = GAIN_MASK
LATE = LATE_BIAS + BIAS_PROJ + 1
LATE_ROWS = -(-LATE // 16) * 16

BF = jnp.bfloat16
F32 = jnp.float32


def mm(a, b):
    return jnp.dot(a, b, preferred_element_type=F32)


def mm_nt(a, b):
    return lax.dot_general(a, b, (((1,), (1,)), ((), ())), preferred_element_type=F32)


def mm_tn(a, b):
    return lax.dot_general(a, b, (((0,), (0,)), ((), ())), preferred_element_type=F32)


def ln(v):
    c = v - jnp.mean(v, axis=-1, keepdims=True)
    r = lax.rsqrt(jnp.mean(c * c, axis=-1, keepdims=True) + EPSILON)
    return c * r, r


def ln_back(n, r, gain, dy):
    dg = dy * gain
    return r * (
        dg - jnp.mean(dg, axis=-1, keepdims=True) - n * jnp.mean(dg * n, axis=-1, keepdims=True)
    )


def rowsum(v):
    return jnp.sum(v, axis=0, keepdims=True)


UP_PART = 2 * D
MASK_PART = UP_PART + 4 * D
LSTM_PART = HALF * G4 // D
PROJ_PART = 2 * CHAIN * HALF_P
SHARD_PART = LSTM_PART + 2 * HALF_P
MISC_SPLIT = 2 * CHAIN * SHARD_PART
MISC_LATE = MISC_SPLIT + SLOTS * SUBF
MISC_EARLY = MISC_LATE + LATE_ROWS
MISC = MISC_EARLY + EARLY_ROWS


def shard_start(shard, rows):
    return -(-shard * BANDS // rows)


def band_blocks(rows):
    if rows == CHAIN * CHAIN:
        three = SLOTS // CHAIN
        return [
            [
                (shard_start(CHAIN * z + q, rows), three, shard_start(CHAIN * z + q + 1, rows) - shard_start(CHAIN * z + q, rows))
                for z in range(CHAIN)
            ]
            for q in range(CHAIN)
        ]
    each = BANDS // CHAIN
    return [[(each * q, SLOTS, each if q + 1 < CHAIN else BANDS - each * q)] for q in range(CHAIN)]


def band_table(rows):
    return [
        [first + i if i < filled else -1 for first, places, filled in blocks for i in range(places)]
        for blocks in band_blocks(rows)
    ]


def wide_row(rows, first, many):
    return jnp.concatenate([rows[pl.ds(first + i, 1), :] for i in range(many)], axis=1)


def forward_chunk(keep, x_ref, w_ref, bias, scale, first_row, outs, gates, hk_s, ck_s, steps, chunk, rows, unroll, hall):
    n = steps // chunk
    j = pl.program_id(0)
    first = (j * chunk, (n - 1 - j) * chunk)

    @pl.when(j == 0)
    def _():
        hk_s[...] = jnp.zeros_like(hk_s)
        ck_s[...] = jnp.zeros_like(ck_s)

    for d in range(2):
        x = x_ref[pl.ds(pl.multiple_of(first[d] * rows, chunk * rows), chunk * rows), :]
        b = wide_row(bias, first_row + d * (G4 // D), G4 // D) * scale[...]
        gates[d] = mm(x, w_ref[d, :D]) + b

    def step(t, carry):
        new = []
        for d in range(2):
            hk, ck = carry[2 * d], carry[2 * d + 1]
            tt = t if d == 0 else chunk - 1 - t
            at = first[d] + tt
            now = keep[d * steps + at]
            later = jnp.minimum(at + 1, steps - 1) if d == 0 else jnp.maximum(at - 1, 0)
            nxt = keep[d * steps + later]
            h_ref, hk_ref, cf_ref = outs[3 * d : 3 * d + 3]
            a = gates[d, pl.ds(pl.multiple_of(tt * rows, rows), rows), :] + mm(hk, w_ref[d, D:])
            ti = jnp.tanh(a[:, :H])
            tf = jnp.tanh(a[:, H : 2 * H])
            g = jnp.tanh(a[:, 2 * H : 3 * H])
            to = jnp.tanh(a[:, 3 * H :])
            i = 0.5 * ti + 0.5
            f = 0.5 * tf + 0.5
            o = 0.5 * to + 0.5
            c = f * ck + i * g
            tc = jnp.tanh(c)
            h = o * tc
            h_low = h.astype(BF)
            hk_ref[tt] = hk
            h_ref[tt] = h_low
            if hall is not None:
                hall[d, pl.ds(pl.multiple_of(at * rows, rows), rows), :] = h_low
            cf_ref[tt, :, :H] = o * (1.0 - tc * tc)
            cf_ref[tt, :, H : 2 * H] = g * (0.5 - 0.5 * ti * ti)
            cf_ref[tt, :, 2 * H : 3 * H] = ck * (0.5 - 0.5 * tf * tf)
            cf_ref[tt, :, 3 * H : 4 * H] = i * (1.0 - g * g)
            cf_ref[tt, :, 4 * H : 5 * H] = tc * (0.5 - 0.5 * to * to)
            cf_ref[tt, :, 5 * H :] = f * now
            new += [(h * nxt).astype(BF), c * nxt]
        return tuple(new)

    done = lax.fori_loop(
        0, chunk, step, (hk_s[0], ck_s[0], hk_s[1], ck_s[1]), unroll=unroll
    )
    for d in range(2):
        hk_s[d] = done[2 * d]
        ck_s[d] = done[2 * d + 1]


def backward_chunk(
    keep, x_ref, ol, w_ref, p_ref, ins, dw, dp, db, wt, pt, da, sh, rg, ch_s, cc_s, steps, chunk, rows, unroll
):
    n = steps // chunk
    j = pl.program_id(0)
    first = ((n - 1 - j) * chunk, j * chunk)
    span = chunk * rows

    @pl.when(j == 0)
    def _():
        ch_s[...] = jnp.zeros_like(ch_s)
        cc_s[...] = jnp.zeros_like(cc_s)
        rg[...] = jnp.zeros_like(rg)
        dw[...] = jnp.zeros_like(dw)
        dp[...] = jnp.zeros_like(dp)
        db[...] = jnp.zeros_like(db)
        for d in range(2):
            wt[d] = w_ref[d].T
            pt[d] = p_ref[pl.ds(d * H, H), :].T

    at_rows = [pl.ds(pl.multiple_of(first[d] * rows, span), span) for d in range(2)]
    for d in range(2):
        sh[d] = mm(ol[at_rows[d], :], pt[d]).astype(BF)

    def step(t, carry):
        new = []
        for d in range(2):
            ch, cc = carry[2 * d], carry[2 * d + 1]
            tt = chunk - 1 - t if d == 0 else t
            now = keep[d * steps + first[d] + tt]
            cf = ins[3 * d + 2]
            here = pl.ds(pl.multiple_of(tt * rows, rows), rows)
            dh = sh[d, here, :].astype(F32) + ch
            dc = cc + dh * cf[tt, :, :H]
            da_now = jnp.concatenate(
                [
                    (dc * cf[tt, :, H : 2 * H]).astype(BF),
                    (dc * cf[tt, :, 2 * H : 3 * H]).astype(BF),
                    (dc * cf[tt, :, 3 * H : 4 * H]).astype(BF),
                    (dh * cf[tt, :, 4 * H : 5 * H]).astype(BF),
                ],
                axis=-1,
            )
            da[d, here, :] = da_now
            new += [mm(da_now, wt[d, :, D:]) * now, dc * cf[tt, :, 5 * H :]]
        return tuple(new)

    done = lax.fori_loop(0, chunk, step, (ch_s[0], cc_s[0], ch_s[1], cc_s[1]), unroll=unroll)
    ones = jnp.ones((8, span), BF)
    for d in range(2):
        ch_s[d] = done[2 * d]
        cc_s[d] = done[2 * d + 1]
        here = at_rows[d]
        grad = da[d]
        rg[here, :] = rg[here, :] + mm(grad, wt[d, :, :D])
        dw[d, :D, :] = dw[d, :D, :] + mm_tn(x_ref[here, :], grad)
        dw[d, D:, :] = dw[d, D:, :] + mm_tn(ins[3 * d + 1][...].reshape(span, H), grad)
        db[d] = db[d] + mm(ones, grad)
        at_p = pl.ds(d * H, H)
        dp[at_p, :] = dp[at_p, :] + mm_tn(ins[3 * d][...].reshape(span, H), ol[here, :])


def lay_weights(side, near, far, w):
    for way in range(2):
        for q in range(CHAIN):
            for part, of in ((near, side), (far, 1 - side)):
                at = pl.multiple_of(q * 2 * HALF + of * HALF, HALF)
                w[way, pl.ds(at, HALF), :] = part[q, way, :HALF, :]


def part_totals(side, dw, dp, scale, places, proj_places):
    for way in range(2):
        for q in range(CHAIN):
            for other in range(2):
                of = 1 - side if other else side
                at = pl.multiple_of(q * 2 * HALF + of * HALF, HALF)
                part = (dw[way, pl.ds(at, HALF), :] * scale[...]).astype(BF)
                out, row = places(other, q, way)
                for c in range(G4 // D):
                    out[row + c * HALF : row + (c + 1) * HALF, :] = part[:, c * D : (c + 1) * D]
                at = pl.multiple_of(way * H + q * 2 * HALF_P + of * HALF_P, HALF_P)
                out, row = proj_places(other, q, way)
                out[row : row + HALF_P, :] = dp[pl.ds(at, HALF_P), :].astype(BF)


def bias_total(db, scale, out, first):
    for way in range(2):
        row = db[way, :1, :] * scale[...]
        for i in range(G4 // D):
            out[pl.ds(first + way * (G4 // D) + i, 1), :] = row[:, i * D : (i + 1) * D]


def band_at(meta, bands, k):
    band = bands[meta[1] * SLOTS + k]
    return jnp.maximum(band, 0), band >= 0


def time_forward_kernel(
    steps, chunk, keep, bands, meta, sp, sm, gain, bias, scale, near, far, p, _,
    emb, at, br, xs, w, _out, h0, hk0, cf0, h1, hk1, cf1,
    gates, hk_s, ck_s, xt, hall,
):
    n = steps // chunk
    j = pl.program_id(0)
    frames = sp.shape[2]

    @pl.when(j == 0)
    def _():
        lay_weights(meta[0], near, far, w)
        xt[...] = jnp.zeros_like(xt)
        for k in range(SLOTS):
            v = sp[:, k].reshape(steps, D).astype(F32)
            band = band_at(meta, bands, k)[0]
            normed = (ln(v)[0] * gain[pl.ds(band, 1), :]).astype(BF)
            e = mm(normed, sm[k]) + bias[pl.ds(band, 1), :]
            emb[:, k] = e.reshape(CHAIN, frames, D)
            xt[pl.ds(k, steps, stride=ROWS_T), :] = ln(e)[0] * gain[pl.ds(GAIN_TIME, 1), :]
        xs[...] = xt[...].astype(BF)

    forward_chunk(
        keep, xs, w, bias, scale, BIAS_LSTM, (h0, hk0, cf0, h1, hk1, cf1), gates, hk_s, ck_s, steps, chunk, ROWS_T, 8, hall
    )

    @pl.when(j == n - 1)
    def _():
        span = 512
        for s in range(0, steps * ROWS_T, span):
            here = pl.ds(s, span)
            xt[here, :] = mm(hall[0, here, :], p[:H]) + mm(hall[1, here, :], p[H:])
        for k in range(SLOTS):
            to = xt[pl.ds(k, steps, stride=ROWS_T), :] + bias[pl.ds(BIAS_PROJ, 1), :]
            a = emb[:, k].reshape(steps, D) + to
            at[:, k] = a.reshape(CHAIN, frames, D)
            br[:, k] = (ln(a)[0] * gain[pl.ds(GAIN_BAND, 1), :]).astype(BF).reshape(CHAIN, frames, D)


def band_forward_kernel(
    steps, chunk, table, keep, rows_in, cores, bias, scale, p,
    bo, xs, w, h0, hk0, cf0, h1, hk1, cf1,
    gates, hk_s, ck_s, hall,
):
    n = steps // chunk
    j = pl.program_id(0)
    frames = rows_in.shape[2]

    @pl.when(j == 0)
    def _():
        for way in range(2):
            for q in range(CHAIN):
                for core in range(2):
                    at = (2 * q + core) * HALF
                    w[way, at : at + HALF, :] = cores[q, core, way]
        for q in range(CHAIN):
            for k in range(SLOTS):
                if table[q][k] >= 0:
                    xs[pl.ds(table[q][k] * frames, frames), :] = rows_in[q, k]
        xs[pl.ds(BANDS * frames, (steps - BANDS) * frames), :] = jnp.zeros(
            ((steps - BANDS) * frames, D), BF
        )

    forward_chunk(
        keep, xs, w, bias, scale, BIAS_LSTM + 2 * G4 // D, (h0, hk0, cf0, h1, hk1, cf1), gates, hk_s, ck_s, steps, chunk, frames, 1, hall
    )

    @pl.when(j == n - 1)
    def _():
        for q in range(CHAIN):
            for k in range(SLOTS):
                here = pl.ds(max(table[q][k], 0) * frames, frames)
                bo[q, k] = (mm(hall[0, here, :], p[:H]) + mm(hall[1, here, :], p[H:])).astype(BF)


def mask_kernel(
    bands, meta, at, bo, cot, um, dm, gain, bias,
    mask, abg, abl, kept, sent, early,
):
    frames = at.shape[2]
    rows = CHAIN * frames

    k = pl.program_id(0)
    band, filled = band_at(meta, bands, k)

    @pl.when(k == 0)
    def _():
        early[...] = jnp.zeros_like(early)

    def halves(v, first):
        half = v.shape[1] // 2
        lower = meta[0] == 0
        near = jnp.where(lower, v[:, :half], v[:, half:]).astype(BF)
        far = jnp.where(lower, v[:, half:], v[:, :half]).astype(BF)
        many = v.shape[0]
        for i in range(half // D):
            kept[0, first + i * many : first + (i + 1) * many, :] = near[:, i * D : (i + 1) * D]
            sent[0, first + i * many : first + (i + 1) * many, :] = far[:, i * D : (i + 1) * D]

    ab = at[:, 0].reshape(rows, D) + (bo[:, 0].reshape(rows, D).astype(F32) + bias[pl.ds(BIAS_PROJ + 1, 1), :])
    n, r = ln(ab)
    mg = gain[pl.ds(GAIN_MASK + band, 1), :]
    mi = (n * mg).astype(BF)
    act_f = jnp.tanh(mm(mi, um[0]) + wide_row(bias, BIAS_UP + 4 * band, 4))
    act = act_f.astype(BF)
    pre = mm(act, dm[0]) + wide_row(bias, BIAS_DOWN + 2 * band, 2)
    value = pre[:, :SUBF]
    gate = 0.5 * jnp.tanh(0.5 * pre[:, SUBF:]) + 0.5
    mask[:, 0] = (value * gate).astype(BF).reshape(CHAIN, frames, SUBF)
    c = cot[:, 0].reshape(rows, D).astype(F32) * filled.astype(F32)
    cg = c * gate
    og = jnp.concatenate([cg.astype(BF), (cg * value * (1.0 - gate)).astype(BF)], axis=-1)
    ddb = rowsum(og.astype(F32))
    halves(mm_tn(act, og), UP_PART)
    pg = (mm_nt(og, dm[0]) * (1.0 - act_f * act_f)).astype(BF)
    dub = rowsum(pg.astype(F32))
    halves(mm_tn(mi, pg), 0)
    dy = mm_nt(pg, um[0])
    dmg = rowsum(dy * n)
    grad = ln_back(n, r, mg, dy)
    abg[:, 0] = grad.reshape(CHAIN, frames, D)
    low = grad.astype(BF)
    abl[:, 0] = low.reshape(CHAIN, frames, D)

    @pl.when(filled)
    def _():
        early[pl.ds(band, 1), :] = dmg
        early[pl.ds(EARLY_BIAS, 1), :] = early[pl.ds(EARLY_BIAS, 1), :] + rowsum(low.astype(F32))
        for i in range(4):
            row = EARLY_BIAS + BIAS_UP - BIAS_PROJ - 1 + 4 * band + i
            early[pl.ds(row, 1), :] = dub[:, i * D : (i + 1) * D]
        for i in range(2):
            row = EARLY_BIAS + BIAS_DOWN - BIAS_PROJ - 1 + 2 * band + i
            early[pl.ds(row, 1), :] = ddb[:, i * D : (i + 1) * D]


def band_backward_kernel(
    steps, chunk, table, keep, meta, scale, ol_in, xs, w, p, mask_k, mask_f, h0, hk0, cf0, h1, hk1, cf1,
    keep_w, send_w, keep_p, send_p, bias_rows, rows_out, mask_sum,
    ol, wt, pt, da, sh, rg, ch_s, cc_s, dw, dp, db,
):
    n = steps // chunk
    j = pl.program_id(0)
    frames = ol_in.shape[2]
    mask_sum[...] = mask_k[...] + mask_f[...]

    @pl.when(j == 0)
    def _():
        for q in range(CHAIN):
            for k in range(SLOTS):
                if table[q][k] >= 0:
                    ol[pl.ds(table[q][k] * frames, frames), :] = ol_in[q, k]
        ol[pl.ds(BANDS * frames, (steps - BANDS) * frames), :] = jnp.zeros(
            ((steps - BANDS) * frames, D), BF
        )

    backward_chunk(
        keep, xs, ol, w, p, (h0, hk0, cf0, h1, hk1, cf1), dw, dp, db,
        wt, pt, da, sh, rg, ch_s, cc_s, steps, chunk, frames, 1,
    )

    @pl.when(j == n - 1)
    def _():
        part_totals(
            meta[0], dw, dp, scale,
            lambda other, q, way: ((keep_w, send_w)[other], (q * 2 + way) * LSTM_PART),
            lambda other, q, way: ((keep_p, send_p)[other], (q * 2 + way) * HALF_P),
        )
        bias_total(db, scale, bias_rows, 0)
        for q in range(CHAIN):
            for k in range(SLOTS):
                if table[q][k] >= 0:
                    rows_out[q, k] = rg[pl.ds(table[q][k] * frames, frames), :].astype(BF)
                else:
                    rows_out[q, k] = jnp.zeros((frames, D), BF)


def time_backward_kernel(
    steps, chunk, keep, bands, meta, scale, bgrad, abg, at, emb, sp, sm, gain, bias_b, keep_b, send_b, early, mask, xs, w, p, h0, hk0, cf0, h1, hk1, cf1,
    keep_m, send_m, leaving,
    ol, wt, pt, da, sh, rg, ch_s, cc_s, dw, dp, db, xt, atg, late, dsm,
):
    n = steps // chunk
    j = pl.program_id(0)
    frames = bgrad.shape[2]

    @pl.when(j == 0)
    def _():
        xt[...] = jnp.zeros_like(xt)
        late[...] = jnp.zeros_like(late)
        dbg = jnp.zeros((1, D), F32)
        dpb = jnp.zeros((1, D), F32)
        for k in range(SLOTS):
            norm, r = ln(at[:, k].reshape(steps, D))
            dy = bgrad[:, k].reshape(steps, D).astype(F32)
            dbg = dbg + rowsum(dy * norm)
            a = abg[:, k].reshape(steps, D) + ln_back(norm, r, gain[pl.ds(GAIN_BAND, 1), :], dy)
            atg[k] = a
            low = a.astype(BF).astype(F32)
            dpb = dpb + rowsum(low)
            xt[pl.ds(k, steps, stride=ROWS_T), :] = low
        ol[...] = xt[...].astype(BF)
        leaving[:, :SLOTS] = mask[...]
        late[pl.ds(GAIN_BAND, 1), :] = dbg
        late[pl.ds(LATE_BIAS + BIAS_PROJ, 1), :] = dpb
        late[pl.ds(LATE_BIAS + BIAS_LSTM + 2 * G4 // D, 2 * G4 // D), :] = bias_b[...]

    backward_chunk(
        keep, xs, ol, w, p, (h0, hk0, cf0, h1, hk1, cf1), dw, dp, db,
        wt, pt, da, sh, rg, ch_s, cc_s, steps, chunk, ROWS_T, 8,
    )

    @pl.when(j == n - 1)
    def _():
        outs = (keep_m, send_m)
        part_totals(
            meta[0], dw, dp, scale,
            lambda other, q, way: (outs[other], (q * 2 + way) * SHARD_PART),
            lambda other, q, way: (outs[other], (q * 2 + way) * SHARD_PART + LSTM_PART),
        )
        bias_total(db, scale, late, LATE_BIAS + BIAS_LSTM)
        dtg = jnp.zeros((1, D), F32)
        for k in range(SLOTS):
            dy = rg[pl.ds(k, steps, stride=ROWS_T), :]
            norm, r = ln(emb[:, k].reshape(steps, D))
            dtg = dtg + rowsum(dy * norm)
            el = (atg[k] + ln_back(norm, r, gain[pl.ds(GAIN_TIME, 1), :], dy)).astype(BF)
            dsb = rowsum(el.astype(F32))
            band, filled = band_at(meta, bands, k)
            own = gain[pl.ds(band, 1), :]
            norm, r = ln(sp[:, k].reshape(steps, D).astype(F32))
            dsm[k] = mm_tn((norm * own).astype(BF), el).astype(BF)
            dy = mm_nt(el, sm[k])
            dsg = rowsum(dy * norm)

            @pl.when(filled)
            def _():
                late[pl.ds(band, 1), :] = dsg
                late[pl.ds(LATE_BIAS + band, 1), :] = dsb

            leaving[:, SLOTS + k] = ln_back(norm, r, own, dy).astype(BF).reshape(CHAIN, frames, D)
        late[pl.ds(GAIN_TIME, 1), :] = dtg
        for out, band_part in ((keep_m, keep_b), (send_m, send_b)):
            for i in range(2 * CHAIN):
                row = (i + 1) * SHARD_PART - HALF_P
                out[row : row + HALF_P, :] = band_part[i * HALF_P : (i + 1) * HALF_P, :]
            out[pl.ds(MISC_EARLY, EARLY_ROWS), :] = early[...].astype(BF)
            out[pl.ds(MISC_SPLIT, SLOTS * SUBF), :] = dsm[...].reshape(SLOTS * SUBF, D)
            out[pl.ds(MISC_LATE, LATE_ROWS), :] = late[...].astype(BF)


def assemble_kernel(table, leaving, mask, grad):
    for q in range(CHAIN):
        for k in range(SLOTS):
            if table[q][k] >= 0:
                mask[table[q][k]] = leaving[q, k]
                at = pl.ds(table[q][k], leaving.shape[2], stride=BANDS)
                grad[at, :] = leaving[q, SLOTS + k].astype(F32)


def columns_kernel(meta, own, far, up, down, over, up_s, down_s):
    many = own.shape[0]
    fill = meta[2]
    lower = meta[0] == 0
    up_s[...] = jnp.zeros_like(up_s)
    down_s[...] = jnp.zeros_like(down_s)
    for i in range(many):
        for core in range(2):
            part = jnp.where(lower == (core == 0), own[i].astype(F32), far[i].astype(F32))
            for c in range(UP_PART // D):
                at = (core * (UP_PART // D) + c) * D
                up_s[FILL + i * D : FILL + (i + 1) * D, at : at + D] = part[c * D : (c + 1) * D, :]
            down_s[4 * (FILL + i * D) : 4 * (FILL + (i + 1) * D), core * D : (core + 1) * D] = part[UP_PART:, :]
    row = 0
    for scratch, out, unit in ((up_s, up, 1), (down_s, down, 4)):
        rows, wide = out.shape
        at = pl.multiple_of((FILL - fill) * unit, 8)
        out[...] = scratch[pl.ds(at, rows), :]
        past = scratch[pl.ds(pl.multiple_of(at + rows, 8), FILL * unit), :].astype(BF)
        for c in range(wide // D):
            over[row : row + FILL * unit, :] = past[:, c * D : (c + 1) * D]
            row += FILL * unit


def totals_kernel(
    meta, up, down, before, split, split_before, near, far, _,
    lstm_t, proj_t, split_t, up_t, down_t, square, split_s,
):
    fill = meta[2]
    lower = meta[0] == 0
    for core in range(2):
        part = jnp.where(lower == (core == 0), near[...].astype(F32), far[...].astype(F32))
        for c in range(G4 // D):
            lstm_t[core * HALF : (core + 1) * HALF, c * D : (c + 1) * D] = part[c * HALF : (c + 1) * HALF, :]
        proj_t[core * HALF_P : (core + 1) * HALF_P, :] = part[LSTM_PART:, :]
    split_s[...] = jnp.zeros_like(split_s)
    split_s[FILL : FILL + split.shape[0], :] = split[...].astype(F32)
    split_t[...] = split_s[pl.ds(pl.multiple_of(FILL - fill, 8), split_t.shape[0]), :]
    up_t[...] = up[...]
    down_t[...] = down[...]
    split_t[:FILL, :] = split_t[:FILL, :] + split_before[...].astype(F32)
    row = 0
    for out, rows in ((up_t, FILL), (down_t, 4 * FILL)):
        for c in range(out.shape[1] // D):
            at = slice(c * D, (c + 1) * D)
            out[:rows, at] = out[:rows, at] + before[row : row + rows, :].astype(F32)
            row += rows
    total = jnp.zeros((1, D), F32)
    for out in (lstm_t, proj_t, split_t, up_t, down_t):
        line = rowsum(out[...] * out[...])
        for c in range(line.shape[1] // D):
            total = total + line[:, c * D : (c + 1) * D]
    square[...] = jnp.broadcast_to(jnp.sum(total, axis=-1, keepdims=True), (8, D))


def plain_call(kernel, outs, scratch, name, meta, *arrays):
    specs = [ANY if v.ndim == 4 else pl.BlockSpec(memory_space=pltpu.VMEM) for v in arrays]
    return pl.pallas_call(
        kernel,
        in_specs=([] if meta is None else [SMEM]) + specs,
        out_specs=[pl.BlockSpec(memory_space=pltpu.VMEM)] * len(outs),
        out_shape=outs,
        scratch_shapes=[pltpu.VMEM(shape, F32) for shape in scratch],
        compiler_params=pltpu.CompilerParams(vmem_limit_bytes=VMEM),
        cost_estimate=cost(3),
        name=name,
    )(*(() if meta is None else (meta,)), *arrays)


def whole(shape):
    zeros = (0,) * len(shape)
    return pl.BlockSpec(shape, lambda j: zeros)


SMEM = pl.BlockSpec(memory_space=pltpu.SMEM)
ANY = pl.BlockSpec(memory_space=pl.ANY)


def sds(shape, dtype):
    return jax.ShapeDtypeStruct(shape, dtype)


def chunk_specs(n, chunk, rows, flip):
    up = lambda j: (j, 0, 0)
    down = lambda j: (n - 1 - j, 0, 0)
    specs = []
    for way in (down, up) if flip else (up, down):
        specs += [
            pl.BlockSpec((chunk, rows, H), way),
            pl.BlockSpec((chunk, rows, H), way),
            pl.BlockSpec((chunk, rows, 6 * H), way),
        ]
    return specs


def chunk_shapes(steps, rows):
    return [
        sds((steps, rows, H), BF),
        sds((steps, rows, H), BF),
        sds((steps, rows, 6 * H), F32),
    ] * 2


def params():
    return pltpu.CompilerParams(vmem_limit_bytes=VMEM, dimension_semantics=("arbitrary",))


def cost(micros):
    return pl.CostEstimate(flops=micros * 10**9, bytes_accessed=micros * 10**6, transcendentals=0)


def time_forward(keep, bands, meta, sp, sm, gain, bias, scale, near, far, p, later):
    frames = sp.shape[2]
    steps, chunk = CHAIN * frames, 32
    n = steps // chunk
    slab = (CHAIN, SLOTS, frames, D)
    return pl.pallas_call(
        functools.partial(time_forward_kernel, steps, chunk),
        grid=(n,),
        in_specs=[SMEM, SMEM, SMEM]
        + [whole(v.shape) for v in (sp, sm, gain, bias, scale, near, far, p)]
        + [ANY],
        out_specs=[whole(slab)] * 3
        + [whole((steps * ROWS_T, D)), whole((2, D + H, G4)), ANY]
        + chunk_specs(n, chunk, ROWS_T, False),
        out_shape=[sds(slab, F32), sds(slab, F32), sds(slab, BF), sds((steps * ROWS_T, D), BF), sds((2, D + H, G4), BF), sds(later.shape, later.dtype)]
        + chunk_shapes(steps, ROWS_T),
        input_output_aliases={11: 5},
        scratch_shapes=[
            pltpu.VMEM((2, chunk * ROWS_T, G4), F32),
            pltpu.VMEM((2, ROWS_T, H), BF),
            pltpu.VMEM((2, ROWS_T, H), F32),
            pltpu.VMEM((steps * ROWS_T, D), F32),
            pltpu.VMEM((2, steps * ROWS_T, H), BF),
        ],
        compiler_params=params(),
        cost_estimate=cost(66),
        name="time_forward",
    )(keep, bands, meta, sp, sm, gain, bias, scale, near, far, p, later)


def band_forward(table, keep, rows_in, cores, bias, scale, p):
    frames = rows_in.shape[2]
    steps, chunk = STEPS_B, 14
    n = steps // chunk
    slab = (CHAIN, SLOTS, frames, D)
    return pl.pallas_call(
        functools.partial(band_forward_kernel, steps, chunk, table),
        grid=(n,),
        in_specs=[SMEM, whole(slab)] + [whole(v.shape) for v in (cores, bias, scale, p)],
        out_specs=[whole(slab), whole((steps * frames, D)), whole((2, D + H, G4))] + chunk_specs(n, chunk, frames, False),
        out_shape=[sds(slab, BF), sds((steps * frames, D), BF), sds((2, D + H, G4), BF)] + chunk_shapes(steps, frames),
        scratch_shapes=[
            pltpu.VMEM((2, chunk * frames, G4), F32),
            pltpu.VMEM((2, frames, H), BF),
            pltpu.VMEM((2, frames, H), F32),
            pltpu.VMEM((2, steps * frames, H), BF),
        ],
        compiler_params=params(),
        cost_estimate=cost(27),
        name="band_forward",
    )(keep, rows_in, cores, bias, scale, p)


def mask_stage(bands, meta, at, bo, cot, um, dm, gain, bias):
    frames = at.shape[2]
    slab = (CHAIN, SLOTS, frames, D)
    part = pl.BlockSpec((CHAIN, 1, frames, D), lambda k: (0, k, 0, 0))

    def band(*shape):
        return pl.BlockSpec((1,) + shape, lambda k: (k, 0, 0))

    return pl.pallas_call(
        mask_kernel,
        grid=(SLOTS,),
        in_specs=[
            SMEM, SMEM, part, part, part, band(D, 4 * D), band(4 * D, 2 * SUBF),
            whole(gain.shape), whole(bias.shape),
        ],
        out_specs=[
            part, part, part, band(MASK_PART, D), band(MASK_PART, D),
            whole((EARLY_ROWS, D)),
        ],
        out_shape=[
            sds(slab, BF), sds(slab, F32), sds(slab, BF),
            sds((SLOTS, MASK_PART, D), BF), sds((SLOTS, MASK_PART, D), BF),
            sds((EARLY_ROWS, D), F32),
        ],
        compiler_params=params(),
        cost_estimate=cost(16),
        name="mask_stage",
    )(bands, meta, at, bo, cot, um, dm, gain, bias)


def backward_scratch(steps, chunk, rows):
    span = chunk * rows
    return [
        pltpu.VMEM((steps * rows, D), BF),
        pltpu.VMEM((2, G4, D + H), BF),
        pltpu.VMEM((2, D, H), BF),
        pltpu.VMEM((2, span, G4), BF),
        pltpu.VMEM((2, span, H), BF),
        pltpu.VMEM((steps * rows, D), F32),
        pltpu.VMEM((2, rows, H), F32),
        pltpu.VMEM((2, rows, H), F32),
        pltpu.VMEM((2, D + H, G4), F32),
        pltpu.VMEM((2 * H, D), F32),
        pltpu.VMEM((2, 8, G4), F32),
    ]


def total_shapes():
    return [sds((2 * CHAIN * LSTM_PART, D), BF)] * 2 + [sds((PROJ_PART, D), BF)] * 2


def band_backward(table, keep, meta, scale, ol_in, xs, w, p, mask_k, mask_f, saved):
    frames = ol_in.shape[2]
    steps, chunk = STEPS_B, 14
    n = steps // chunk
    slab = (CHAIN, SLOTS, frames, D)
    third = pl.BlockSpec((SLOTS // n, MASK_PART, D), lambda j: (j, 0, 0))
    return pl.pallas_call(
        functools.partial(band_backward_kernel, steps, chunk, table),
        grid=(n,),
        in_specs=[SMEM, SMEM]
        + [whole(v.shape) for v in (scale, ol_in, xs, w, p)]
        + [third, third]
        + chunk_specs(n, chunk, frames, True),
        out_specs=[whole(v.shape) for v in total_shapes()] + [whole((2 * G4 // D, D)), whole(slab), third],
        out_shape=total_shapes() + [sds((2 * G4 // D, D), F32), sds(slab, BF), sds(mask_k.shape, BF)],
        scratch_shapes=backward_scratch(steps, chunk, frames),
        compiler_params=params(),
        cost_estimate=cost(32),
        name="band_backward",
    )(keep, meta, scale, ol_in, xs, w, p, mask_k, mask_f, *saved)


def time_backward(keep, bands, meta, scale, bgrad, abg, at, emb, sp, sm, gain, bias_b, keep_b, send_b, early, mask, xs, w, p, saved):
    frames = bgrad.shape[2]
    steps, chunk = CHAIN * frames, 32
    n = steps // chunk
    slab = (CHAIN, SLOTS, frames, D)
    outs = [sds((MISC, D), BF)] * 2 + [sds((CHAIN, 2 * SLOTS, frames, D), BF)]
    return pl.pallas_call(
        functools.partial(time_backward_kernel, steps, chunk),
        grid=(n,),
        in_specs=[SMEM, SMEM, SMEM]
        + [whole(v.shape) for v in (scale, bgrad, abg, at, emb, sp, sm, gain, bias_b, keep_b, send_b, early, mask, xs, w, p)]
        + chunk_specs(n, chunk, ROWS_T, True),
        out_specs=[whole(v.shape) for v in outs],
        out_shape=outs,
        scratch_shapes=backward_scratch(steps, chunk, ROWS_T)
        + [pltpu.VMEM((steps * ROWS_T, D), F32), pltpu.VMEM((SLOTS, steps, D), F32)]
        + [pltpu.VMEM((LATE_ROWS, D), F32), pltpu.VMEM((SLOTS, SUBF, D), BF)],
        compiler_params=params(),
        cost_estimate=cost(96),
        name="time_backward",
    )(keep, bands, meta, scale, bgrad, abg, at, emb, sp, sm, gain, bias_b, keep_b, send_b, early, mask, xs, w, p, *saved)


def chain_groups():
    many = lax.axis_size("rows") // CHAIN
    return [[CHAIN * g + q for q in range(CHAIN)] for g in range(many)]


def place_groups():
    many = lax.axis_size("rows") // CHAIN
    return [[CHAIN * g + q for g in range(many)] for q in range(CHAIN)]


def across(v, groups, axis=0):
    return lax.all_to_all(v, "rows", axis, axis, axis_index_groups=groups, tiled=True)


def spread(v, groups):
    return across(jnp.broadcast_to(v[None], (len(groups[0]),) + v.shape), groups)


def swap_dir(v):
    return lax.ppermute(v, "dir", [(0, 1), (1, 0)])


def ordered(side, near, far):
    return jnp.where(side == 0, jnp.stack([near, far]), jnp.stack([far, near]))


def to_bands(v, more=None):
    v = jnp.concatenate([v, v[:1]])
    parts = []
    for blocks in band_blocks(lax.axis_size("rows")):
        cuts = [v[first : first + places] for first, places, _ in blocks]
        parts.append(jnp.concatenate(cuts + ([] if more is None else [more])))
    return jnp.stack(parts)


def my_bit(bit):
    return (lax.axis_index("rows") >> bit) & 1


def swap_bit(v, bit):
    return lax.ppermute(v, "rows", [(r, r ^ (1 << bit)) for r in range(lax.axis_size("rows"))])


def double(v, bit):
    return ordered(my_bit(bit), v, swap_bit(v, bit))


def halve(v, bit, axis):
    mine = my_bit(bit)
    kept = lax.dynamic_index_in_dim(v, mine, axis, False)
    return kept + swap_bit(lax.dynamic_index_in_dim(v, 1 - mine, axis, False), bit)


def my_rows(values):
    return jnp.asarray(np.array(values, np.int32))[lax.axis_index("rows")]


def fills(rows):
    return [shard_start(s, rows) * D - s * BANDS * D // rows for s in range(rows)]


def tied(v, *others):
    for other in others:
        one = lax.slice(other, (0,) * other.ndim, (1,) * other.ndim).reshape(())
        v = jnp.where(jnp.isnan(one), jnp.zeros_like(v), v)
    return v


def rows_after(shard):
    rows = lax.axis_size("rows")
    head = FILL * (shard.shape[0] * rows // (BANDS * D))
    if not square_slice():
        return shard[:1]
    return lax.ppermute(shard[:head].astype(BF), "rows", [(r + 1, r) for r in range(rows - 1)])


def whole_bands(shard, after):
    rows = lax.axis_size("rows")
    unit = shard.shape[0] * rows // (BANDS * D)
    head = FILL * unit
    spare = jnp.zeros((head,) + shard.shape[1:], shard.dtype)
    long = jnp.concatenate([shard, after, spare])
    return lax.dynamic_slice_in_dim(long, my_rows(fills(rows)) * unit, SLOTS // CHAIN * D * unit, 0)


def past_shard(own, unit):
    rows = lax.axis_size("rows")
    fill = my_rows(fills(rows)) * unit
    head = jnp.zeros((FILL * unit,) + own.shape[1:], own.dtype)
    many = BANDS * D * unit // rows
    over = lax.dynamic_slice_in_dim(jnp.concatenate([own, head]), many - fill, FILL * unit, 0)
    return lax.ppermute(over, "rows", [(r, r + 1) for r in range(rows - 1)])


def to_shard(own, before, unit):
    rows = lax.axis_size("rows")
    fill = my_rows(fills(rows)) * unit
    many = BANDS * D * unit // rows
    head = jnp.zeros((FILL * unit,) + own.shape[1:], own.dtype)
    moved = lax.dynamic_slice_in_dim(jnp.concatenate([head, own]), FILL * unit - fill, many, 0)
    before = jnp.concatenate([before, jnp.zeros((many - FILL * unit,) + own.shape[1:], own.dtype)])
    row = lax.broadcasted_iota(jnp.int32, (many, 1), 0)
    return jnp.where(row < fill, before, moved)


def square_slice():
    return lax.axis_size("rows") == CHAIN * CHAIN


def pick_bands(wide):
    blocks = band_blocks(lax.axis_size("rows"))
    place = lax.axis_index("rows") % CHAIN
    wide = jnp.concatenate([wide, wide[:1]])
    cuts = []
    for at in range(len(blocks[0])):
        first = jnp.asarray(np.array([b[at][0] for b in blocks], np.int32))[place]
        cuts.append(lax.dynamic_slice_in_dim(wide, first, blocks[0][at][1], 0))
    return jnp.concatenate(cuts)


def place_bands(part, valid):
    blocks = band_blocks(lax.axis_size("rows"))
    place = lax.axis_index("rows") % CHAIN
    part = part * valid[:, None]
    total = jnp.zeros((BANDS + 1, part.shape[1]), F32)
    row = 0
    for at in range(len(blocks[0])):
        first = jnp.asarray(np.array([b[at][0] for b in blocks], np.int32))[place]
        cut = part[row : row + blocks[0][at][1]]
        total = lax.dynamic_update_slice_in_dim(total, cut, first, 0)
        row += blocks[0][at][1]
    return total[:BANDS]


def band_weights(shard, after, gate):
    rows = lax.axis_size("rows")
    unit = shard.shape[0] * rows // BANDS
    low = shard.astype(BF)
    if not square_slice():
        full = lax.all_gather(low, "rows", axis=0, tiled=True).reshape(BANDS, unit, -1)
        return pick_bands(full)
    own = whole_bands(low, after)
    own = tied(own, gate)
    own = lax.all_gather(own, "rows", axis=0, axis_index_groups=place_groups(), tiled=True)
    return own.reshape(SLOTS, unit, -1)


def band_sums(grads, apart):
    if not square_slice():
        return grads
    if not apart:
        return halve(halve(grads.reshape(2, 2, SLOTS // CHAIN, *grads.shape[1:]), 2, 1), 3, 0)
    return lax.psum_scatter(
        grads, "rows", scatter_dimension=0, axis_index_groups=place_groups(), tiled=True
    )


def shard_parts(own, unit):
    if not square_slice():
        return own, own
    own = own.reshape(SLOTS // CHAIN * unit, -1)
    return own, past_shard(own, unit // D)


def shard_sums(parts, unit, valid):
    own, before = parts
    if square_slice():
        return to_shard(own, before, unit // D).astype(F32)
    flat = place_bands(own.reshape(SLOTS, -1).astype(F32), valid).astype(BF)
    flat = flat.reshape(BANDS * unit, -1)
    return lax.psum_scatter(flat, "rows", scatter_dimension=0, tiled=True).astype(F32)


def both_cores(kept, sent):
    return kept + swap_dir(sent)


def mask_columns(side, own, far):
    pair = ordered(side, own, far)
    many = own.shape[0]
    up = pair[:, :, :UP_PART].reshape(2, many, UP_PART // D, D, D)
    up = jnp.transpose(up, (1, 3, 0, 2, 4)).reshape(many, D, 4 * D)
    down = jnp.transpose(pair[:, :, UP_PART:], (1, 2, 0, 3)).reshape(many, 4 * D, 2 * SUBF)
    return up, down


def sum_rows(v, bits, wire=F32):
    for bit in bits:
        v = v.astype(wire)
        v = v.astype(F32) + swap_bit(v, bit).astype(F32)
    return v


def gather_first(side, lstm_low, proj_low, split_weight, sp_parts, up_after, down_after):
    if not square_slice():
        lstm = lax.all_gather(lstm_low, "rows", axis=0, tiled=True)
        proj = lax.all_gather(proj_low, "rows", axis=0, tiled=True).reshape(2, 2 * H, D)
        cut = jnp.transpose(lstm.reshape(2, 2, CHAIN, 2, HALF, G4), (0, 3, 2, 1, 4, 5))
        sp = across(sp_parts, chain_groups())
        near = lax.dynamic_index_in_dim(cut[0], side, 0, False)
        far = lax.dynamic_index_in_dim(cut[0], 1 - side, 0, False)
        return near, far, jnp.swapaxes(cut[1], 0, 1), proj, band_weights(split_weight, None, None), sp
    flat = HALF_P * D // G4
    packed = jnp.concatenate(
        [
            lax.dynamic_slice_in_dim(lstm_low, side * HALF, HALF, 0),
            lax.dynamic_slice_in_dim(proj_low, side * HALF_P, HALF_P, 0).reshape(flat, G4),
        ]
    )
    split = whole_bands(split_weight.astype(BF), rows_after(split_weight))
    column = double(packed, 3)
    sp = across(tied(sp_parts, column), chain_groups())
    column = double(tied(column, split), 2)
    split = double(split, 3)
    time = jnp.concatenate([column[:, 0], column[:, 1, HALF:]], axis=1)
    band = column[:, 1, :HALF]
    time = tied(time, split)
    split = double(split, 2)
    time = double(time, 0)
    time = double(tied(time, split, sp, up_after, down_after), 1)
    split = jnp.swapaxes(split, 0, 1).reshape(SLOTS, SUBF, D)
    near = time.reshape(CHAIN, 2, HALF + 2 * flat, G4)
    far = swap_dir(near)
    band = ordered(side, band, swap_dir(band))
    band = spread(tied(band, near), chain_groups())
    proj = ordered(side, near[:, :, HALF:], far[:, :, HALF:]).reshape(2, CHAIN, 2, 2, flat, G4)
    proj = jnp.transpose(proj, (3, 2, 1, 0, 4, 5)).reshape(2, 2 * H, D)
    return near, far, band, proj, split, sp


def unpacked(pair):
    lead = pair.shape[:-3]
    v = jnp.swapaxes(pair.reshape(*lead, 2, G4 // D, HALF, D), -3, -2)
    return v.reshape(*lead, 2 * HALF, G4)


def traded(parts, bit):
    flat = [v.reshape(-1, D) for v in parts]
    got = swap_bit(jnp.concatenate(flat), bit)
    out, row = [], 0
    for v, rows in zip(parts, flat):
        out.append(got[row : row + rows.shape[0]].reshape(v.shape))
        row += rows.shape[0]
    return out


def cut(v, bit, axis):
    mine = my_bit(bit)
    return (
        lax.dynamic_index_in_dim(v, mine, axis, False),
        lax.dynamic_index_in_dim(v, 1 - mine, axis, False),
    )


def all_totals(side, sums, lstm_b, valid):
    v = sums[:MISC_SPLIT].reshape(CHAIN, 2, SHARD_PART, D)
    split = sums[MISC_SPLIT:MISC_LATE]
    small = sums[MISC_LATE:].astype(F32)
    if not square_slice():
        bits = range((lax.axis_size("rows") - 1).bit_length())
        band = lstm_b.reshape(CHAIN, 2, LSTM_PART, D)
        lstm = jnp.stack([v[:, :, :LSTM_PART], band])
        lstm = jnp.transpose(ordered(side, lstm, swap_dir(lstm)), (1, 3, 2, 0, 4, 5))
        lstm = unpacked(lstm).reshape(-1, G4)
        proj = v[:, :, LSTM_PART:].reshape(CHAIN, 2, 2, HALF_P, D)
        proj = jnp.transpose(ordered(side, proj, swap_dir(proj)), (3, 2, 1, 0, 4, 5)).reshape(-1, D)
        lstm, proj = (
            lax.psum_scatter(t, "rows", scatter_dimension=0, tiled=True).astype(F32) for t in (lstm, proj)
        )
        split = shard_sums((split.reshape(SLOTS, SUBF, D), None), SUBF, valid)
        return lstm, proj, split, sum_rows(small, bits, BF), small
    kept, sent = cut(v.reshape(2, 2, 2, SHARD_PART, D), 0, 1)
    got, more = traded([sent, small.astype(BF)], 0)
    v, small = kept + got, small.astype(BF).astype(F32) + more.astype(F32)
    kept, sent = cut(v, 1, 0)
    got, more = traded([sent, small.astype(BF)], 1)
    v, small = kept + got, small.astype(BF).astype(F32) + more.astype(F32)
    late = v
    time_rows = LSTM_PART + HALF_P
    band = jnp.concatenate([lstm_b.reshape(2, LSTM_PART, D), v[:, time_rows:]], axis=1)
    v = jnp.stack([v[:, :time_rows], band])
    split = split.reshape(2, 2, SLOTS // CHAIN * SUBF, D)
    for bit, axis in ((2, 1), (3, 0)):
        kept, sent = cut(v, bit, axis)
        kept_s, sent_s = cut(split, bit, axis)
        got, got_s, more = traded([sent, sent_s, small.astype(BF)], bit)
        v, split = kept + got, kept_s + got_s
        small = small.astype(BF).astype(F32) + more.astype(F32)
    return v, split, small, late


def finish_kernel(*refs):
    square, small = refs[:2]
    totals = refs[2:7]
    olds = refs[7:28]
    norm_out = refs[28]
    outs = refs[29:]
    gain_rows = [(0, LATE_BIAS, 0), (LATE_ROWS, EARLY_BIAS, LATE_BIAS)]
    bias_rows = [(LATE_BIAS, LATE - LATE_BIAS, 0), (LATE_ROWS + EARLY_BIAS, EARLY - EARLY_BIAS, LATE - LATE_BIAS)]
    line = rowsum(small[...] * small[...])
    norm = jnp.sqrt(square[:1, :1] + jnp.sum(line, axis=-1, keepdims=True))
    norm_out[...] = norm
    clip = jnp.minimum(1.0, CLIP_NORM / (norm + 1e-06))

    def put(index, at, gradient, rate):
        velocity, weight, average = olds[3 * index : 3 * index + 3]
        clipped = gradient * clip
        velocity_new = MOMENTUM * velocity[at, :] + clipped
        weight_new = weight[at, :] - rate * (clipped + MOMENTUM * velocity_new)
        results = (clipped, velocity_new, weight_new, AVERAGE * average[at, :] + (1.0 - AVERAGE) * weight_new)
        for out, value in zip(outs[4 * index : 4 * index + 4], results):
            out[at, :] = value

    for index in range(5):
        rows = totals[index].shape[0]
        put(index, slice(0, rows), totals[index][...], LEARN_RATE)
    for index, pieces in ((5, gain_rows), (6, bias_rows)):
        for first, many, at in pieces:
            put(index, slice(at, at + many), small[first : first + many, :], GAIN_RATE)


def finish(square, small, totals, olds):
    arrays = (square, small) + totals + olds
    outs = [sds((1, 1), F32)]
    for old in olds[::3]:
        outs += [sds(old.shape, F32)] * 4
    return pl.pallas_call(
        finish_kernel,
        grid=(1,),
        in_specs=[whole(v.shape) for v in arrays],
        out_specs=[whole(v.shape) for v in outs],
        out_shape=outs,
        compiler_params=params(),
        cost_estimate=cost(8),
        name="finish",
    )(*arrays)


def halved_columns():
    scale = np.full((1, G4), 0.5, np.float32)
    scale[:, 2 * H : 3 * H] = 1.0
    return jnp.asarray(scale)


def on_device(
    spectra,
    mask_grad,
    clip_starts,
    split_weight,
    split_velocity,
    split_average,
    lstm_weight,
    lstm_velocity,
    lstm_average,
    proj_weight,
    proj_velocity,
    proj_average,
    up_weight,
    up_velocity,
    up_average,
    down_weight,
    down_velocity,
    down_average,
    gain_weight,
    gain_velocity,
    gain_average,
    bias_weight,
    bias_velocity,
    bias_average,
):
    side = lax.axis_index("dir")
    row = lax.axis_index("rows")
    place = row % CHAIN
    rows = lax.axis_size("rows")
    bits = range((rows - 1).bit_length())
    frames = spectra.shape[1]
    steps = CHAIN * frames
    scale = halved_columns()
    fill = my_rows(fills(rows)) if square_slice() else place
    meta = jnp.stack([side, place, fill]).astype(jnp.int32)
    table = band_table(rows)
    valid = jnp.asarray((np.array(table) >= 0).astype(np.float32))[place]
    bands = jnp.asarray(np.array(table, np.int32).reshape(-1))

    flags = lax.dynamic_index_in_dim(clip_starts[0], side, 1, False).astype(BF)
    flag_slab = jnp.broadcast_to(flags[:, None], (frames, SUBF))
    sp_parts = to_bands(jnp.transpose(spectra[0, :, 0], (1, 0, 2)), flag_slab[None])
    up_after, down_after = rows_after(up_weight), rows_after(down_weight)
    near, far, band_w, proj, split_mat, sp = gather_first(
        side, (lstm_weight * scale).astype(BF), proj_weight.astype(BF), split_weight, sp_parts, up_after, down_after
    )
    starts = sp[:, SLOTS, :, 0].reshape(steps).astype(F32)
    keep_time = jnp.concatenate([1.0 - starts, 1.0 - starts[1:], jnp.ones((1,), F32)])
    keep_np = np.ones((2 * STEPS_B,), np.float32)
    keep_np[STEPS_B + BANDS - 1] = 0.0
    keep_band = jnp.asarray(keep_np)
    cot_parts = to_bands(jnp.transpose(mask_grad[0, :, 0], (1, 0, 2)))

    up_mat = band_weights(up_weight, up_after, near)
    down_mat = band_weights(down_weight, down_after, near)

    emb, after_time, band_rows, xs_t, w_time, cot_parts, *saved_t = time_forward(
        keep_time, bands, meta, sp, split_mat, gain_weight, bias_weight, scale, near, far, proj[0], cot_parts
    )
    band_out, xs_b, w_band, *saved_b = band_forward(
        table, keep_band, across(band_rows, chain_groups()), band_w, bias_weight, scale, proj[1]
    )
    mask, abg, abl, kept, sent, early = mask_stage(
        bands, meta, after_time, across(band_out, chain_groups()), across(cot_parts, chain_groups()),
        up_mat, down_mat, gain_weight, bias_weight,
    )

    ol_in = across(abl, chain_groups())
    keep_w, send_w, keep_b, send_b, bias_b, bgrad, mask_sum = band_backward(
        table, keep_band, meta, scale, ol_in, xs_b, w_band, proj[1], kept, swap_dir(sent), saved_b
    )
    bgrad = across(bgrad, chain_groups())
    lstm_sum = both_cores(tied(keep_w, bgrad), send_w)
    mask_own = band_sums(mask_sum, True)
    lstm_b = lstm_sum
    if square_slice():
        lstm_b = lax.psum_scatter(
            lstm_sum, "rows", scatter_dimension=0, axis_index_groups=chain_groups(), tiled=True
        )
    keep_m, send_m, leaving = time_backward(
        keep_time, bands, meta, scale, bgrad, abg, after_time, emb, sp, split_mat,
        gain_weight, bias_b, keep_b, send_b, early, mask, xs_t, w_time, proj[0], saved_t,
    )
    sums = both_cores(tied(keep_m, lstm_b, mask_own), send_m)
    mask_far = swap_dir(mask_own)
    if square_slice():
        units = BANDS * D // rows
        up_own, down_own, over = plain_call(
            columns_kernel,
            [
                sds((units, 4 * D), F32), sds((4 * units, 2 * SUBF), F32),
                sds((FILL * 4 + 4 * FILL * 2, D), BF),
            ],
            [(5 * D, 4 * D), (20 * D, 2 * SUBF)], "mask_columns", meta, mask_own, mask_far,
        )
        before = lax.ppermute(over, "rows", [(r, r + 1) for r in range(rows - 1)])
        v, split, small, _ = all_totals(side, sums, lstm_b, valid)
        leaving = across(leaving, chain_groups())
        split_before = past_shard(split, 1)
        lstm_total, proj_total, split_total, up_total, down_total, square = plain_call(
            totals_kernel,
            [
                sds(lstm_weight.shape, F32), sds(proj_weight.shape, F32), sds(split_weight.shape, F32),
                sds(up_weight.shape, F32), sds(down_weight.shape, F32), sds((8, D), F32),
            ],
            [(5 * D, D)], "totals", meta, up_own, down_own, before, split, split_before,
            v, swap_dir(v), leaving,
        )
    else:
        up_own, down_own = mask_columns(side, mask_own, mask_far)
        lstm_total, proj_total, split_total, small, _ = all_totals(side, sums, lstm_b, valid)
        leaving = across(leaving, chain_groups())
        up_total = shard_sums(shard_parts(up_own, D), D, valid)
        down_total = shard_sums(shard_parts(down_own, 4 * D), 4 * D, valid)
        parts = (split_total, lstm_total, proj_total, up_total, down_total)
        square = jnp.full((8, D), sum(jnp.sum(v * v) for v in parts), F32)
    band_mask, spectra_grad = pl.pallas_call(
        functools.partial(assemble_kernel, table),
        grid=(1,),
        in_specs=[whole(leaving.shape)],
        out_specs=[whole((BANDS, frames, D)), whole((frames * BANDS, D))],
        out_shape=[sds((BANDS, frames, D), BF), sds((frames * BANDS, D), F32)],
        compiler_params=params(),
        cost_estimate=cost(3),
        name="assemble",
    )(leaving)
    band_mask = jnp.transpose(band_mask, (1, 0, 2))[None, :, None]
    spectra_grad = spectra_grad.reshape(1, frames, 1, BANDS, D)
    square = sum_rows(square, bits)
    norm, *results = finish(
        square,
        small,
        (split_total, lstm_total, proj_total, up_total, down_total),
        (
            split_velocity, split_weight, split_average, lstm_velocity, lstm_weight, lstm_average,
            proj_velocity, proj_weight, proj_average, up_velocity, up_weight, up_average,
            down_velocity, down_weight, down_average, gain_velocity, gain_weight, gain_average,
            bias_velocity, bias_weight, bias_average,
        ),
    )
    return (band_mask, spectra_grad, norm.reshape(())) + tuple(results)


def solution(mesh):
    per_row = P("rows", None)
    row_major = P("rows", None, "dir", None, None)
    return jax.shard_map(
        on_device,
        mesh=mesh,
        in_specs=(row_major, row_major, P("rows", None, None)) + (per_row,) * 15 + (P(),) * 6,
        out_specs=(row_major, row_major, P()) + (per_row,) * 20 + (P(),) * 8,
        check_vma=False,
    )
```

```python
import functools

import jax
import jax.numpy as jnp
import numpy as np
from jax import lax
from jax.experimental import pallas as pl
from jax.experimental.pallas import tpu as pltpu
from jax.sharding import PartitionSpec as P

D = 128
H = 256
G4 = 4 * H
BANDS = 41
SUBF = 128
CHAIN = 4
SLOTS = 12
FILL = 128
ROWS_T = 16
STEPS_B = 42
VMEM = 60 << 20
PAIR = 2
HALF = (D + H) // CHAIN // 2
HALF_P = H // CHAIN // 2

EPSILON = 1e-05
MOMENTUM = 0.9
LEARN_RATE = 5.0
GAIN_RATE = 50.0
AVERAGE = 0.5
CLIP_NORM = 5.0


GAIN_TIME, GAIN_BAND, GAIN_MASK = BANDS, BANDS + 1, BANDS + 2
BIAS_LSTM = BANDS
BIAS_PROJ = BIAS_LSTM + 16 * H // D
BIAS_UP = BIAS_PROJ + 2
BIAS_DOWN = BIAS_UP + 4 * BANDS
EARLY_BIAS = BANDS
EARLY = EARLY_BIAS + BIAS_DOWN + 2 * BANDS - BIAS_PROJ - 1
EARLY_ROWS = -(-EARLY // 16) * 16
LATE_BIAS = GAIN_MASK
LATE = LATE_BIAS + BIAS_PROJ + 1
LATE_ROWS = -(-LATE // 16) * 16

BF = jnp.bfloat16
F32 = jnp.float32


def mm(a, b):
    return jnp.dot(a, b, preferred_element_type=F32)


def mm_nt(a, b):
    return lax.dot_general(a, b, (((1,), (1,)), ((), ())), preferred_element_type=F32)


def mm_tn(a, b):
    return lax.dot_general(a, b, (((0,), (0,)), ((), ())), preferred_element_type=F32)


def ln(v):
    c = v - jnp.mean(v, axis=-1, keepdims=True)
    r = lax.rsqrt(jnp.mean(c * c, axis=-1, keepdims=True) + EPSILON)
    return c * r, r


def ln_back(n, r, gain, dy):
    dg = dy * gain
    return r * (
        dg - jnp.mean(dg, axis=-1, keepdims=True) - n * jnp.mean(dg * n, axis=-1, keepdims=True)
    )


def rowsum(v):
    return jnp.sum(v, axis=0, keepdims=True)


UP_PART = 2 * D
MASK_PART = UP_PART + 4 * D
LSTM_PART = HALF * G4 // D
PROJ_PART = 2 * CHAIN * HALF_P
SHARD_PART = LSTM_PART + 2 * HALF_P
MISC_SPLIT = 2 * CHAIN * SHARD_PART
MISC_LATE = MISC_SPLIT + SLOTS * SUBF
MISC_EARLY = MISC_LATE + LATE_ROWS
MISC = MISC_EARLY + EARLY_ROWS


def shard_start(shard, rows):
    return -(-shard * BANDS // rows)


def band_blocks(rows):
    if rows == CHAIN * CHAIN:
        three = SLOTS // CHAIN
        return [
            [
                (shard_start(CHAIN * z + q, rows), three, shard_start(CHAIN * z + q + 1, rows) - shard_start(CHAIN * z + q, rows))
                for z in range(CHAIN)
            ]
            for q in range(CHAIN)
        ]
    each = BANDS // CHAIN
    return [[(each * q, SLOTS, each if q + 1 < CHAIN else BANDS - each * q)] for q in range(CHAIN)]


def band_table(rows):
    return [
        [first + i if i < filled else -1 for first, places, filled in blocks for i in range(places)]
        for blocks in band_blocks(rows)
    ]


def wide_row(rows, first, many):
    return jnp.concatenate([rows[pl.ds(first + i, 1), :] for i in range(many)], axis=1)


def forward_chunk(keep, x_ref, w_ref, bias, scale, first_row, outs, gates, hk_s, ck_s, steps, chunk, rows, unroll, hall):
    n = steps // chunk
    j = pl.program_id(0)
    first = (j * chunk, (n - 1 - j) * chunk)

    @pl.when(j == 0)
    def _():
        hk_s[...] = jnp.zeros_like(hk_s)
        ck_s[...] = jnp.zeros_like(ck_s)

    for d in range(2):
        x = x_ref[pl.ds(pl.multiple_of(first[d] * rows, chunk * rows), chunk * rows), :]
        b = wide_row(bias, first_row + d * (G4 // D), G4 // D) * scale[...]
        gates[d] = mm(x, w_ref[d, :D]) + b

    def step(t, carry):
        new = []
        for d in range(2):
            hk, ck = carry[2 * d], carry[2 * d + 1]
            tt = t if d == 0 else chunk - 1 - t
            at = first[d] + tt
            now = keep[d * steps + at]
            later = jnp.minimum(at + 1, steps - 1) if d == 0 else jnp.maximum(at - 1, 0)
            nxt = keep[d * steps + later]
            h_ref, hk_ref, cf_ref = outs[3 * d : 3 * d + 3]
            a = gates[d, pl.ds(pl.multiple_of(tt * rows, rows), rows), :] + mm(hk, w_ref[d, D:])
            ti = jnp.tanh(a[:, :H])
            tf = jnp.tanh(a[:, H : 2 * H])
            g = jnp.tanh(a[:, 2 * H : 3 * H])
            to = jnp.tanh(a[:, 3 * H :])
            i = 0.5 * ti + 0.5
            f = 0.5 * tf + 0.5
            o = 0.5 * to + 0.5
            c = f * ck + i * g
            tc = jnp.tanh(c)
            h = o * tc
            h_low = h.astype(BF)
            hk_ref[tt] = hk
            h_ref[tt] = h_low
            if hall is not None:
                hall[d, pl.ds(pl.multiple_of(at * rows, rows), rows), :] = h_low
            cf_ref[tt, :, :H] = o * (1.0 - tc * tc)
            cf_ref[tt, :, H : 2 * H] = g * (0.5 - 0.5 * ti * ti)
            cf_ref[tt, :, 2 * H : 3 * H] = ck * (0.5 - 0.5 * tf * tf)
            cf_ref[tt, :, 3 * H : 4 * H] = i * (1.0 - g * g)
            cf_ref[tt, :, 4 * H : 5 * H] = tc * (0.5 - 0.5 * to * to)
            cf_ref[tt, :, 5 * H :] = f * now
            new += [(h * nxt).astype(BF), c * nxt]
        return tuple(new)

    done = lax.fori_loop(
        0, chunk, step, (hk_s[0], ck_s[0], hk_s[1], ck_s[1]), unroll=unroll
    )
    for d in range(2):
        hk_s[d] = done[2 * d]
        ck_s[d] = done[2 * d + 1]


def backward_chunk(
    keep, x_ref, ol, w_ref, p_ref, ins, dw, dp, db, wt, pt, da, sh, rg, ch_s, cc_s, steps, chunk, rows, unroll
):
    n = steps // chunk
    j = pl.program_id(0)
    first = ((n - 1 - j) * chunk, j * chunk)
    span = chunk * rows

    @pl.when(j == 0)
    def _():
        ch_s[...] = jnp.zeros_like(ch_s)
        cc_s[...] = jnp.zeros_like(cc_s)
        rg[...] = jnp.zeros_like(rg)
        dw[...] = jnp.zeros_like(dw)
        dp[...] = jnp.zeros_like(dp)
        db[...] = jnp.zeros_like(db)
        for d in range(2):
            wt[d] = w_ref[d].T
            pt[d] = p_ref[pl.ds(d * H, H), :].T

    at_rows = [pl.ds(pl.multiple_of(first[d] * rows, span), span) for d in range(2)]
    for d in range(2):
        sh[d] = mm(ol[at_rows[d], :], pt[d]).astype(BF)

    def step(t, carry):
        new = []
        for d in range(2):
            ch, cc = carry[2 * d], carry[2 * d + 1]
            tt = chunk - 1 - t if d == 0 else t
            now = keep[d * steps + first[d] + tt]
            cf = ins[3 * d + 2]
            here = pl.ds(pl.multiple_of(tt * rows, rows), rows)
            dh = sh[d, here, :].astype(F32) + ch
            dc = cc + dh * cf[tt, :, :H]
            da_now = jnp.concatenate(
                [
                    (dc * cf[tt, :, H : 2 * H]).astype(BF),
                    (dc * cf[tt, :, 2 * H : 3 * H]).astype(BF),
                    (dc * cf[tt, :, 3 * H : 4 * H]).astype(BF),
                    (dh * cf[tt, :, 4 * H : 5 * H]).astype(BF),
                ],
                axis=-1,
            )
            da[d, here, :] = da_now
            new += [mm(da_now, wt[d, :, D:]) * now, dc * cf[tt, :, 5 * H :]]
        return tuple(new)

    done = lax.fori_loop(0, chunk, step, (ch_s[0], cc_s[0], ch_s[1], cc_s[1]), unroll=unroll)
    ones = jnp.ones((8, span), BF)
    for d in range(2):
        ch_s[d] = done[2 * d]
        cc_s[d] = done[2 * d + 1]
        here = at_rows[d]
        grad = da[d]
        rg[here, :] = rg[here, :] + mm(grad, wt[d, :, :D])
        dw[d, :D, :] = dw[d, :D, :] + mm_tn(x_ref[here, :], grad)
        dw[d, D:, :] = dw[d, D:, :] + mm_tn(ins[3 * d + 1][...].reshape(span, H), grad)
        db[d] = db[d] + mm(ones, grad)
        at_p = pl.ds(d * H, H)
        dp[at_p, :] = dp[at_p, :] + mm_tn(ins[3 * d][...].reshape(span, H), ol[here, :])


def lay_weights(side, near, far, w):
    for way in range(2):
        for q in range(CHAIN):
            for part, of in ((near, side), (far, 1 - side)):
                at = pl.multiple_of(q * 2 * HALF + of * HALF, HALF)
                w[way, pl.ds(at, HALF), :] = part[q, way, :HALF, :]


def part_totals(side, dw, dp, scale, places, proj_places):
    for way in range(2):
        for q in range(CHAIN):
            for other in range(2):
                of = 1 - side if other else side
                at = pl.multiple_of(q * 2 * HALF + of * HALF, HALF)
                part = (dw[way, pl.ds(at, HALF), :] * scale[...]).astype(BF)
                out, row = places(other, q, way)
                for c in range(G4 // D):
                    out[row + c * HALF : row + (c + 1) * HALF, :] = part[:, c * D : (c + 1) * D]
                at = pl.multiple_of(way * H + q * 2 * HALF_P + of * HALF_P, HALF_P)
                out, row = proj_places(other, q, way)
                out[row : row + HALF_P, :] = dp[pl.ds(at, HALF_P), :].astype(BF)


def bias_total(db, scale, out, first):
    for way in range(2):
        row = db[way, :1, :] * scale[...]
        for i in range(G4 // D):
            out[pl.ds(first + way * (G4 // D) + i, 1), :] = row[:, i * D : (i + 1) * D]


def band_at(meta, bands, k):
    band = bands[meta[1] * SLOTS + k]
    return jnp.maximum(band, 0), band >= 0


def time_forward_kernel(
    steps, chunk, table, keep, bands, meta, sp, sm, gain, bias, scale, near, far, p, cot,
    emb, at, br, xs, w, cot_parts, h0, hk0, cf0, h1, hk1, cf1,
    gates, hk_s, ck_s, xt, hall,
):
    n = steps // chunk
    j = pl.program_id(0)
    frames = sp.shape[2]

    @pl.when(j == 0)
    def _():
        lay_weights(meta[0], near, far, w)
        for q in range(CHAIN):
            for k in range(SLOTS):
                cot_parts[q, k] = cot[max(table[q][k], 0)]
        xt[...] = jnp.zeros_like(xt)
        for k in range(SLOTS):
            v = sp[:, k].reshape(steps, D).astype(F32)
            band = band_at(meta, bands, k)[0]
            normed = (ln(v)[0] * gain[pl.ds(band, 1), :]).astype(BF)
            e = mm(normed, sm[k]) + bias[pl.ds(band, 1), :]
            emb[:, k] = e.reshape(CHAIN, frames, D)
            xt[pl.ds(k, steps, stride=ROWS_T), :] = ln(e)[0] * gain[pl.ds(GAIN_TIME, 1), :]
        xs[...] = xt[...].astype(BF)

    forward_chunk(
        keep, xs, w, bias, scale, BIAS_LSTM, (h0, hk0, cf0, h1, hk1, cf1), gates, hk_s, ck_s, steps, chunk, ROWS_T, 16, hall
    )

    @pl.when(j == n - 1)
    def _():
        span = 512
        for s in range(0, steps * ROWS_T, span):
            here = pl.ds(s, span)
            xt[here, :] = mm(hall[0, here, :], p[:H]) + mm(hall[1, here, :], p[H:])
        for k in range(SLOTS):
            to = xt[pl.ds(k, steps, stride=ROWS_T), :] + bias[pl.ds(BIAS_PROJ, 1), :]
            a = emb[:, k].reshape(steps, D) + to
            at[:, k] = a.reshape(CHAIN, frames, D)
            br[:, k] = (ln(a)[0] * gain[pl.ds(GAIN_BAND, 1), :]).astype(BF).reshape(CHAIN, frames, D)


def band_forward_kernel(
    steps, chunk, table, keep, rows_in, cores, bias, scale, p,
    bo, xs, w, h0, hk0, cf0, h1, hk1, cf1,
    gates, hk_s, ck_s, hall,
):
    n = steps // chunk
    j = pl.program_id(0)
    frames = rows_in.shape[2]

    @pl.when(j == 0)
    def _():
        for way in range(2):
            for q in range(CHAIN):
                for core in range(2):
                    at = (2 * q + core) * HALF
                    w[way, at : at + HALF, :] = cores[q, core, way]
        for q in range(CHAIN):
            for k in range(SLOTS):
                if table[q][k] >= 0:
                    xs[pl.ds(table[q][k] * frames, frames), :] = rows_in[q, k]
        xs[pl.ds(BANDS * frames, (steps - BANDS) * frames), :] = jnp.zeros(
            ((steps - BANDS) * frames, D), BF
        )

    forward_chunk(
        keep, xs, w, bias, scale, BIAS_LSTM + 2 * G4 // D, (h0, hk0, cf0, h1, hk1, cf1), gates, hk_s, ck_s, steps, chunk, frames, 2, hall
    )

    @pl.when(j == n - 1)
    def _():
        for q in range(CHAIN):
            for k in range(SLOTS):
                here = pl.ds(max(table[q][k], 0) * frames, frames)
                bo[q, k] = (mm(hall[0, here, :], p[:H]) + mm(hall[1, here, :], p[H:])).astype(BF)


def mask_kernel(
    bands, meta, at, bo, cot, um, dm, gain, bias,
    mask, abg, abl, kept, sent, early,
):
    frames = at.shape[2]
    rows = CHAIN * frames

    both = range(PAIR)
    found = [band_at(meta, bands, pl.program_id(0) * PAIR + i) for i in both]

    @pl.when(pl.program_id(0) == 0)
    def _():
        early[...] = jnp.zeros_like(early)

    def halves(i, v, first):
        half = v.shape[1] // 2
        lower = meta[0] == 0
        near = jnp.where(lower, v[:, :half], v[:, half:]).astype(BF)
        far = jnp.where(lower, v[:, half:], v[:, :half]).astype(BF)
        many = v.shape[0]
        for c in range(half // D):
            kept[i, first + c * many : first + (c + 1) * many, :] = near[:, c * D : (c + 1) * D]
            sent[i, first + c * many : first + (c + 1) * many, :] = far[:, c * D : (c + 1) * D]

    pb = bias[pl.ds(BIAS_PROJ + 1, 1), :]
    normed = [
        ln(at[:, i].reshape(rows, D) + (bo[:, i].reshape(rows, D).astype(F32) + pb)) for i in both
    ]
    mg = [gain[pl.ds(GAIN_MASK + found[i][0], 1), :] for i in both]
    mi = [(normed[i][0] * mg[i]).astype(BF) for i in both]
    act_f = [jnp.tanh(mm(mi[i], um[i]) + wide_row(bias, BIAS_UP + 4 * found[i][0], 4)) for i in both]
    act = [v.astype(BF) for v in act_f]
    pre = [mm(act[i], dm[i]) + wide_row(bias, BIAS_DOWN + 2 * found[i][0], 2) for i in both]
    og = []
    for i in both:
        value = pre[i][:, :SUBF]
        gate = 0.5 * jnp.tanh(0.5 * pre[i][:, SUBF:]) + 0.5
        mask[:, i] = (value * gate).astype(BF).reshape(CHAIN, frames, SUBF)
        cg = cot[:, i].reshape(rows, D).astype(F32) * found[i][1].astype(F32) * gate
        og.append(jnp.concatenate([cg.astype(BF), (cg * value * (1.0 - gate)).astype(BF)], axis=-1))
    pg = [(mm_nt(og[i], dm[i]) * (1.0 - act_f[i] * act_f[i])).astype(BF) for i in both]
    dy = [mm_nt(pg[i], um[i]) for i in both]
    low = []
    for i in both:
        halves(i, mm_tn(act[i], og[i]), UP_PART)
        halves(i, mm_tn(mi[i], pg[i]), 0)
        grad = ln_back(*normed[i], mg[i], dy[i])
        abg[:, i] = grad.reshape(CHAIN, frames, D)
        low.append(grad.astype(BF))
        abl[:, i] = low[i].reshape(CHAIN, frames, D)
    sums = [
        [rowsum(v) for v in (dy[i] * normed[i][0], low[i].astype(F32), pg[i].astype(F32), og[i].astype(F32))]
        for i in both
    ]
    for i in both:
        dmg, dpb, dub, ddb = sums[i]
        band = found[i][0]

        @pl.when(found[i][1])
        def _():
            early[pl.ds(band, 1), :] = dmg
            early[pl.ds(EARLY_BIAS, 1), :] = early[pl.ds(EARLY_BIAS, 1), :] + dpb
            for c in range(4):
                row = EARLY_BIAS + BIAS_UP - BIAS_PROJ - 1 + 4 * band + c
                early[pl.ds(row, 1), :] = dub[:, c * D : (c + 1) * D]
            for c in range(2):
                row = EARLY_BIAS + BIAS_DOWN - BIAS_PROJ - 1 + 2 * band + c
                early[pl.ds(row, 1), :] = ddb[:, c * D : (c + 1) * D]


def band_backward_kernel(
    steps, chunk, table, keep, meta, scale, ol_in, xs, w, p, mask_k, mask_f, h0, hk0, cf0, h1, hk1, cf1,
    keep_w, send_w, keep_p, send_p, bias_rows, rows_out, mask_sum,
    ol, wt, pt, da, sh, rg, ch_s, cc_s, dw, dp, db,
):
    n = steps // chunk
    j = pl.program_id(0)
    frames = ol_in.shape[2]
    mask_sum[...] = mask_k[...] + mask_f[...]

    @pl.when(j == 0)
    def _():
        for q in range(CHAIN):
            for k in range(SLOTS):
                if table[q][k] >= 0:
                    ol[pl.ds(table[q][k] * frames, frames), :] = ol_in[q, k]
        ol[pl.ds(BANDS * frames, (steps - BANDS) * frames), :] = jnp.zeros(
            ((steps - BANDS) * frames, D), BF
        )

    backward_chunk(
        keep, xs, ol, w, p, (h0, hk0, cf0, h1, hk1, cf1), dw, dp, db,
        wt, pt, da, sh, rg, ch_s, cc_s, steps, chunk, frames, 2,
    )

    @pl.when(j == n - 1)
    def _():
        part_totals(
            meta[0], dw, dp, scale,
            lambda other, q, way: ((keep_w, send_w)[other], (q * 2 + way) * LSTM_PART),
            lambda other, q, way: ((keep_p, send_p)[other], (q * 2 + way) * HALF_P),
        )
        bias_total(db, scale, bias_rows, 0)
        for q in range(CHAIN):
            for k in range(SLOTS):
                if table[q][k] >= 0:
                    rows_out[q, k] = rg[pl.ds(table[q][k] * frames, frames), :].astype(BF)
                else:
                    rows_out[q, k] = jnp.zeros((frames, D), BF)


def time_backward_kernel(
    steps, chunk, keep, bands, meta, scale, bgrad, abg, at, emb, sp, sm, gain, bias_b, keep_b, send_b, early, mask, xs, w, p, h0, hk0, cf0, h1, hk1, cf1,
    keep_m, send_m, leaving,
    ol, wt, pt, da, sh, rg, ch_s, cc_s, dw, dp, db, xt, atg, late, dsm,
):
    n = steps // chunk
    j = pl.program_id(0)
    frames = bgrad.shape[2]

    @pl.when(j == 0)
    def _():
        xt[...] = jnp.zeros_like(xt)
        late[...] = jnp.zeros_like(late)
        dbg = jnp.zeros((1, D), F32)
        dpb = jnp.zeros((1, D), F32)
        for k in range(SLOTS):
            norm, r = ln(at[:, k].reshape(steps, D))
            dy = bgrad[:, k].reshape(steps, D).astype(F32)
            dbg = dbg + rowsum(dy * norm)
            a = abg[:, k].reshape(steps, D) + ln_back(norm, r, gain[pl.ds(GAIN_BAND, 1), :], dy)
            atg[k] = a
            low = a.astype(BF).astype(F32)
            dpb = dpb + rowsum(low)
            xt[pl.ds(k, steps, stride=ROWS_T), :] = low
        ol[...] = xt[...].astype(BF)
        leaving[:, :SLOTS] = mask[...]
        late[pl.ds(GAIN_BAND, 1), :] = dbg
        late[pl.ds(LATE_BIAS + BIAS_PROJ, 1), :] = dpb
        late[pl.ds(LATE_BIAS + BIAS_LSTM + 2 * G4 // D, 2 * G4 // D), :] = bias_b[...]

    backward_chunk(
        keep, xs, ol, w, p, (h0, hk0, cf0, h1, hk1, cf1), dw, dp, db,
        wt, pt, da, sh, rg, ch_s, cc_s, steps, chunk, ROWS_T, 16,
    )

    @pl.when(j == n - 1)
    def _():
        outs = (keep_m, send_m)
        part_totals(
            meta[0], dw, dp, scale,
            lambda other, q, way: (outs[other], (q * 2 + way) * SHARD_PART),
            lambda other, q, way: (outs[other], (q * 2 + way) * SHARD_PART + LSTM_PART),
        )
        bias_total(db, scale, late, LATE_BIAS + BIAS_LSTM)
        dtg = jnp.zeros((1, D), F32)
        for k in range(SLOTS):
            dy = rg[pl.ds(k, steps, stride=ROWS_T), :]
            norm, r = ln(emb[:, k].reshape(steps, D))
            dtg = dtg + rowsum(dy * norm)
            el = (atg[k] + ln_back(norm, r, gain[pl.ds(GAIN_TIME, 1), :], dy)).astype(BF)
            dsb = rowsum(el.astype(F32))
            band, filled = band_at(meta, bands, k)
            own = gain[pl.ds(band, 1), :]
            norm, r = ln(sp[:, k].reshape(steps, D).astype(F32))
            dsm[k] = mm_tn((norm * own).astype(BF), el).astype(BF)
            dy = mm_nt(el, sm[k])
            dsg = rowsum(dy * norm)

            @pl.when(filled)
            def _():
                late[pl.ds(band, 1), :] = dsg
                late[pl.ds(LATE_BIAS + band, 1), :] = dsb

            leaving[:, SLOTS + k] = ln_back(norm, r, own, dy).astype(BF).reshape(CHAIN, frames, D)
        late[pl.ds(GAIN_TIME, 1), :] = dtg
        for out, band_part in ((keep_m, keep_b), (send_m, send_b)):
            for i in range(2 * CHAIN):
                row = (i + 1) * SHARD_PART - HALF_P
                out[row : row + HALF_P, :] = band_part[i * HALF_P : (i + 1) * HALF_P, :]
            out[pl.ds(MISC_EARLY, EARLY_ROWS), :] = early[...].astype(BF)
            out[pl.ds(MISC_SPLIT, SLOTS * SUBF), :] = dsm[...].reshape(SLOTS * SUBF, D)
            out[pl.ds(MISC_LATE, LATE_ROWS), :] = late[...].astype(BF)


def assemble_kernel(table, leaving, mask, grad):
    for q in range(CHAIN):
        for k in range(SLOTS):
            if table[q][k] >= 0:
                mask[table[q][k]] = leaving[q, k]
                at = pl.ds(table[q][k], leaving.shape[2], stride=BANDS)
                grad[at, :] = leaving[q, SLOTS + k].astype(F32)


def columns_kernel(meta, own, far, up, down, over, up_s, down_s):
    many = own.shape[0]
    fill = meta[2]
    lower = meta[0] == 0
    up_s[...] = jnp.zeros_like(up_s)
    down_s[...] = jnp.zeros_like(down_s)
    for i in range(many):
        for core in range(2):
            part = jnp.where(lower == (core == 0), own[i].astype(F32), far[i].astype(F32))
            for c in range(UP_PART // D):
                at = (core * (UP_PART // D) + c) * D
                up_s[FILL + i * D : FILL + (i + 1) * D, at : at + D] = part[c * D : (c + 1) * D, :]
            down_s[4 * (FILL + i * D) : 4 * (FILL + (i + 1) * D), core * D : (core + 1) * D] = part[UP_PART:, :]
    row = 0
    for scratch, out, unit in ((up_s, up, 1), (down_s, down, 4)):
        rows, wide = out.shape
        at = pl.multiple_of((FILL - fill) * unit, 8)
        out[...] = scratch[pl.ds(at, rows), :]
        past = scratch[pl.ds(pl.multiple_of(at + rows, 8), FILL * unit), :].astype(BF)
        for c in range(wide // D):
            over[row : row + FILL * unit, :] = past[:, c * D : (c + 1) * D]
            row += FILL * unit


def totals_kernel(
    meta, up, down, before, split, split_before, near, far, _,
    lstm_t, proj_t, split_t, up_t, down_t, square, split_s,
):
    fill = meta[2]
    lower = meta[0] == 0
    for core in range(2):
        part = jnp.where(lower == (core == 0), near[...].astype(F32), far[...].astype(F32))
        for c in range(G4 // D):
            lstm_t[core * HALF : (core + 1) * HALF, c * D : (c + 1) * D] = part[c * HALF : (c + 1) * HALF, :]
        proj_t[core * HALF_P : (core + 1) * HALF_P, :] = part[LSTM_PART:, :]
    split_s[...] = jnp.zeros_like(split_s)
    split_s[FILL : FILL + split.shape[0], :] = split[...].astype(F32)
    split_t[...] = split_s[pl.ds(pl.multiple_of(FILL - fill, 8), split_t.shape[0]), :]
    up_t[...] = up[...]
    down_t[...] = down[...]
    split_t[:FILL, :] = split_t[:FILL, :] + split_before[...].astype(F32)
    row = 0
    for out, rows in ((up_t, FILL), (down_t, 4 * FILL)):
        for c in range(out.shape[1] // D):
            at = slice(c * D, (c + 1) * D)
            out[:rows, at] = out[:rows, at] + before[row : row + rows, :].astype(F32)
            row += rows
    total = jnp.zeros((1, D), F32)
    for out in (lstm_t, proj_t, split_t, up_t, down_t):
        line = rowsum(out[...] * out[...])
        for c in range(line.shape[1] // D):
            total = total + line[:, c * D : (c + 1) * D]
    square[...] = jnp.broadcast_to(jnp.sum(total, axis=-1, keepdims=True), (8, D))


def plain_call(kernel, outs, scratch, name, meta, *arrays):
    specs = [ANY if v.ndim == 4 else pl.BlockSpec(memory_space=pltpu.VMEM) for v in arrays]
    return pl.pallas_call(
        kernel,
        in_specs=([] if meta is None else [SMEM]) + specs,
        out_specs=[pl.BlockSpec(memory_space=pltpu.VMEM)] * len(outs),
        out_shape=outs,
        scratch_shapes=[pltpu.VMEM(shape, F32) for shape in scratch],
        compiler_params=pltpu.CompilerParams(vmem_limit_bytes=VMEM),
        cost_estimate=cost(3),
        name=name,
    )(*(() if meta is None else (meta,)), *arrays)


def whole(shape):
    zeros = (0,) * len(shape)
    return pl.BlockSpec(shape, lambda j: zeros)


SMEM = pl.BlockSpec(memory_space=pltpu.SMEM)
ANY = pl.BlockSpec(memory_space=pl.ANY)


def sds(shape, dtype):
    return jax.ShapeDtypeStruct(shape, dtype)


def chunk_specs(n, chunk, rows, flip):
    up = lambda j: (j, 0, 0)
    down = lambda j: (n - 1 - j, 0, 0)
    specs = []
    for way in (down, up) if flip else (up, down):
        specs += [
            pl.BlockSpec((chunk, rows, H), way),
            pl.BlockSpec((chunk, rows, H), way),
            pl.BlockSpec((chunk, rows, 6 * H), way),
        ]
    return specs


def chunk_shapes(steps, rows):
    return [
        sds((steps, rows, H), BF),
        sds((steps, rows, H), BF),
        sds((steps, rows, 6 * H), F32),
    ] * 2


def params():
    return pltpu.CompilerParams(vmem_limit_bytes=VMEM, dimension_semantics=("arbitrary",))


def cost(micros):
    return pl.CostEstimate(flops=micros * 10**9, bytes_accessed=micros * 10**6, transcendentals=0)


def time_forward(table, keep, bands, meta, sp, sm, gain, bias, scale, near, far, p, cot):
    frames = sp.shape[2]
    steps, chunk = CHAIN * frames, 32
    n = steps // chunk
    slab = (CHAIN, SLOTS, frames, D)
    return pl.pallas_call(
        functools.partial(time_forward_kernel, steps, chunk, table),
        grid=(n,),
        in_specs=[SMEM, SMEM, SMEM]
        + [whole(v.shape) for v in (sp, sm, gain, bias, scale, near, far, p, cot)],
        out_specs=[whole(slab)] * 3
        + [whole((steps * ROWS_T, D)), whole((2, D + H, G4)), whole(slab)]
        + chunk_specs(n, chunk, ROWS_T, False),
        out_shape=[sds(slab, F32), sds(slab, F32), sds(slab, BF), sds((steps * ROWS_T, D), BF), sds((2, D + H, G4), BF), sds(slab, BF)]
        + chunk_shapes(steps, ROWS_T),
        scratch_shapes=[
            pltpu.VMEM((2, chunk * ROWS_T, G4), F32),
            pltpu.VMEM((2, ROWS_T, H), BF),
            pltpu.VMEM((2, ROWS_T, H), F32),
            pltpu.VMEM((steps * ROWS_T, D), F32),
            pltpu.VMEM((2, steps * ROWS_T, H), BF),
        ],
        compiler_params=params(),
        cost_estimate=cost(66),
        name="time_forward",
    )(keep, bands, meta, sp, sm, gain, bias, scale, near, far, p, cot)


def band_forward(table, keep, rows_in, cores, bias, scale, p):
    frames = rows_in.shape[2]
    steps, chunk = STEPS_B, 14
    n = steps // chunk
    slab = (CHAIN, SLOTS, frames, D)
    return pl.pallas_call(
        functools.partial(band_forward_kernel, steps, chunk, table),
        grid=(n,),
        in_specs=[SMEM, whole(slab)] + [whole(v.shape) for v in (cores, bias, scale, p)],
        out_specs=[whole(slab), whole((steps * frames, D)), whole((2, D + H, G4))] + chunk_specs(n, chunk, frames, False),
        out_shape=[sds(slab, BF), sds((steps * frames, D), BF), sds((2, D + H, G4), BF)] + chunk_shapes(steps, frames),
        scratch_shapes=[
            pltpu.VMEM((2, chunk * frames, G4), F32),
            pltpu.VMEM((2, frames, H), BF),
            pltpu.VMEM((2, frames, H), F32),
            pltpu.VMEM((2, steps * frames, H), BF),
        ],
        compiler_params=params(),
        cost_estimate=cost(27),
        name="band_forward",
    )(keep, rows_in, cores, bias, scale, p)


def mask_stage(bands, meta, at, bo, cot, um, dm, gain, bias):
    frames = at.shape[2]
    slab = (CHAIN, SLOTS, frames, D)
    part = pl.BlockSpec((CHAIN, PAIR, frames, D), lambda k: (0, k, 0, 0))

    def band(*shape):
        return pl.BlockSpec((PAIR,) + shape, lambda k: (k, 0, 0))

    return pl.pallas_call(
        mask_kernel,
        grid=(SLOTS // PAIR,),
        in_specs=[
            SMEM, SMEM, part, part, part, band(D, 4 * D), band(4 * D, 2 * SUBF),
            whole(gain.shape), whole(bias.shape),
        ],
        out_specs=[
            part, part, part, band(MASK_PART, D), band(MASK_PART, D),
            whole((EARLY_ROWS, D)),
        ],
        out_shape=[
            sds(slab, BF), sds(slab, F32), sds(slab, BF),
            sds((SLOTS, MASK_PART, D), BF), sds((SLOTS, MASK_PART, D), BF),
            sds((EARLY_ROWS, D), F32),
        ],
        compiler_params=params(),
        cost_estimate=cost(16),
        name="mask_stage",
    )(bands, meta, at, bo, cot, um, dm, gain, bias)


def backward_scratch(steps, chunk, rows):
    span = chunk * rows
    return [
        pltpu.VMEM((steps * rows, D), BF),
        pltpu.VMEM((2, G4, D + H), BF),
        pltpu.VMEM((2, D, H), BF),
        pltpu.VMEM((2, span, G4), BF),
        pltpu.VMEM((2, span, H), BF),
        pltpu.VMEM((steps * rows, D), F32),
        pltpu.VMEM((2, rows, H), F32),
        pltpu.VMEM((2, rows, H), F32),
        pltpu.VMEM((2, D + H, G4), F32),
        pltpu.VMEM((2 * H, D), F32),
        pltpu.VMEM((2, 8, G4), F32),
    ]


def total_shapes():
    return [sds((2 * CHAIN * LSTM_PART, D), BF)] * 2 + [sds((PROJ_PART, D), BF)] * 2


def band_backward(table, keep, meta, scale, ol_in, xs, w, p, mask_k, mask_f, saved):
    frames = ol_in.shape[2]
    steps, chunk = STEPS_B, 14
    n = steps // chunk
    slab = (CHAIN, SLOTS, frames, D)
    third = pl.BlockSpec((SLOTS // n, MASK_PART, D), lambda j: (j, 0, 0))
    return pl.pallas_call(
        functools.partial(band_backward_kernel, steps, chunk, table),
        grid=(n,),
        in_specs=[SMEM, SMEM]
        + [whole(v.shape) for v in (scale, ol_in, xs, w, p)]
        + [third, third]
        + chunk_specs(n, chunk, frames, True),
        out_specs=[whole(v.shape) for v in total_shapes()] + [whole((2 * G4 // D, D)), whole(slab), third],
        out_shape=total_shapes() + [sds((2 * G4 // D, D), F32), sds(slab, BF), sds(mask_k.shape, BF)],
        scratch_shapes=backward_scratch(steps, chunk, frames),
        compiler_params=params(),
        cost_estimate=cost(32),
        name="band_backward",
    )(keep, meta, scale, ol_in, xs, w, p, mask_k, mask_f, *saved)


def time_backward(keep, bands, meta, scale, bgrad, abg, at, emb, sp, sm, gain, bias_b, keep_b, send_b, early, mask, xs, w, p, saved):
    frames = bgrad.shape[2]
    steps, chunk = CHAIN * frames, 32
    n = steps // chunk
    slab = (CHAIN, SLOTS, frames, D)
    outs = [sds((MISC, D), BF)] * 2 + [sds((CHAIN, 2 * SLOTS, frames, D), BF)]
    return pl.pallas_call(
        functools.partial(time_backward_kernel, steps, chunk),
        grid=(n,),
        in_specs=[SMEM, SMEM, SMEM]
        + [whole(v.shape) for v in (scale, bgrad, abg, at, emb, sp, sm, gain, bias_b, keep_b, send_b, early, mask, xs, w, p)]
        + chunk_specs(n, chunk, ROWS_T, True),
        out_specs=[whole(v.shape) for v in outs],
        out_shape=outs,
        scratch_shapes=backward_scratch(steps, chunk, ROWS_T)
        + [pltpu.VMEM((steps * ROWS_T, D), F32), pltpu.VMEM((SLOTS, steps, D), F32)]
        + [pltpu.VMEM((LATE_ROWS, D), F32), pltpu.VMEM((SLOTS, SUBF, D), BF)],
        compiler_params=params(),
        cost_estimate=cost(96),
        name="time_backward",
    )(keep, bands, meta, scale, bgrad, abg, at, emb, sp, sm, gain, bias_b, keep_b, send_b, early, mask, xs, w, p, *saved)


def chain_groups():
    many = lax.axis_size("rows") // CHAIN
    return [[CHAIN * g + q for q in range(CHAIN)] for g in range(many)]


def place_groups():
    many = lax.axis_size("rows") // CHAIN
    return [[CHAIN * g + q for g in range(many)] for q in range(CHAIN)]


def across(v, groups, axis=0):
    return lax.all_to_all(v, "rows", axis, axis, axis_index_groups=groups, tiled=True)


def spread(v, groups):
    return across(jnp.broadcast_to(v[None], (len(groups[0]),) + v.shape), groups)


def swap_dir(v):
    return lax.ppermute(v, "dir", [(0, 1), (1, 0)])


def ordered(side, near, far):
    return jnp.where(side == 0, jnp.stack([near, far]), jnp.stack([far, near]))


def to_bands(v, more=None):
    v = jnp.concatenate([v, v[:1]])
    parts = []
    for blocks in band_blocks(lax.axis_size("rows")):
        cuts = [v[first : first + places] for first, places, _ in blocks]
        parts.append(jnp.concatenate(cuts + ([] if more is None else [more])))
    return jnp.stack(parts)


def my_bit(bit):
    return (lax.axis_index("rows") >> bit) & 1


def swap_bit(v, bit):
    return lax.ppermute(v, "rows", [(r, r ^ (1 << bit)) for r in range(lax.axis_size("rows"))])


def double(v, bit):
    return ordered(my_bit(bit), v, swap_bit(v, bit))


def halve(v, bit, axis):
    mine = my_bit(bit)
    kept = lax.dynamic_index_in_dim(v, mine, axis, False)
    return kept + swap_bit(lax.dynamic_index_in_dim(v, 1 - mine, axis, False), bit)


def my_rows(values):
    return jnp.asarray(np.array(values, np.int32))[lax.axis_index("rows")]


def fills(rows):
    return [shard_start(s, rows) * D - s * BANDS * D // rows for s in range(rows)]


def tied(v, *others):
    for other in others:
        one = lax.slice(other, (0,) * other.ndim, (1,) * other.ndim).reshape(())
        v = jnp.where(jnp.isnan(one), jnp.zeros_like(v), v)
    return v


def rows_after(shard):
    rows = lax.axis_size("rows")
    head = FILL * (shard.shape[0] * rows // (BANDS * D))
    if not square_slice():
        return shard[:1]
    return lax.ppermute(shard[:head].astype(BF), "rows", [(r + 1, r) for r in range(rows - 1)])


def whole_bands(shard, after):
    rows = lax.axis_size("rows")
    unit = shard.shape[0] * rows // (BANDS * D)
    head = FILL * unit
    spare = jnp.zeros((head,) + shard.shape[1:], shard.dtype)
    long = jnp.concatenate([shard, after, spare])
    return lax.dynamic_slice_in_dim(long, my_rows(fills(rows)) * unit, SLOTS // CHAIN * D * unit, 0)


def past_shard(own, unit):
    rows = lax.axis_size("rows")
    fill = my_rows(fills(rows)) * unit
    head = jnp.zeros((FILL * unit,) + own.shape[1:], own.dtype)
    many = BANDS * D * unit // rows
    over = lax.dynamic_slice_in_dim(jnp.concatenate([own, head]), many - fill, FILL * unit, 0)
    return lax.ppermute(over, "rows", [(r, r + 1) for r in range(rows - 1)])


def to_shard(own, before, unit):
    rows = lax.axis_size("rows")
    fill = my_rows(fills(rows)) * unit
    many = BANDS * D * unit // rows
    head = jnp.zeros((FILL * unit,) + own.shape[1:], own.dtype)
    moved = lax.dynamic_slice_in_dim(jnp.concatenate([head, own]), FILL * unit - fill, many, 0)
    before = jnp.concatenate([before, jnp.zeros((many - FILL * unit,) + own.shape[1:], own.dtype)])
    row = lax.broadcasted_iota(jnp.int32, (many, 1), 0)
    return jnp.where(row < fill, before, moved)


def square_slice():
    return lax.axis_size("rows") == CHAIN * CHAIN


def pick_bands(wide):
    blocks = band_blocks(lax.axis_size("rows"))
    place = lax.axis_index("rows") % CHAIN
    wide = jnp.concatenate([wide, wide[:1]])
    cuts = []
    for at in range(len(blocks[0])):
        first = jnp.asarray(np.array([b[at][0] for b in blocks], np.int32))[place]
        cuts.append(lax.dynamic_slice_in_dim(wide, first, blocks[0][at][1], 0))
    return jnp.concatenate(cuts)


def place_bands(part, valid):
    blocks = band_blocks(lax.axis_size("rows"))
    place = lax.axis_index("rows") % CHAIN
    part = part * valid[:, None]
    total = jnp.zeros((BANDS + 1, part.shape[1]), F32)
    row = 0
    for at in range(len(blocks[0])):
        first = jnp.asarray(np.array([b[at][0] for b in blocks], np.int32))[place]
        cut = part[row : row + blocks[0][at][1]]
        total = lax.dynamic_update_slice_in_dim(total, cut, first, 0)
        row += blocks[0][at][1]
    return total[:BANDS]


def band_weights(shard, after, gate):
    rows = lax.axis_size("rows")
    unit = shard.shape[0] * rows // BANDS
    low = shard.astype(BF)
    if not square_slice():
        full = lax.all_gather(low, "rows", axis=0, tiled=True).reshape(BANDS, unit, -1)
        return pick_bands(full)
    own = whole_bands(low, after)
    own = tied(own, gate)
    own = lax.all_gather(own, "rows", axis=0, axis_index_groups=place_groups(), tiled=True)
    return own.reshape(SLOTS, unit, -1)


def band_sums(grads, apart):
    if not square_slice():
        return grads
    if not apart:
        return halve(halve(grads.reshape(2, 2, SLOTS // CHAIN, *grads.shape[1:]), 2, 1), 3, 0)
    return lax.psum_scatter(
        grads, "rows", scatter_dimension=0, axis_index_groups=place_groups(), tiled=True
    )


def shard_parts(own, unit):
    if not square_slice():
        return own, own
    own = own.reshape(SLOTS // CHAIN * unit, -1)
    return own, past_shard(own, unit // D)


def shard_sums(parts, unit, valid):
    own, before = parts
    if square_slice():
        return to_shard(own, before, unit // D).astype(F32)
    flat = place_bands(own.reshape(SLOTS, -1).astype(F32), valid).astype(BF)
    flat = flat.reshape(BANDS * unit, -1)
    return lax.psum_scatter(flat, "rows", scatter_dimension=0, tiled=True).astype(F32)


def both_cores(kept, sent):
    return kept + swap_dir(sent)


def mask_columns(side, own, far):
    pair = ordered(side, own, far)
    many = own.shape[0]
    up = pair[:, :, :UP_PART].reshape(2, many, UP_PART // D, D, D)
    up = jnp.transpose(up, (1, 3, 0, 2, 4)).reshape(many, D, 4 * D)
    down = jnp.transpose(pair[:, :, UP_PART:], (1, 2, 0, 3)).reshape(many, 4 * D, 2 * SUBF)
    return up, down


def sum_rows(v, bits, wire=F32):
    for bit in bits:
        v = v.astype(wire)
        v = v.astype(F32) + swap_bit(v, bit).astype(F32)
    return v


def gather_first(side, lstm_low, proj_low, split_weight, sp_parts, up_after, down_after):
    if not square_slice():
        lstm = lax.all_gather(lstm_low, "rows", axis=0, tiled=True)
        proj = lax.all_gather(proj_low, "rows", axis=0, tiled=True).reshape(2, 2 * H, D)
        cut = jnp.transpose(lstm.reshape(2, 2, CHAIN, 2, HALF, G4), (0, 3, 2, 1, 4, 5))
        sp = across(sp_parts, chain_groups())
        near = lax.dynamic_index_in_dim(cut[0], side, 0, False)
        far = lax.dynamic_index_in_dim(cut[0], 1 - side, 0, False)
        return near, far, jnp.swapaxes(cut[1], 0, 1), proj, band_weights(split_weight, None, None), sp
    flat = HALF_P * D // G4
    packed = jnp.concatenate(
        [
            lax.dynamic_slice_in_dim(lstm_low, side * HALF, HALF, 0),
            lax.dynamic_slice_in_dim(proj_low, side * HALF_P, HALF_P, 0).reshape(flat, G4),
        ]
    )
    split = whole_bands(split_weight.astype(BF), rows_after(split_weight))
    column = double(packed, 3)
    sp = across(tied(sp_parts, column), chain_groups())
    column = double(tied(column, split), 2)
    split = double(split, 3)
    time = jnp.concatenate([column[:, 0], column[:, 1, HALF:]], axis=1)
    band = column[:, 1, :HALF]
    time = tied(time, split)
    split = double(split, 2)
    time = double(time, 0)
    time = double(tied(time, split, sp, up_after, down_after), 1)
    split = jnp.swapaxes(split, 0, 1).reshape(SLOTS, SUBF, D)
    near = time.reshape(CHAIN, 2, HALF + 2 * flat, G4)
    far = swap_dir(near)
    band = ordered(side, band, swap_dir(band))
    band = spread(tied(band, near), chain_groups())
    proj = ordered(side, near[:, :, HALF:], far[:, :, HALF:]).reshape(2, CHAIN, 2, 2, flat, G4)
    proj = jnp.transpose(proj, (3, 2, 1, 0, 4, 5)).reshape(2, 2 * H, D)
    return near, far, band, proj, split, sp


def unpacked(pair):
    lead = pair.shape[:-3]
    v = jnp.swapaxes(pair.reshape(*lead, 2, G4 // D, HALF, D), -3, -2)
    return v.reshape(*lead, 2 * HALF, G4)


def traded(parts, bit):
    flat = [v.reshape(-1, D) for v in parts]
    got = swap_bit(jnp.concatenate(flat), bit)
    out, row = [], 0
    for v, rows in zip(parts, flat):
        out.append(got[row : row + rows.shape[0]].reshape(v.shape))
        row += rows.shape[0]
    return out


def cut(v, bit, axis):
    mine = my_bit(bit)
    return (
        lax.dynamic_index_in_dim(v, mine, axis, False),
        lax.dynamic_index_in_dim(v, 1 - mine, axis, False),
    )


def all_totals(side, sums, lstm_b, valid):
    v = sums[:MISC_SPLIT].reshape(CHAIN, 2, SHARD_PART, D)
    split = sums[MISC_SPLIT:MISC_LATE]
    small = sums[MISC_LATE:].astype(F32)
    if not square_slice():
        bits = range((lax.axis_size("rows") - 1).bit_length())
        band = lstm_b.reshape(CHAIN, 2, LSTM_PART, D)
        lstm = jnp.stack([v[:, :, :LSTM_PART], band])
        lstm = jnp.transpose(ordered(side, lstm, swap_dir(lstm)), (1, 3, 2, 0, 4, 5))
        lstm = unpacked(lstm).reshape(-1, G4)
        proj = v[:, :, LSTM_PART:].reshape(CHAIN, 2, 2, HALF_P, D)
        proj = jnp.transpose(ordered(side, proj, swap_dir(proj)), (3, 2, 1, 0, 4, 5)).reshape(-1, D)
        lstm, proj = (
            lax.psum_scatter(t, "rows", scatter_dimension=0, tiled=True).astype(F32) for t in (lstm, proj)
        )
        split = shard_sums((split.reshape(SLOTS, SUBF, D), None), SUBF, valid)
        return lstm, proj, split, sum_rows(small, bits, BF), small
    kept, sent = cut(v.reshape(2, 2, 2, SHARD_PART, D), 0, 1)
    got, more = traded([sent, small.astype(BF)], 0)
    v, small = kept + got, small.astype(BF).astype(F32) + more.astype(F32)
    kept, sent = cut(v, 1, 0)
    got, more = traded([sent, small.astype(BF)], 1)
    v, small = kept + got, small.astype(BF).astype(F32) + more.astype(F32)
    late = v
    time_rows = LSTM_PART + HALF_P
    band = jnp.concatenate([lstm_b.reshape(2, LSTM_PART, D), v[:, time_rows:]], axis=1)
    v = jnp.stack([v[:, :time_rows], band])
    split = split.reshape(2, 2, SLOTS // CHAIN * SUBF, D)
    for bit, axis in ((2, 1), (3, 0)):
        kept, sent = cut(v, bit, axis)
        kept_s, sent_s = cut(split, bit, axis)
        got, got_s, more = traded([sent, sent_s, small.astype(BF)], bit)
        v, split = kept + got, kept_s + got_s
        small = small.astype(BF).astype(F32) + more.astype(F32)
    return v, split, small, late


def finish_kernel(*refs):
    square, small = refs[:2]
    totals = refs[2:7]
    olds = refs[7:28]
    norm_out = refs[28]
    outs = refs[29:]
    gain_rows = [(0, LATE_BIAS, 0), (LATE_ROWS, EARLY_BIAS, LATE_BIAS)]
    bias_rows = [(LATE_BIAS, LATE - LATE_BIAS, 0), (LATE_ROWS + EARLY_BIAS, EARLY - EARLY_BIAS, LATE - LATE_BIAS)]
    line = rowsum(small[...] * small[...])
    norm = jnp.sqrt(square[:1, :1] + jnp.sum(line, axis=-1, keepdims=True))
    norm_out[...] = norm
    clip = jnp.minimum(1.0, CLIP_NORM / (norm + 1e-06))

    def put(index, at, gradient, rate):
        velocity, weight, average = olds[3 * index : 3 * index + 3]
        clipped = gradient * clip
        velocity_new = MOMENTUM * velocity[at, :] + clipped
        weight_new = weight[at, :] - rate * (clipped + MOMENTUM * velocity_new)
        results = (clipped, velocity_new, weight_new, AVERAGE * average[at, :] + (1.0 - AVERAGE) * weight_new)
        for out, value in zip(outs[4 * index : 4 * index + 4], results):
            out[at, :] = value

    for index in range(5):
        rows = totals[index].shape[0]
        put(index, slice(0, rows), totals[index][...], LEARN_RATE)
    for index, pieces in ((5, gain_rows), (6, bias_rows)):
        for first, many, at in pieces:
            put(index, slice(at, at + many), small[first : first + many, :], GAIN_RATE)


def finish(square, small, totals, olds):
    arrays = (square, small) + totals + olds
    outs = [sds((1, 1), F32)]
    for old in olds[::3]:
        outs += [sds(old.shape, F32)] * 4
    return pl.pallas_call(
        finish_kernel,
        grid=(1,),
        in_specs=[whole(v.shape) for v in arrays],
        out_specs=[whole(v.shape) for v in outs],
        out_shape=outs,
        compiler_params=params(),
        cost_estimate=cost(8),
        name="finish",
    )(*arrays)


def halved_columns():
    scale = np.full((1, G4), 0.5, np.float32)
    scale[:, 2 * H : 3 * H] = 1.0
    return jnp.asarray(scale)


def on_device(
    spectra,
    mask_grad,
    clip_starts,
    split_weight,
    split_velocity,
    split_average,
    lstm_weight,
    lstm_velocity,
    lstm_average,
    proj_weight,
    proj_velocity,
    proj_average,
    up_weight,
    up_velocity,
    up_average,
    down_weight,
    down_velocity,
    down_average,
    gain_weight,
    gain_velocity,
    gain_average,
    bias_weight,
    bias_velocity,
    bias_average,
):
    side = lax.axis_index("dir")
    row = lax.axis_index("rows")
    place = row % CHAIN
    rows = lax.axis_size("rows")
    bits = range((rows - 1).bit_length())
    frames = spectra.shape[1]
    steps = CHAIN * frames
    scale = halved_columns()
    fill = my_rows(fills(rows)) if square_slice() else place
    meta = jnp.stack([side, place, fill]).astype(jnp.int32)
    table = band_table(rows)
    valid = jnp.asarray((np.array(table) >= 0).astype(np.float32))[place]
    bands = jnp.asarray(np.array(table, np.int32).reshape(-1))

    flags = lax.dynamic_index_in_dim(clip_starts[0], side, 1, False).astype(BF)
    flag_slab = jnp.broadcast_to(flags[:, None], (frames, SUBF))
    sp_parts = to_bands(jnp.transpose(spectra[0, :, 0], (1, 0, 2)), flag_slab[None])
    up_after, down_after = rows_after(up_weight), rows_after(down_weight)
    near, far, band_w, proj, split_mat, sp = gather_first(
        side, (lstm_weight * scale).astype(BF), proj_weight.astype(BF), split_weight, sp_parts, up_after, down_after
    )
    starts = sp[:, SLOTS, :, 0].reshape(steps).astype(F32)
    keep_time = jnp.concatenate([1.0 - starts, 1.0 - starts[1:], jnp.ones((1,), F32)])
    keep_np = np.ones((2 * STEPS_B,), np.float32)
    keep_np[STEPS_B + BANDS - 1] = 0.0
    keep_band = jnp.asarray(keep_np)

    up_mat = band_weights(up_weight, up_after, near)
    down_mat = band_weights(down_weight, down_after, near)

    emb, after_time, band_rows, xs_t, w_time, cot_parts, *saved_t = time_forward(
        table, keep_time, bands, meta, sp, split_mat, gain_weight, bias_weight, scale, near, far, proj[0],
        jnp.transpose(mask_grad[0, :, 0], (1, 0, 2)),
    )
    band_out, xs_b, w_band, *saved_b = band_forward(
        table, keep_band, across(band_rows, chain_groups()), band_w, bias_weight, scale, proj[1]
    )
    mask, abg, abl, kept, sent, early = mask_stage(
        bands, meta, after_time, across(band_out, chain_groups()), across(cot_parts, chain_groups()),
        up_mat, down_mat, gain_weight, bias_weight,
    )

    ol_in = across(abl, chain_groups())
    keep_w, send_w, keep_b, send_b, bias_b, bgrad, mask_sum = band_backward(
        table, keep_band, meta, scale, ol_in, xs_b, w_band, proj[1], kept, swap_dir(sent), saved_b
    )
    bgrad = across(bgrad, chain_groups())
    lstm_sum = both_cores(tied(keep_w, bgrad), send_w)
    mask_own = band_sums(mask_sum, True)
    lstm_b = lstm_sum
    if square_slice():
        lstm_b = lax.psum_scatter(
            lstm_sum, "rows", scatter_dimension=0, axis_index_groups=chain_groups(), tiled=True
        )
    keep_m, send_m, leaving = time_backward(
        keep_time, bands, meta, scale, bgrad, abg, after_time, emb, sp, split_mat,
        gain_weight, bias_b, keep_b, send_b, early, mask, xs_t, w_time, proj[0], saved_t,
    )
    sums = both_cores(tied(keep_m, lstm_b, mask_own), send_m)
    mask_far = swap_dir(mask_own)
    if square_slice():
        units = BANDS * D // rows
        up_own, down_own, over = plain_call(
            columns_kernel,
            [
                sds((units, 4 * D), F32), sds((4 * units, 2 * SUBF), F32),
                sds((FILL * 4 + 4 * FILL * 2, D), BF),
            ],
            [(5 * D, 4 * D), (20 * D, 2 * SUBF)], "mask_columns", meta, mask_own, mask_far,
        )
        before = lax.ppermute(over, "rows", [(r, r + 1) for r in range(rows - 1)])
        v, split, small, _ = all_totals(side, sums, lstm_b, valid)
        leaving = across(leaving, chain_groups())
        split_before = past_shard(split, 1)
        lstm_total, proj_total, split_total, up_total, down_total, square = plain_call(
            totals_kernel,
            [
                sds(lstm_weight.shape, F32), sds(proj_weight.shape, F32), sds(split_weight.shape, F32),
                sds(up_weight.shape, F32), sds(down_weight.shape, F32), sds((8, D), F32),
            ],
            [(5 * D, D)], "totals", meta, up_own, down_own, before, split, split_before,
            v, swap_dir(v), leaving,
        )
    else:
        up_own, down_own = mask_columns(side, mask_own, mask_far)
        lstm_total, proj_total, split_total, small, _ = all_totals(side, sums, lstm_b, valid)
        leaving = across(leaving, chain_groups())
        up_total = shard_sums(shard_parts(up_own, D), D, valid)
        down_total = shard_sums(shard_parts(down_own, 4 * D), 4 * D, valid)
        parts = (split_total, lstm_total, proj_total, up_total, down_total)
        square = jnp.full((8, D), sum(jnp.sum(v * v) for v in parts), F32)
    band_mask, spectra_grad = pl.pallas_call(
        functools.partial(assemble_kernel, table),
        grid=(1,),
        in_specs=[whole(leaving.shape)],
        out_specs=[whole((BANDS, frames, D)), whole((frames * BANDS, D))],
        out_shape=[sds((BANDS, frames, D), BF), sds((frames * BANDS, D), F32)],
        compiler_params=params(),
        cost_estimate=cost(3),
        name="assemble",
    )(leaving)
    band_mask = jnp.transpose(band_mask, (1, 0, 2))[None, :, None]
    spectra_grad = spectra_grad.reshape(1, frames, 1, BANDS, D)
    square = sum_rows(square, bits)
    norm, *results = finish(
        square,
        small,
        (split_total, lstm_total, proj_total, up_total, down_total),
        (
            split_velocity, split_weight, split_average, lstm_velocity, lstm_weight, lstm_average,
            proj_velocity, proj_weight, proj_average, up_velocity, up_weight, up_average,
            down_velocity, down_weight, down_average, gain_velocity, gain_weight, gain_average,
            bias_velocity, bias_weight, bias_average,
        ),
    )
    return (band_mask, spectra_grad, norm.reshape(())) + tuple(results)


def solution(mesh):
    per_row = P("rows", None)
    row_major = P("rows", None, "dir", None, None)
    return jax.shard_map(
        on_device,
        mesh=mesh,
        in_specs=(row_major, row_major, P("rows", None, None)) + (per_row,) * 15 + (P(),) * 6,
        out_specs=(row_major, row_major, P()) + (per_row,) * 20 + (P(),) * 8,
        check_vma=False,
    )
```

```python
import functools

import jax
import jax.numpy as jnp
import numpy as np
from jax import lax
from jax.experimental import pallas as pl
from jax.experimental.pallas import tpu as pltpu
from jax.sharding import PartitionSpec as P

D = 128
H = 256
G4 = 4 * H
BANDS = 41
SUBF = 128
CHAIN = 4
SLOTS = 12
FILL = 128
ROWS_T = 16
STEPS_B = 42
VMEM = 60 << 20
PAIR = 3
HALF = (D + H) // CHAIN // 2
HALF_P = H // CHAIN // 2

EPSILON = 1e-05
MOMENTUM = 0.9
LEARN_RATE = 5.0
GAIN_RATE = 50.0
AVERAGE = 0.5
CLIP_NORM = 5.0


GAIN_TIME, GAIN_BAND, GAIN_MASK = BANDS, BANDS + 1, BANDS + 2
BIAS_LSTM = BANDS
BIAS_PROJ = BIAS_LSTM + 16 * H // D
BIAS_UP = BIAS_PROJ + 2
BIAS_DOWN = BIAS_UP + 4 * BANDS
EARLY_BIAS = BANDS
EARLY = EARLY_BIAS + BIAS_DOWN + 2 * BANDS - BIAS_PROJ - 1
EARLY_ROWS = -(-EARLY // 16) * 16
LATE_BIAS = GAIN_MASK
LATE = LATE_BIAS + BIAS_PROJ + 1
LATE_ROWS = -(-LATE // 16) * 16

BF = jnp.bfloat16
F32 = jnp.float32


def mm(a, b):
    return jnp.dot(a, b, preferred_element_type=F32)


def mm_nt(a, b):
    return lax.dot_general(a, b, (((1,), (1,)), ((), ())), preferred_element_type=F32)


def mm_tn(a, b):
    return lax.dot_general(a, b, (((0,), (0,)), ((), ())), preferred_element_type=F32)


def ln(v):
    c = v - jnp.mean(v, axis=-1, keepdims=True)
    r = lax.rsqrt(jnp.mean(c * c, axis=-1, keepdims=True) + EPSILON)
    return c * r, r


def ln_back(n, r, gain, dy):
    dg = dy * gain
    return r * (
        dg - jnp.mean(dg, axis=-1, keepdims=True) - n * jnp.mean(dg * n, axis=-1, keepdims=True)
    )


def rowsum(v):
    return jnp.sum(v, axis=0, keepdims=True)


UP_PART = 2 * D
MASK_PART = UP_PART + 4 * D
LSTM_PART = HALF * G4 // D
PROJ_PART = 2 * CHAIN * HALF_P
SHARD_PART = LSTM_PART + 2 * HALF_P
MISC_SPLIT = 2 * CHAIN * SHARD_PART
MISC_LATE = MISC_SPLIT + SLOTS * SUBF
MISC_EARLY = MISC_LATE + LATE_ROWS
MISC = MISC_EARLY + EARLY_ROWS


def shard_start(shard, rows):
    return -(-shard * BANDS // rows)


def band_blocks(rows):
    if rows == CHAIN * CHAIN:
        three = SLOTS // CHAIN
        return [
            [
                (shard_start(CHAIN * z + q, rows), three, shard_start(CHAIN * z + q + 1, rows) - shard_start(CHAIN * z + q, rows))
                for z in range(CHAIN)
            ]
            for q in range(CHAIN)
        ]
    each = BANDS // CHAIN
    return [[(each * q, SLOTS, each if q + 1 < CHAIN else BANDS - each * q)] for q in range(CHAIN)]


def band_table(rows):
    return [
        [first + i if i < filled else -1 for first, places, filled in blocks for i in range(places)]
        for blocks in band_blocks(rows)
    ]


def wide_row(rows, first, many):
    return jnp.concatenate([rows[pl.ds(first + i, 1), :] for i in range(many)], axis=1)


def forward_chunk(keep, x_ref, w_ref, bias, scale, first_row, outs, gates, hk_s, ck_s, steps, chunk, rows, unroll, hall):
    n = steps // chunk
    j = pl.program_id(0)
    first = (j * chunk, (n - 1 - j) * chunk)

    @pl.when(j == 0)
    def _():
        hk_s[...] = jnp.zeros_like(hk_s)
        ck_s[...] = jnp.zeros_like(ck_s)

    for d in range(2):
        x = x_ref[pl.ds(pl.multiple_of(first[d] * rows, chunk * rows), chunk * rows), :]
        b = wide_row(bias, first_row + d * (G4 // D), G4 // D) * scale[...]
        gates[d] = mm(x, w_ref[d, :D]) + b

    def step(t, carry):
        new = []
        for d in range(2):
            hk, ck = carry[2 * d], carry[2 * d + 1]
            tt = t if d == 0 else chunk - 1 - t
            at = first[d] + tt
            now = keep[d * steps + at]
            later = jnp.minimum(at + 1, steps - 1) if d == 0 else jnp.maximum(at - 1, 0)
            nxt = keep[d * steps + later]
            h_ref, hk_ref, cf_ref = outs[3 * d : 3 * d + 3]
            a = gates[d, pl.ds(pl.multiple_of(tt * rows, rows), rows), :] + mm(hk, w_ref[d, D:])
            ti = jnp.tanh(a[:, :H])
            tf = jnp.tanh(a[:, H : 2 * H])
            g = jnp.tanh(a[:, 2 * H : 3 * H])
            to = jnp.tanh(a[:, 3 * H :])
            i = 0.5 * ti + 0.5
            f = 0.5 * tf + 0.5
            o = 0.5 * to + 0.5
            c = f * ck + i * g
            tc = jnp.tanh(c)
            h = o * tc
            h_low = h.astype(BF)
            hk_ref[tt] = hk
            h_ref[tt] = h_low
            if hall is not None:
                hall[d, pl.ds(pl.multiple_of(at * rows, rows), rows), :] = h_low
            cf_ref[tt, :, :H] = o * (1.0 - tc * tc)
            cf_ref[tt, :, H : 2 * H] = g * (0.5 - 0.5 * ti * ti)
            cf_ref[tt, :, 2 * H : 3 * H] = ck * (0.5 - 0.5 * tf * tf)
            cf_ref[tt, :, 3 * H : 4 * H] = i * (1.0 - g * g)
            cf_ref[tt, :, 4 * H : 5 * H] = tc * (0.5 - 0.5 * to * to)
            cf_ref[tt, :, 5 * H :] = f * now
            new += [(h * nxt).astype(BF), c * nxt]
        return tuple(new)

    done = lax.fori_loop(
        0, chunk, step, (hk_s[0], ck_s[0], hk_s[1], ck_s[1]), unroll=unroll
    )
    for d in range(2):
        hk_s[d] = done[2 * d]
        ck_s[d] = done[2 * d + 1]


def backward_chunk(
    keep, x_ref, ol, w_ref, p_ref, ins, dw, dp, db, wt, pt, da, sh, rg, ch_s, cc_s, steps, chunk, rows, unroll
):
    n = steps // chunk
    j = pl.program_id(0)
    first = ((n - 1 - j) * chunk, j * chunk)
    span = chunk * rows

    @pl.when(j == 0)
    def _():
        ch_s[...] = jnp.zeros_like(ch_s)
        cc_s[...] = jnp.zeros_like(cc_s)
        rg[...] = jnp.zeros_like(rg)
        dw[...] = jnp.zeros_like(dw)
        dp[...] = jnp.zeros_like(dp)
        db[...] = jnp.zeros_like(db)
        for d in range(2):
            wt[d] = w_ref[d].T
            pt[d] = p_ref[pl.ds(d * H, H), :].T

    at_rows = [pl.ds(pl.multiple_of(first[d] * rows, span), span) for d in range(2)]
    for d in range(2):
        sh[d] = mm(ol[at_rows[d], :], pt[d]).astype(BF)

    def step(t, carry):
        new = []
        for d in range(2):
            ch, cc = carry[2 * d], carry[2 * d + 1]
            tt = chunk - 1 - t if d == 0 else t
            now = keep[d * steps + first[d] + tt]
            cf = ins[3 * d + 2]
            here = pl.ds(pl.multiple_of(tt * rows, rows), rows)
            dh = sh[d, here, :].astype(F32) + ch
            dc = cc + dh * cf[tt, :, :H]
            da_now = jnp.concatenate(
                [
                    (dc * cf[tt, :, H : 2 * H]).astype(BF),
                    (dc * cf[tt, :, 2 * H : 3 * H]).astype(BF),
                    (dc * cf[tt, :, 3 * H : 4 * H]).astype(BF),
                    (dh * cf[tt, :, 4 * H : 5 * H]).astype(BF),
                ],
                axis=-1,
            )
            da[d, here, :] = da_now
            new += [mm(da_now, wt[d, :, D:]) * now, dc * cf[tt, :, 5 * H :]]
        return tuple(new)

    done = lax.fori_loop(0, chunk, step, (ch_s[0], cc_s[0], ch_s[1], cc_s[1]), unroll=unroll)
    ones = jnp.ones((8, span), BF)
    for d in range(2):
        ch_s[d] = done[2 * d]
        cc_s[d] = done[2 * d + 1]
        here = at_rows[d]
        grad = da[d]
        rg[here, :] = rg[here, :] + mm(grad, wt[d, :, :D])
        dw[d, :D, :] = dw[d, :D, :] + mm_tn(x_ref[here, :], grad)
        dw[d, D:, :] = dw[d, D:, :] + mm_tn(ins[3 * d + 1][...].reshape(span, H), grad)
        db[d] = db[d] + mm(ones, grad)
        at_p = pl.ds(d * H, H)
        dp[at_p, :] = dp[at_p, :] + mm_tn(ins[3 * d][...].reshape(span, H), ol[here, :])


def lay_weights(side, near, far, w):
    for way in range(2):
        for q in range(CHAIN):
            for part, of in ((near, side), (far, 1 - side)):
                at = pl.multiple_of(q * 2 * HALF + of * HALF, HALF)
                w[way, pl.ds(at, HALF), :] = part[q, way, :HALF, :]


def part_totals(side, dw, dp, scale, places, proj_places):
    for way in range(2):
        for q in range(CHAIN):
            for other in range(2):
                of = 1 - side if other else side
                at = pl.multiple_of(q * 2 * HALF + of * HALF, HALF)
                part = (dw[way, pl.ds(at, HALF), :] * scale[...]).astype(BF)
                out, row = places(other, q, way)
                for c in range(G4 // D):
                    out[row + c * HALF : row + (c + 1) * HALF, :] = part[:, c * D : (c + 1) * D]
                at = pl.multiple_of(way * H + q * 2 * HALF_P + of * HALF_P, HALF_P)
                out, row = proj_places(other, q, way)
                out[row : row + HALF_P, :] = dp[pl.ds(at, HALF_P), :].astype(BF)


def bias_total(db, scale, out, first):
    for way in range(2):
        row = db[way, :1, :] * scale[...]
        for i in range(G4 // D):
            out[pl.ds(first + way * (G4 // D) + i, 1), :] = row[:, i * D : (i + 1) * D]


def band_at(meta, bands, k):
    band = bands[meta[1] * SLOTS + k]
    return jnp.maximum(band, 0), band >= 0


def time_forward_kernel(
    steps, chunk, table, keep, bands, meta, sp, sm, gain, bias, scale, near, far, p, cot,
    emb, at, br, xs, w, cot_parts, h0, hk0, cf0, h1, hk1, cf1,
    gates, hk_s, ck_s, xt, hall,
):
    n = steps // chunk
    j = pl.program_id(0)
    frames = sp.shape[2]

    @pl.when(j == 0)
    def _():
        lay_weights(meta[0], near, far, w)
        for q in range(CHAIN):
            for k in range(SLOTS):
                cot_parts[q, k] = cot[max(table[q][k], 0)]
        xt[...] = jnp.zeros_like(xt)
        for k in range(SLOTS):
            v = sp[:, k].reshape(steps, D).astype(F32)
            band = band_at(meta, bands, k)[0]
            normed = (ln(v)[0] * gain[pl.ds(band, 1), :]).astype(BF)
            e = mm(normed, sm[k]) + bias[pl.ds(band, 1), :]
            emb[:, k] = e.reshape(CHAIN, frames, D)
            xt[pl.ds(k, steps, stride=ROWS_T), :] = ln(e)[0] * gain[pl.ds(GAIN_TIME, 1), :]
        xs[...] = xt[...].astype(BF)

    forward_chunk(
        keep, xs, w, bias, scale, BIAS_LSTM, (h0, hk0, cf0, h1, hk1, cf1), gates, hk_s, ck_s, steps, chunk, ROWS_T, 32, hall
    )

    @pl.when(j == n - 1)
    def _():
        span = 512
        for s in range(0, steps * ROWS_T, span):
            here = pl.ds(s, span)
            xt[here, :] = mm(hall[0, here, :], p[:H]) + mm(hall[1, here, :], p[H:])
        for k in range(SLOTS):
            to = xt[pl.ds(k, steps, stride=ROWS_T), :] + bias[pl.ds(BIAS_PROJ, 1), :]
            a = emb[:, k].reshape(steps, D) + to
            at[:, k] = a.reshape(CHAIN, frames, D)
            br[:, k] = (ln(a)[0] * gain[pl.ds(GAIN_BAND, 1), :]).astype(BF).reshape(CHAIN, frames, D)


def band_forward_kernel(
    steps, chunk, table, keep, rows_in, cores, bias, scale, p,
    bo, xs, w, h0, hk0, cf0, h1, hk1, cf1,
    gates, hk_s, ck_s, hall,
):
    n = steps // chunk
    j = pl.program_id(0)
    frames = rows_in.shape[2]

    @pl.when(j == 0)
    def _():
        for way in range(2):
            for q in range(CHAIN):
                for core in range(2):
                    at = (2 * q + core) * HALF
                    w[way, at : at + HALF, :] = cores[q, core, way]
        for q in range(CHAIN):
            for k in range(SLOTS):
                if table[q][k] >= 0:
                    xs[pl.ds(table[q][k] * frames, frames), :] = rows_in[q, k]
        xs[pl.ds(BANDS * frames, (steps - BANDS) * frames), :] = jnp.zeros(
            ((steps - BANDS) * frames, D), BF
        )

    forward_chunk(
        keep, xs, w, bias, scale, BIAS_LSTM + 2 * G4 // D, (h0, hk0, cf0, h1, hk1, cf1), gates, hk_s, ck_s, steps, chunk, frames, 7, hall
    )

    @pl.when(j == n - 1)
    def _():
        for q in range(CHAIN):
            for k in range(SLOTS):
                here = pl.ds(max(table[q][k], 0) * frames, frames)
                bo[q, k] = (mm(hall[0, here, :], p[:H]) + mm(hall[1, here, :], p[H:])).astype(BF)


def mask_kernel(
    bands, meta, at, bo, cot, um, dm, gain, bias,
    mask, abg, abl, kept, sent, early,
):
    frames = at.shape[2]
    rows = CHAIN * frames

    group = range(PAIR)
    found = [band_at(meta, bands, pl.program_id(0) * PAIR + i) for i in group]

    @pl.when(pl.program_id(0) == 0)
    def _():
        early[...] = jnp.zeros_like(early)

    def halves(i, v, first):
        half = v.shape[1] // 2
        lower = meta[0] == 0
        near = jnp.where(lower, v[:, :half], v[:, half:]).astype(BF)
        far = jnp.where(lower, v[:, half:], v[:, :half]).astype(BF)
        many = v.shape[0]
        for c in range(half // D):
            kept[i, first + c * many : first + (c + 1) * many, :] = near[:, c * D : (c + 1) * D]
            sent[i, first + c * many : first + (c + 1) * many, :] = far[:, c * D : (c + 1) * D]

    pb = bias[pl.ds(BIAS_PROJ + 1, 1), :]
    normed = [
        ln(at[:, i].reshape(rows, D) + (bo[:, i].reshape(rows, D).astype(F32) + pb)) for i in group
    ]
    mg = [gain[pl.ds(GAIN_MASK + found[i][0], 1), :] for i in group]
    mi = [(normed[i][0] * mg[i]).astype(BF) for i in group]
    act_f = [jnp.tanh(mm(mi[i], um[i]) + wide_row(bias, BIAS_UP + 4 * found[i][0], 4)) for i in group]
    act = [v.astype(BF) for v in act_f]
    pre = [mm(act[i], dm[i]) + wide_row(bias, BIAS_DOWN + 2 * found[i][0], 2) for i in group]
    og = []
    for i in group:
        value = pre[i][:, :SUBF]
        gate = 0.5 * jnp.tanh(0.5 * pre[i][:, SUBF:]) + 0.5
        mask[:, i] = (value * gate).astype(BF).reshape(CHAIN, frames, SUBF)
        cg = cot[:, i].reshape(rows, D).astype(F32) * found[i][1].astype(F32) * gate
        og.append(jnp.concatenate([cg.astype(BF), (cg * value * (1.0 - gate)).astype(BF)], axis=-1))
    pg = [(mm_nt(og[i], dm[i]) * (1.0 - act_f[i] * act_f[i])).astype(BF) for i in group]
    dy = [mm_nt(pg[i], um[i]) for i in group]
    low = []
    for i in group:
        halves(i, mm_tn(act[i], og[i]), UP_PART)
        halves(i, mm_tn(mi[i], pg[i]), 0)
        grad = ln_back(*normed[i], mg[i], dy[i])
        abg[:, i] = grad.reshape(CHAIN, frames, D)
        low.append(grad.astype(BF))
        abl[:, i] = low[i].reshape(CHAIN, frames, D)
    sums = [
        [rowsum(v) for v in (dy[i] * normed[i][0], low[i].astype(F32), pg[i].astype(F32), og[i].astype(F32))]
        for i in group
    ]
    for i in group:
        dmg, dpb, dub, ddb = sums[i]
        band = found[i][0]

        @pl.when(found[i][1])
        def _():
            early[pl.ds(band, 1), :] = dmg
            early[pl.ds(EARLY_BIAS, 1), :] = early[pl.ds(EARLY_BIAS, 1), :] + dpb
            for c in range(4):
                row = EARLY_BIAS + BIAS_UP - BIAS_PROJ - 1 + 4 * band + c
                early[pl.ds(row, 1), :] = dub[:, c * D : (c + 1) * D]
            for c in range(2):
                row = EARLY_BIAS + BIAS_DOWN - BIAS_PROJ - 1 + 2 * band + c
                early[pl.ds(row, 1), :] = ddb[:, c * D : (c + 1) * D]


def band_backward_kernel(
    steps, chunk, table, keep, meta, scale, ol_in, xs, w, p, mask_k, mask_f, h0, hk0, cf0, h1, hk1, cf1,
    keep_w, send_w, keep_p, send_p, bias_rows, rows_out, mask_sum,
    ol, wt, pt, da, sh, rg, ch_s, cc_s, dw, dp, db,
):
    n = steps // chunk
    j = pl.program_id(0)
    frames = ol_in.shape[2]
    mask_sum[...] = mask_k[...] + mask_f[...]

    @pl.when(j == 0)
    def _():
        for q in range(CHAIN):
            for k in range(SLOTS):
                if table[q][k] >= 0:
                    ol[pl.ds(table[q][k] * frames, frames), :] = ol_in[q, k]
        ol[pl.ds(BANDS * frames, (steps - BANDS) * frames), :] = jnp.zeros(
            ((steps - BANDS) * frames, D), BF
        )

    backward_chunk(
        keep, xs, ol, w, p, (h0, hk0, cf0, h1, hk1, cf1), dw, dp, db,
        wt, pt, da, sh, rg, ch_s, cc_s, steps, chunk, frames, 7,
    )

    @pl.when(j == n - 1)
    def _():
        part_totals(
            meta[0], dw, dp, scale,
            lambda other, q, way: ((keep_w, send_w)[other], (q * 2 + way) * LSTM_PART),
            lambda other, q, way: ((keep_p, send_p)[other], (q * 2 + way) * HALF_P),
        )
        bias_total(db, scale, bias_rows, 0)
        for q in range(CHAIN):
            for k in range(SLOTS):
                if table[q][k] >= 0:
                    rows_out[q, k] = rg[pl.ds(table[q][k] * frames, frames), :].astype(BF)
                else:
                    rows_out[q, k] = jnp.zeros((frames, D), BF)


def time_backward_kernel(
    steps, chunk, keep, bands, meta, scale, bgrad, abg, at, emb, sp, sm, gain, bias_b, keep_b, send_b, early, mask, xs, w, p, h0, hk0, cf0, h1, hk1, cf1,
    keep_m, send_m, leaving,
    ol, wt, pt, da, sh, rg, ch_s, cc_s, dw, dp, db, xt, atg, late, dsm,
):
    n = steps // chunk
    j = pl.program_id(0)
    frames = bgrad.shape[2]

    @pl.when(j == 0)
    def _():
        xt[...] = jnp.zeros_like(xt)
        late[...] = jnp.zeros_like(late)
        dbg = jnp.zeros((1, D), F32)
        dpb = jnp.zeros((1, D), F32)
        for k in range(SLOTS):
            norm, r = ln(at[:, k].reshape(steps, D))
            dy = bgrad[:, k].reshape(steps, D).astype(F32)
            dbg = dbg + rowsum(dy * norm)
            a = abg[:, k].reshape(steps, D) + ln_back(norm, r, gain[pl.ds(GAIN_BAND, 1), :], dy)
            atg[k] = a
            low = a.astype(BF).astype(F32)
            dpb = dpb + rowsum(low)
            xt[pl.ds(k, steps, stride=ROWS_T), :] = low
        ol[...] = xt[...].astype(BF)
        leaving[:, :SLOTS] = mask[...]
        late[pl.ds(GAIN_BAND, 1), :] = dbg
        late[pl.ds(LATE_BIAS + BIAS_PROJ, 1), :] = dpb
        late[pl.ds(LATE_BIAS + BIAS_LSTM + 2 * G4 // D, 2 * G4 // D), :] = bias_b[...]

    backward_chunk(
        keep, xs, ol, w, p, (h0, hk0, cf0, h1, hk1, cf1), dw, dp, db,
        wt, pt, da, sh, rg, ch_s, cc_s, steps, chunk, ROWS_T, 32,
    )

    @pl.when(j == n - 1)
    def _():
        outs = (keep_m, send_m)
        part_totals(
            meta[0], dw, dp, scale,
            lambda other, q, way: (outs[other], (q * 2 + way) * SHARD_PART),
            lambda other, q, way: (outs[other], (q * 2 + way) * SHARD_PART + LSTM_PART),
        )
        bias_total(db, scale, late, LATE_BIAS + BIAS_LSTM)
        dtg = jnp.zeros((1, D), F32)
        for k in range(SLOTS):
            dy = rg[pl.ds(k, steps, stride=ROWS_T), :]
            norm, r = ln(emb[:, k].reshape(steps, D))
            dtg = dtg + rowsum(dy * norm)
            el = (atg[k] + ln_back(norm, r, gain[pl.ds(GAIN_TIME, 1), :], dy)).astype(BF)
            dsb = rowsum(el.astype(F32))
            band, filled = band_at(meta, bands, k)
            own = gain[pl.ds(band, 1), :]
            norm, r = ln(sp[:, k].reshape(steps, D).astype(F32))
            dsm[k] = mm_tn((norm * own).astype(BF), el).astype(BF)
            dy = mm_nt(el, sm[k])
            dsg = rowsum(dy * norm)

            @pl.when(filled)
            def _():
                late[pl.ds(band, 1), :] = dsg
                late[pl.ds(LATE_BIAS + band, 1), :] = dsb

            leaving[:, SLOTS + k] = ln_back(norm, r, own, dy).astype(BF).reshape(CHAIN, frames, D)
        late[pl.ds(GAIN_TIME, 1), :] = dtg
        for out, band_part in ((keep_m, keep_b), (send_m, send_b)):
            for i in range(2 * CHAIN):
                row = (i + 1) * SHARD_PART - HALF_P
                out[row : row + HALF_P, :] = band_part[i * HALF_P : (i + 1) * HALF_P, :]
            out[pl.ds(MISC_EARLY, EARLY_ROWS), :] = early[...].astype(BF)
            out[pl.ds(MISC_SPLIT, SLOTS * SUBF), :] = dsm[...].reshape(SLOTS * SUBF, D)
            out[pl.ds(MISC_LATE, LATE_ROWS), :] = late[...].astype(BF)


def assemble_kernel(table, leaving, mask, grad):
    for q in range(CHAIN):
        for k in range(SLOTS):
            if table[q][k] >= 0:
                mask[table[q][k]] = leaving[q, k]
                at = pl.ds(table[q][k], leaving.shape[2], stride=BANDS)
                grad[at, :] = leaving[q, SLOTS + k].astype(F32)


def columns_kernel(meta, own, far, up, down, over, up_s, down_s):
    many = own.shape[0]
    fill = meta[2]
    lower = meta[0] == 0
    up_s[...] = jnp.zeros_like(up_s)
    down_s[...] = jnp.zeros_like(down_s)
    for i in range(many):
        for core in range(2):
            part = jnp.where(lower == (core == 0), own[i].astype(F32), far[i].astype(F32))
            for c in range(UP_PART // D):
                at = (core * (UP_PART // D) + c) * D
                up_s[FILL + i * D : FILL + (i + 1) * D, at : at + D] = part[c * D : (c + 1) * D, :]
            down_s[4 * (FILL + i * D) : 4 * (FILL + (i + 1) * D), core * D : (core + 1) * D] = part[UP_PART:, :]
    row = 0
    for scratch, out, unit in ((up_s, up, 1), (down_s, down, 4)):
        rows, wide = out.shape
        at = pl.multiple_of((FILL - fill) * unit, 8)
        out[...] = scratch[pl.ds(at, rows), :]
        past = scratch[pl.ds(pl.multiple_of(at + rows, 8), FILL * unit), :].astype(BF)
        for c in range(wide // D):
            over[row : row + FILL * unit, :] = past[:, c * D : (c + 1) * D]
            row += FILL * unit


def totals_kernel(
    meta, up, down, before, split, split_before, near, far, _,
    lstm_t, proj_t, split_t, up_t, down_t, square, split_s,
):
    fill = meta[2]
    lower = meta[0] == 0
    for core in range(2):
        part = jnp.where(lower == (core == 0), near[...].astype(F32), far[...].astype(F32))
        for c in range(G4 // D):
            lstm_t[core * HALF : (core + 1) * HALF, c * D : (c + 1) * D] = part[c * HALF : (c + 1) * HALF, :]
        proj_t[core * HALF_P : (core + 1) * HALF_P, :] = part[LSTM_PART:, :]
    split_s[...] = jnp.zeros_like(split_s)
    split_s[FILL : FILL + split.shape[0], :] = split[...].astype(F32)
    split_t[...] = split_s[pl.ds(pl.multiple_of(FILL - fill, 8), split_t.shape[0]), :]
    up_t[...] = up[...]
    down_t[...] = down[...]
    split_t[:FILL, :] = split_t[:FILL, :] + split_before[...].astype(F32)
    row = 0
    for out, rows in ((up_t, FILL), (down_t, 4 * FILL)):
        for c in range(out.shape[1] // D):
            at = slice(c * D, (c + 1) * D)
            out[:rows, at] = out[:rows, at] + before[row : row + rows, :].astype(F32)
            row += rows
    total = jnp.zeros((1, D), F32)
    for out in (lstm_t, proj_t, split_t, up_t, down_t):
        line = rowsum(out[...] * out[...])
        for c in range(line.shape[1] // D):
            total = total + line[:, c * D : (c + 1) * D]
    square[...] = jnp.broadcast_to(jnp.sum(total, axis=-1, keepdims=True), (8, D))


def plain_call(kernel, outs, scratch, name, meta, *arrays):
    specs = [ANY if v.ndim == 4 else pl.BlockSpec(memory_space=pltpu.VMEM) for v in arrays]
    return pl.pallas_call(
        kernel,
        in_specs=([] if meta is None else [SMEM]) + specs,
        out_specs=[pl.BlockSpec(memory_space=pltpu.VMEM)] * len(outs),
        out_shape=outs,
        scratch_shapes=[pltpu.VMEM(shape, F32) for shape in scratch],
        compiler_params=pltpu.CompilerParams(vmem_limit_bytes=VMEM),
        cost_estimate=cost(3),
        name=name,
    )(*(() if meta is None else (meta,)), *arrays)


def whole(shape):
    zeros = (0,) * len(shape)
    return pl.BlockSpec(shape, lambda j: zeros)


SMEM = pl.BlockSpec(memory_space=pltpu.SMEM)
ANY = pl.BlockSpec(memory_space=pl.ANY)


def sds(shape, dtype):
    return jax.ShapeDtypeStruct(shape, dtype)


def chunk_specs(n, chunk, rows, flip):
    up = lambda j: (j, 0, 0)
    down = lambda j: (n - 1 - j, 0, 0)
    specs = []
    for way in (down, up) if flip else (up, down):
        specs += [
            pl.BlockSpec((chunk, rows, H), way),
            pl.BlockSpec((chunk, rows, H), way),
            pl.BlockSpec((chunk, rows, 6 * H), way),
        ]
    return specs


def chunk_shapes(steps, rows):
    return [
        sds((steps, rows, H), BF),
        sds((steps, rows, H), BF),
        sds((steps, rows, 6 * H), F32),
    ] * 2


def params():
    return pltpu.CompilerParams(vmem_limit_bytes=VMEM, dimension_semantics=("arbitrary",))


def cost(micros):
    return pl.CostEstimate(flops=micros * 10**9, bytes_accessed=micros * 10**6, transcendentals=0)


def time_forward(table, keep, bands, meta, sp, sm, gain, bias, scale, near, far, p, cot):
    frames = sp.shape[2]
    steps, chunk = CHAIN * frames, 32
    n = steps // chunk
    slab = (CHAIN, SLOTS, frames, D)
    return pl.pallas_call(
        functools.partial(time_forward_kernel, steps, chunk, table),
        grid=(n,),
        in_specs=[SMEM, SMEM, SMEM]
        + [whole(v.shape) for v in (sp, sm, gain, bias, scale, near, far, p, cot)],
        out_specs=[whole(slab)] * 3
        + [whole((steps * ROWS_T, D)), whole((2, D + H, G4)), whole(slab)]
        + chunk_specs(n, chunk, ROWS_T, False),
        out_shape=[sds(slab, F32), sds(slab, F32), sds(slab, BF), sds((steps * ROWS_T, D), BF), sds((2, D + H, G4), BF), sds(slab, BF)]
        + chunk_shapes(steps, ROWS_T),
        scratch_shapes=[
            pltpu.VMEM((2, chunk * ROWS_T, G4), F32),
            pltpu.VMEM((2, ROWS_T, H), BF),
            pltpu.VMEM((2, ROWS_T, H), F32),
            pltpu.VMEM((steps * ROWS_T, D), F32),
            pltpu.VMEM((2, steps * ROWS_T, H), BF),
        ],
        compiler_params=params(),
        cost_estimate=cost(66),
        name="time_forward",
    )(keep, bands, meta, sp, sm, gain, bias, scale, near, far, p, cot)


def band_forward(table, keep, rows_in, cores, bias, scale, p):
    frames = rows_in.shape[2]
    steps, chunk = STEPS_B, 14
    n = steps // chunk
    slab = (CHAIN, SLOTS, frames, D)
    return pl.pallas_call(
        functools.partial(band_forward_kernel, steps, chunk, table),
        grid=(n,),
        in_specs=[SMEM, whole(slab)] + [whole(v.shape) for v in (cores, bias, scale, p)],
        out_specs=[whole(slab), whole((steps * frames, D)), whole((2, D + H, G4))] + chunk_specs(n, chunk, frames, False),
        out_shape=[sds(slab, BF), sds((steps * frames, D), BF), sds((2, D + H, G4), BF)] + chunk_shapes(steps, frames),
        scratch_shapes=[
            pltpu.VMEM((2, chunk * frames, G4), F32),
            pltpu.VMEM((2, frames, H), BF),
            pltpu.VMEM((2, frames, H), F32),
            pltpu.VMEM((2, steps * frames, H), BF),
        ],
        compiler_params=params(),
        cost_estimate=cost(27),
        name="band_forward",
    )(keep, rows_in, cores, bias, scale, p)


def mask_stage(bands, meta, at, bo, cot, um, dm, gain, bias):
    frames = at.shape[2]
    slab = (CHAIN, SLOTS, frames, D)
    part = pl.BlockSpec((CHAIN, PAIR, frames, D), lambda k: (0, k, 0, 0))

    def band(*shape):
        return pl.BlockSpec((PAIR,) + shape, lambda k: (k, 0, 0))

    return pl.pallas_call(
        mask_kernel,
        grid=(SLOTS // PAIR,),
        in_specs=[
            SMEM, SMEM, part, part, part, band(D, 4 * D), band(4 * D, 2 * SUBF),
            whole(gain.shape), whole(bias.shape),
        ],
        out_specs=[
            part, part, part, band(MASK_PART, D), band(MASK_PART, D),
            whole((EARLY_ROWS, D)),
        ],
        out_shape=[
            sds(slab, BF), sds(slab, F32), sds(slab, BF),
            sds((SLOTS, MASK_PART, D), BF), sds((SLOTS, MASK_PART, D), BF),
            sds((EARLY_ROWS, D), F32),
        ],
        compiler_params=params(),
        cost_estimate=cost(16),
        name="mask_stage",
    )(bands, meta, at, bo, cot, um, dm, gain, bias)


def backward_scratch(steps, chunk, rows):
    span = chunk * rows
    return [
        pltpu.VMEM((steps * rows, D), BF),
        pltpu.VMEM((2, G4, D + H), BF),
        pltpu.VMEM((2, D, H), BF),
        pltpu.VMEM((2, span, G4), BF),
        pltpu.VMEM((2, span, H), BF),
        pltpu.VMEM((steps * rows, D), F32),
        pltpu.VMEM((2, rows, H), F32),
        pltpu.VMEM((2, rows, H), F32),
        pltpu.VMEM((2, D + H, G4), F32),
        pltpu.VMEM((2 * H, D), F32),
        pltpu.VMEM((2, 8, G4), F32),
    ]


def total_shapes():
    return [sds((2 * CHAIN * LSTM_PART, D), BF)] * 2 + [sds((PROJ_PART, D), BF)] * 2


def band_backward(table, keep, meta, scale, ol_in, xs, w, p, mask_k, mask_f, saved):
    frames = ol_in.shape[2]
    steps, chunk = STEPS_B, 14
    n = steps // chunk
    slab = (CHAIN, SLOTS, frames, D)
    third = pl.BlockSpec((SLOTS // n, MASK_PART, D), lambda j: (j, 0, 0))
    return pl.pallas_call(
        functools.partial(band_backward_kernel, steps, chunk, table),
        grid=(n,),
        in_specs=[SMEM, SMEM]
        + [whole(v.shape) for v in (scale, ol_in, xs, w, p)]
        + [third, third]
        + chunk_specs(n, chunk, frames, True),
        out_specs=[whole(v.shape) for v in total_shapes()] + [whole((2 * G4 // D, D)), whole(slab), third],
        out_shape=total_shapes() + [sds((2 * G4 // D, D), F32), sds(slab, BF), sds(mask_k.shape, BF)],
        scratch_shapes=backward_scratch(steps, chunk, frames),
        compiler_params=params(),
        cost_estimate=cost(32),
        name="band_backward",
    )(keep, meta, scale, ol_in, xs, w, p, mask_k, mask_f, *saved)


def time_backward(keep, bands, meta, scale, bgrad, abg, at, emb, sp, sm, gain, bias_b, keep_b, send_b, early, mask, xs, w, p, saved):
    frames = bgrad.shape[2]
    steps, chunk = CHAIN * frames, 32
    n = steps // chunk
    slab = (CHAIN, SLOTS, frames, D)
    outs = [sds((MISC, D), BF)] * 2 + [sds((CHAIN, 2 * SLOTS, frames, D), BF)]
    return pl.pallas_call(
        functools.partial(time_backward_kernel, steps, chunk),
        grid=(n,),
        in_specs=[SMEM, SMEM, SMEM]
        + [whole(v.shape) for v in (scale, bgrad, abg, at, emb, sp, sm, gain, bias_b, keep_b, send_b, early, mask, xs, w, p)]
        + chunk_specs(n, chunk, ROWS_T, True),
        out_specs=[whole(v.shape) for v in outs],
        out_shape=outs,
        scratch_shapes=backward_scratch(steps, chunk, ROWS_T)
        + [pltpu.VMEM((steps * ROWS_T, D), F32), pltpu.VMEM((SLOTS, steps, D), F32)]
        + [pltpu.VMEM((LATE_ROWS, D), F32), pltpu.VMEM((SLOTS, SUBF, D), BF)],
        compiler_params=params(),
        cost_estimate=cost(96),
        name="time_backward",
    )(keep, bands, meta, scale, bgrad, abg, at, emb, sp, sm, gain, bias_b, keep_b, send_b, early, mask, xs, w, p, *saved)


def chain_groups():
    many = lax.axis_size("rows") // CHAIN
    return [[CHAIN * g + q for q in range(CHAIN)] for g in range(many)]


def place_groups():
    many = lax.axis_size("rows") // CHAIN
    return [[CHAIN * g + q for g in range(many)] for q in range(CHAIN)]


def across(v, groups, axis=0):
    return lax.all_to_all(v, "rows", axis, axis, axis_index_groups=groups, tiled=True)


def spread(v, groups):
    return across(jnp.broadcast_to(v[None], (len(groups[0]),) + v.shape), groups)


def swap_dir(v):
    return lax.ppermute(v, "dir", [(0, 1), (1, 0)])


def ordered(side, near, far):
    return jnp.where(side == 0, jnp.stack([near, far]), jnp.stack([far, near]))


def to_bands(v, more=None):
    v = jnp.concatenate([v, v[:1]])
    parts = []
    for blocks in band_blocks(lax.axis_size("rows")):
        cuts = [v[first : first + places] for first, places, _ in blocks]
        parts.append(jnp.concatenate(cuts + ([] if more is None else [more])))
    return jnp.stack(parts)


def my_bit(bit):
    return (lax.axis_index("rows") >> bit) & 1


def swap_bit(v, bit):
    return lax.ppermute(v, "rows", [(r, r ^ (1 << bit)) for r in range(lax.axis_size("rows"))])


def double(v, bit):
    return ordered(my_bit(bit), v, swap_bit(v, bit))


def halve(v, bit, axis):
    mine = my_bit(bit)
    kept = lax.dynamic_index_in_dim(v, mine, axis, False)
    return kept + swap_bit(lax.dynamic_index_in_dim(v, 1 - mine, axis, False), bit)


def my_rows(values):
    return jnp.asarray(np.array(values, np.int32))[lax.axis_index("rows")]


def fills(rows):
    return [shard_start(s, rows) * D - s * BANDS * D // rows for s in range(rows)]


def tied(v, *others):
    for other in others:
        one = lax.slice(other, (0,) * other.ndim, (1,) * other.ndim).reshape(())
        v = jnp.where(jnp.isnan(one), jnp.zeros_like(v), v)
    return v


def rows_after(shard):
    rows = lax.axis_size("rows")
    head = FILL * (shard.shape[0] * rows // (BANDS * D))
    if not square_slice():
        return shard[:1]
    return lax.ppermute(shard[:head].astype(BF), "rows", [(r + 1, r) for r in range(rows - 1)])


def whole_bands(shard, after):
    rows = lax.axis_size("rows")
    unit = shard.shape[0] * rows // (BANDS * D)
    head = FILL * unit
    spare = jnp.zeros((head,) + shard.shape[1:], shard.dtype)
    long = jnp.concatenate([shard, after, spare])
    return lax.dynamic_slice_in_dim(long, my_rows(fills(rows)) * unit, SLOTS // CHAIN * D * unit, 0)


def past_shard(own, unit):
    rows = lax.axis_size("rows")
    fill = my_rows(fills(rows)) * unit
    head = jnp.zeros((FILL * unit,) + own.shape[1:], own.dtype)
    many = BANDS * D * unit // rows
    over = lax.dynamic_slice_in_dim(jnp.concatenate([own, head]), many - fill, FILL * unit, 0)
    return lax.ppermute(over, "rows", [(r, r + 1) for r in range(rows - 1)])


def to_shard(own, before, unit):
    rows = lax.axis_size("rows")
    fill = my_rows(fills(rows)) * unit
    many = BANDS * D * unit // rows
    head = jnp.zeros((FILL * unit,) + own.shape[1:], own.dtype)
    moved = lax.dynamic_slice_in_dim(jnp.concatenate([head, own]), FILL * unit - fill, many, 0)
    before = jnp.concatenate([before, jnp.zeros((many - FILL * unit,) + own.shape[1:], own.dtype)])
    row = lax.broadcasted_iota(jnp.int32, (many, 1), 0)
    return jnp.where(row < fill, before, moved)


def square_slice():
    return lax.axis_size("rows") == CHAIN * CHAIN


def pick_bands(wide):
    blocks = band_blocks(lax.axis_size("rows"))
    place = lax.axis_index("rows") % CHAIN
    wide = jnp.concatenate([wide, wide[:1]])
    cuts = []
    for at in range(len(blocks[0])):
        first = jnp.asarray(np.array([b[at][0] for b in blocks], np.int32))[place]
        cuts.append(lax.dynamic_slice_in_dim(wide, first, blocks[0][at][1], 0))
    return jnp.concatenate(cuts)


def place_bands(part, valid):
    blocks = band_blocks(lax.axis_size("rows"))
    place = lax.axis_index("rows") % CHAIN
    part = part * valid[:, None]
    total = jnp.zeros((BANDS + 1, part.shape[1]), F32)
    row = 0
    for at in range(len(blocks[0])):
        first = jnp.asarray(np.array([b[at][0] for b in blocks], np.int32))[place]
        cut = part[row : row + blocks[0][at][1]]
        total = lax.dynamic_update_slice_in_dim(total, cut, first, 0)
        row += blocks[0][at][1]
    return total[:BANDS]


def band_weights(shard, after, gate):
    rows = lax.axis_size("rows")
    unit = shard.shape[0] * rows // BANDS
    low = shard.astype(BF)
    if not square_slice():
        full = lax.all_gather(low, "rows", axis=0, tiled=True).reshape(BANDS, unit, -1)
        return pick_bands(full)
    own = whole_bands(low, after)
    own = tied(own, gate)
    own = lax.all_gather(own, "rows", axis=0, axis_index_groups=place_groups(), tiled=True)
    return own.reshape(SLOTS, unit, -1)


def band_sums(grads, apart):
    if not square_slice():
        return grads
    if not apart:
        return halve(halve(grads.reshape(2, 2, SLOTS // CHAIN, *grads.shape[1:]), 2, 1), 3, 0)
    return lax.psum_scatter(
        grads, "rows", scatter_dimension=0, axis_index_groups=place_groups(), tiled=True
    )


def shard_parts(own, unit):
    if not square_slice():
        return own, own
    own = own.reshape(SLOTS // CHAIN * unit, -1)
    return own, past_shard(own, unit // D)


def shard_sums(parts, unit, valid):
    own, before = parts
    if square_slice():
        return to_shard(own, before, unit // D).astype(F32)
    flat = place_bands(own.reshape(SLOTS, -1).astype(F32), valid).astype(BF)
    flat = flat.reshape(BANDS * unit, -1)
    return lax.psum_scatter(flat, "rows", scatter_dimension=0, tiled=True).astype(F32)


def both_cores(kept, sent):
    return kept + swap_dir(sent)


def mask_columns(side, own, far):
    pair = ordered(side, own, far)
    many = own.shape[0]
    up = pair[:, :, :UP_PART].reshape(2, many, UP_PART // D, D, D)
    up = jnp.transpose(up, (1, 3, 0, 2, 4)).reshape(many, D, 4 * D)
    down = jnp.transpose(pair[:, :, UP_PART:], (1, 2, 0, 3)).reshape(many, 4 * D, 2 * SUBF)
    return up, down


def sum_rows(v, bits, wire=F32):
    for bit in bits:
        v = v.astype(wire)
        v = v.astype(F32) + swap_bit(v, bit).astype(F32)
    return v


def gather_first(side, lstm_low, proj_low, split_weight, sp_parts, up_after, down_after):
    if not square_slice():
        lstm = lax.all_gather(lstm_low, "rows", axis=0, tiled=True)
        proj = lax.all_gather(proj_low, "rows", axis=0, tiled=True).reshape(2, 2 * H, D)
        cut = jnp.transpose(lstm.reshape(2, 2, CHAIN, 2, HALF, G4), (0, 3, 2, 1, 4, 5))
        sp = across(sp_parts, chain_groups())
        near = lax.dynamic_index_in_dim(cut[0], side, 0, False)
        far = lax.dynamic_index_in_dim(cut[0], 1 - side, 0, False)
        return near, far, jnp.swapaxes(cut[1], 0, 1), proj, band_weights(split_weight, None, None), sp
    flat = HALF_P * D // G4
    packed = jnp.concatenate(
        [
            lax.dynamic_slice_in_dim(lstm_low, side * HALF, HALF, 0),
            lax.dynamic_slice_in_dim(proj_low, side * HALF_P, HALF_P, 0).reshape(flat, G4),
        ]
    )
    split = whole_bands(split_weight.astype(BF), rows_after(split_weight))
    column = double(packed, 3)
    sp = across(tied(sp_parts, column), chain_groups())
    column = double(tied(column, split), 2)
    split = double(split, 3)
    time = jnp.concatenate([column[:, 0], column[:, 1, HALF:]], axis=1)
    band = column[:, 1, :HALF]
    time = tied(time, split)
    split = double(split, 2)
    time = double(time, 0)
    time = double(tied(time, split, sp, up_after, down_after), 1)
    split = jnp.swapaxes(split, 0, 1).reshape(SLOTS, SUBF, D)
    near = time.reshape(CHAIN, 2, HALF + 2 * flat, G4)
    far = swap_dir(near)
    band = ordered(side, band, swap_dir(band))
    band = spread(tied(band, near), chain_groups())
    proj = ordered(side, near[:, :, HALF:], far[:, :, HALF:]).reshape(2, CHAIN, 2, 2, flat, G4)
    proj = jnp.transpose(proj, (3, 2, 1, 0, 4, 5)).reshape(2, 2 * H, D)
    return near, far, band, proj, split, sp


def unpacked(pair):
    lead = pair.shape[:-3]
    v = jnp.swapaxes(pair.reshape(*lead, 2, G4 // D, HALF, D), -3, -2)
    return v.reshape(*lead, 2 * HALF, G4)


def traded(parts, bit):
    flat = [v.reshape(-1, D) for v in parts]
    got = swap_bit(jnp.concatenate(flat), bit)
    out, row = [], 0
    for v, rows in zip(parts, flat):
        out.append(got[row : row + rows.shape[0]].reshape(v.shape))
        row += rows.shape[0]
    return out


def cut(v, bit, axis):
    mine = my_bit(bit)
    return (
        lax.dynamic_index_in_dim(v, mine, axis, False),
        lax.dynamic_index_in_dim(v, 1 - mine, axis, False),
    )


def all_totals(side, sums, lstm_b, valid):
    v = sums[:MISC_SPLIT].reshape(CHAIN, 2, SHARD_PART, D)
    split = sums[MISC_SPLIT:MISC_LATE]
    small = sums[MISC_LATE:].astype(F32)
    if not square_slice():
        bits = range((lax.axis_size("rows") - 1).bit_length())
        band = lstm_b.reshape(CHAIN, 2, LSTM_PART, D)
        lstm = jnp.stack([v[:, :, :LSTM_PART], band])
        lstm = jnp.transpose(ordered(side, lstm, swap_dir(lstm)), (1, 3, 2, 0, 4, 5))
        lstm = unpacked(lstm).reshape(-1, G4)
        proj = v[:, :, LSTM_PART:].reshape(CHAIN, 2, 2, HALF_P, D)
        proj = jnp.transpose(ordered(side, proj, swap_dir(proj)), (3, 2, 1, 0, 4, 5)).reshape(-1, D)
        lstm, proj = (
            lax.psum_scatter(t, "rows", scatter_dimension=0, tiled=True).astype(F32) for t in (lstm, proj)
        )
        split = shard_sums((split.reshape(SLOTS, SUBF, D), None), SUBF, valid)
        return lstm, proj, split, sum_rows(small, bits, BF), small
    kept, sent = cut(v.reshape(2, 2, 2, SHARD_PART, D), 0, 1)
    got, more = traded([sent, small.astype(BF)], 0)
    v, small = kept + got, small.astype(BF).astype(F32) + more.astype(F32)
    kept, sent = cut(v, 1, 0)
    got, more = traded([sent, small.astype(BF)], 1)
    v, small = kept + got, small.astype(BF).astype(F32) + more.astype(F32)
    late = v
    time_rows = LSTM_PART + HALF_P
    band = jnp.concatenate([lstm_b.reshape(2, LSTM_PART, D), v[:, time_rows:]], axis=1)
    v = jnp.stack([v[:, :time_rows], band])
    split = split.reshape(2, 2, SLOTS // CHAIN * SUBF, D)
    for bit, axis in ((2, 1), (3, 0)):
        kept, sent = cut(v, bit, axis)
        kept_s, sent_s = cut(split, bit, axis)
        got, got_s, more = traded([sent, sent_s, small.astype(BF)], bit)
        v, split = kept + got, kept_s + got_s
        small = small.astype(BF).astype(F32) + more.astype(F32)
    return v, split, small, late


def finish_kernel(*refs):
    square, small = refs[:2]
    totals = refs[2:7]
    olds = refs[7:28]
    norm_out = refs[28]
    outs = refs[29:]
    gain_rows = [(0, LATE_BIAS, 0), (LATE_ROWS, EARLY_BIAS, LATE_BIAS)]
    bias_rows = [(LATE_BIAS, LATE - LATE_BIAS, 0), (LATE_ROWS + EARLY_BIAS, EARLY - EARLY_BIAS, LATE - LATE_BIAS)]
    line = rowsum(small[...] * small[...])
    norm = jnp.sqrt(square[:1, :1] + jnp.sum(line, axis=-1, keepdims=True))
    norm_out[...] = norm
    clip = jnp.minimum(1.0, CLIP_NORM / (norm + 1e-06))

    def put(index, at, gradient, rate):
        velocity, weight, average = olds[3 * index : 3 * index + 3]
        clipped = gradient * clip
        velocity_new = MOMENTUM * velocity[at, :] + clipped
        weight_new = weight[at, :] - rate * (clipped + MOMENTUM * velocity_new)
        results = (clipped, velocity_new, weight_new, AVERAGE * average[at, :] + (1.0 - AVERAGE) * weight_new)
        for out, value in zip(outs[4 * index : 4 * index + 4], results):
            out[at, :] = value

    for index in range(5):
        rows = totals[index].shape[0]
        put(index, slice(0, rows), totals[index][...], LEARN_RATE)
    for index, pieces in ((5, gain_rows), (6, bias_rows)):
        for first, many, at in pieces:
            put(index, slice(at, at + many), small[first : first + many, :], GAIN_RATE)


def finish(square, small, totals, olds):
    arrays = (square, small) + totals + olds
    outs = [sds((1, 1), F32)]
    for old in olds[::3]:
        outs += [sds(old.shape, F32)] * 4
    return pl.pallas_call(
        finish_kernel,
        grid=(1,),
        in_specs=[whole(v.shape) for v in arrays],
        out_specs=[whole(v.shape) for v in outs],
        out_shape=outs,
        compiler_params=params(),
        cost_estimate=cost(8),
        name="finish",
    )(*arrays)


def halved_columns():
    scale = np.full((1, G4), 0.5, np.float32)
    scale[:, 2 * H : 3 * H] = 1.0
    return jnp.asarray(scale)


def on_device(
    spectra,
    mask_grad,
    clip_starts,
    split_weight,
    split_velocity,
    split_average,
    lstm_weight,
    lstm_velocity,
    lstm_average,
    proj_weight,
    proj_velocity,
    proj_average,
    up_weight,
    up_velocity,
    up_average,
    down_weight,
    down_velocity,
    down_average,
    gain_weight,
    gain_velocity,
    gain_average,
    bias_weight,
    bias_velocity,
    bias_average,
):
    side = lax.axis_index("dir")
    row = lax.axis_index("rows")
    place = row % CHAIN
    rows = lax.axis_size("rows")
    bits = range((rows - 1).bit_length())
    frames = spectra.shape[1]
    steps = CHAIN * frames
    scale = halved_columns()
    fill = my_rows(fills(rows)) if square_slice() else place
    meta = jnp.stack([side, place, fill]).astype(jnp.int32)
    table = band_table(rows)
    valid = jnp.asarray((np.array(table) >= 0).astype(np.float32))[place]
    bands = jnp.asarray(np.array(table, np.int32).reshape(-1))

    flags = lax.dynamic_index_in_dim(clip_starts[0], side, 1, False).astype(BF)
    flag_slab = jnp.broadcast_to(flags[:, None], (frames, SUBF))
    sp_parts = to_bands(jnp.transpose(spectra[0, :, 0], (1, 0, 2)), flag_slab[None])
    up_after, down_after = rows_after(up_weight), rows_after(down_weight)
    near, far, band_w, proj, split_mat, sp = gather_first(
        side, (lstm_weight * scale).astype(BF), proj_weight.astype(BF), split_weight, sp_parts, up_after, down_after
    )
    starts = sp[:, SLOTS, :, 0].reshape(steps).astype(F32)
    keep_time = jnp.concatenate([1.0 - starts, 1.0 - starts[1:], jnp.ones((1,), F32)])
    keep_np = np.ones((2 * STEPS_B,), np.float32)
    keep_np[STEPS_B + BANDS - 1] = 0.0
    keep_band = jnp.asarray(keep_np)

    up_mat = band_weights(up_weight, up_after, near)
    down_mat = band_weights(down_weight, down_after, near)

    emb, after_time, band_rows, xs_t, w_time, cot_parts, *saved_t = time_forward(
        table, keep_time, bands, meta, sp, split_mat, gain_weight, bias_weight, scale, near, far, proj[0],
        jnp.transpose(mask_grad[0, :, 0], (1, 0, 2)),
    )
    band_out, xs_b, w_band, *saved_b = band_forward(
        table, keep_band, across(band_rows, chain_groups()), band_w, bias_weight, scale, proj[1]
    )
    mask, abg, abl, kept, sent, early = mask_stage(
        bands, meta, after_time, across(band_out, chain_groups()), across(cot_parts, chain_groups()),
        up_mat, down_mat, gain_weight, bias_weight,
    )

    ol_in = across(abl, chain_groups())
    keep_w, send_w, keep_b, send_b, bias_b, bgrad, mask_sum = band_backward(
        table, keep_band, meta, scale, ol_in, xs_b, w_band, proj[1], kept, swap_dir(sent), saved_b
    )
    bgrad = across(bgrad, chain_groups())
    lstm_sum = both_cores(tied(keep_w, bgrad), send_w)
    mask_own = band_sums(mask_sum, True)
    lstm_b = lstm_sum
    if square_slice():
        lstm_b = lax.psum_scatter(
            lstm_sum, "rows", scatter_dimension=0, axis_index_groups=chain_groups(), tiled=True
        )
    keep_m, send_m, leaving = time_backward(
        keep_time, bands, meta, scale, bgrad, abg, after_time, emb, sp, split_mat,
        gain_weight, bias_b, keep_b, send_b, early, mask, xs_t, w_time, proj[0], saved_t,
    )
    sums = both_cores(tied(keep_m, lstm_b, mask_own), send_m)
    mask_far = swap_dir(mask_own)
    if square_slice():
        units = BANDS * D // rows
        up_own, down_own, over = plain_call(
            columns_kernel,
            [
                sds((units, 4 * D), F32), sds((4 * units, 2 * SUBF), F32),
                sds((FILL * 4 + 4 * FILL * 2, D), BF),
            ],
            [(5 * D, 4 * D), (20 * D, 2 * SUBF)], "mask_columns", meta, mask_own, mask_far,
        )
        before = lax.ppermute(over, "rows", [(r, r + 1) for r in range(rows - 1)])
        v, split, small, _ = all_totals(side, sums, lstm_b, valid)
        leaving = across(leaving, chain_groups())
        split_before = past_shard(split, 1)
        lstm_total, proj_total, split_total, up_total, down_total, square = plain_call(
            totals_kernel,
            [
                sds(lstm_weight.shape, F32), sds(proj_weight.shape, F32), sds(split_weight.shape, F32),
                sds(up_weight.shape, F32), sds(down_weight.shape, F32), sds((8, D), F32),
            ],
            [(5 * D, D)], "totals", meta, up_own, down_own, before, split, split_before,
            v, swap_dir(v), leaving,
        )
    else:
        up_own, down_own = mask_columns(side, mask_own, mask_far)
        lstm_total, proj_total, split_total, small, _ = all_totals(side, sums, lstm_b, valid)
        leaving = across(leaving, chain_groups())
        up_total = shard_sums(shard_parts(up_own, D), D, valid)
        down_total = shard_sums(shard_parts(down_own, 4 * D), 4 * D, valid)
        parts = (split_total, lstm_total, proj_total, up_total, down_total)
        square = jnp.full((8, D), sum(jnp.sum(v * v) for v in parts), F32)
    band_mask, spectra_grad = pl.pallas_call(
        functools.partial(assemble_kernel, table),
        grid=(1,),
        in_specs=[whole(leaving.shape)],
        out_specs=[whole((BANDS, frames, D)), whole((frames * BANDS, D))],
        out_shape=[sds((BANDS, frames, D), BF), sds((frames * BANDS, D), F32)],
        compiler_params=params(),
        cost_estimate=cost(3),
        name="assemble",
    )(leaving)
    band_mask = jnp.transpose(band_mask, (1, 0, 2))[None, :, None]
    spectra_grad = spectra_grad.reshape(1, frames, 1, BANDS, D)
    square = sum_rows(square, bits)
    norm, *results = finish(
        square,
        small,
        (split_total, lstm_total, proj_total, up_total, down_total),
        (
            split_velocity, split_weight, split_average, lstm_velocity, lstm_weight, lstm_average,
            proj_velocity, proj_weight, proj_average, up_velocity, up_weight, up_average,
            down_velocity, down_weight, down_average, gain_velocity, gain_weight, gain_average,
            bias_velocity, bias_weight, bias_average,
        ),
    )
    return (band_mask, spectra_grad, norm.reshape(())) + tuple(results)


def solution(mesh):
    per_row = P("rows", None)
    row_major = P("rows", None, "dir", None, None)
    return jax.shard_map(
        on_device,
        mesh=mesh,
        in_specs=(row_major, row_major, P("rows", None, None)) + (per_row,) * 15 + (P(),) * 6,
        out_specs=(row_major, row_major, P()) + (per_row,) * 20 + (P(),) * 8,
        check_vma=False,
    )
```
